32 devices in a mesh: seq: 8 (over z, y), batch: 4 (over x, core).
Axes of the slice: x: 2, y: 2, z: 4, core: 2. Of those that a mesh axis runs over, the one named last changes fastest.
Arguments:
- inputs: bfloat16 [8, 4096, 512], P('batch', 'seq'), may hold values from -6 to 6
- lengths: int32 [8], P('batch'), may hold values from 50 to 4096, as said below
- norm1_gain: float32 [512], replicated, may hold values from 0.25 to 1.75
- norm1_bias: float32 [512], replicated, may hold values from -2 to 2
- qkv_weight: bfloat16 [512, 1536], replicated, may hold values from -0.25 to 0.25
- features: bfloat16 [8, 256, 64], replicated, may hold values from -4 to 4
- out_weight: bfloat16 [512, 512], replicated, may hold values from -1 to 1
- norm2_gain: float32 [512], replicated, may hold values from 0.25 to 1.75
- norm2_bias: float32 [512], replicated, may hold values from -2 to 2
- up_weight: bfloat16 [512, 2048], replicated, may hold values from -0.25 to 0.25
- down_weight: bfloat16 [2048, 512], replicated, may hold values from -0.125 to 0.125
- cotangent: bfloat16 [8, 4096, 512], P('batch', 'seq'), may hold values from -6 to 6
Outputs:
- block_out: bfloat16 [8, 4096, 512], P('batch', 'seq')
- input_grad: float32 [8, 4096, 512], P('batch', 'seq')
- norm1_gain_grad: float32 [512], replicated
- norm1_bias_grad: float32 [512], replicated
- qkv_weight_grad: float32 [512, 1536], replicated
- out_weight_grad: float32 [512, 512], replicated
- norm2_gain_grad: float32 [512], replicated
- norm2_bias_grad: float32 [512], replicated
- up_weight_grad: float32 [512, 2048], replicated
- down_weight_grad: float32 [2048, 512], replicated
The draws below stay inside these ranges and needn't reach their ends.
Inputs may be any that keep to these rules, and one draw needn't show every extreme that they name: lengths[b] is the number of real tokens of sequence b; its other 4096 - lengths[b] positions are padding. Among the 2 sequences of each index of batch, one, drawn from the seed, has all 4096 positions real.
All inputs are finite; a program needn't handle non-finite values.
Results may differ from the reference program's by a relative error of at most 0.029.
Values sent between devices are 32-bit elements; how exact they have to be, the bound alone decides.
No kernel may reach another device: no remote copies, remote signals or barrier semaphores. Data moves between devices by JAX's collectives and lax.ppermute only.
A program may use at most 256 MiB of HBM per device.

```python
import jax
import jax.numpy as jnp
from jax import lax

D = 512
H = 8
DH = 64
M = 256
FF = 2048
STRETCH = 512
SEQ_DEV = 2
MIN_LEN = 50
SLOTS = 4096
SEQS = 8
N_SEQ = 8
N_BATCH = 4


def draw_lengths(key, part):
    key = jax.random.fold_in(key, 7)
    key_span, key_shift, key_pick = jax.random.split(key, 3)
    full_length = STRETCH * N_SEQ
    seq_total = SEQ_DEV * N_BATCH
    span_draws = jax.random.randint(key_span, (seq_total,), 0, full_length - MIN_LEN + 1)
    shifts = jax.random.randint(key_shift, (seq_total,), 0, 6)
    base_length = MIN_LEN + jnp.right_shift(span_draws, shifts)
    longest_slot = jax.random.randint(key_pick, (N_BATCH,), 0, SEQ_DEV)
    slot_index = jnp.arange(seq_total, dtype=jnp.int32) % SEQ_DEV
    group_index = jnp.arange(seq_total, dtype=jnp.int32) // SEQ_DEV
    longest = slot_index == longest_slot[group_index]
    return jnp.where(longest, full_length, base_length).astype(jnp.int32)


def level_of(rng, shape, shards, smallest, largest):
    def one(position, shards_of):
        draws = jax.random.uniform(jax.random.fold_in(jax.random.fold_in(rng, 6), position), (shards_of,), jnp.float32, smallest / len(shards), largest / len(shards))
        return jnp.repeat(jnp.exp(draws), shape[position] // shards_of).reshape((-1,) + (1,) * (len(shape) - position - 1))

    factor_of = one(*shards[0])
    for cut in shards[1:]:
        factor_of = factor_of * one(*cut)
    return factor_of


def bell_draw(own_key, extent, width, most, pieces=(), kind=jnp.bfloat16):
    entries = width * jax.random.normal(own_key, extent, jnp.float32)
    if pieces:
        entries = entries * level_of(own_key, extent, pieces, -0.22, 0.18)
    return jnp.clip(entries, -most, most).astype(kind)


def setup_inputs(seed: int = 0) -> dict:
    key_list = jax.random.split(jax.random.key(seed), 13)
    inputs = bell_draw(key_list[0], (SEQS, SLOTS, D), 1.0, 6.0, ((0, 4), (1, 8)))
    lengths = draw_lengths(jax.random.fold_in(key_list[12], 71), 0)
    norm1_gain = jnp.clip(1.0 + 0.15 * jax.random.normal(key_list[2], (D,), jnp.float32), 0.25, 1.75)
    norm1_bias = bell_draw(key_list[3], (D,), 0.3, 2.0, (), jnp.float32)
    qkv_weight = bell_draw(key_list[4], (D, 3 * D), D ** -0.5, 0.25)
    features = bell_draw(key_list[5], (H, M, DH), 1.0, 4.0)
    out_weight = bell_draw(key_list[6], (D, D), 32 ** -0.5, 1.0)
    norm2_gain = jnp.clip(1.0 + 0.15 * jax.random.normal(key_list[7], (D,), jnp.float32), 0.25, 1.75)
    norm2_bias = bell_draw(key_list[8], (D,), 0.3, 2.0, (), jnp.float32)
    up_weight = bell_draw(key_list[9], (D, FF), D ** -0.5, 0.25)
    down_weight = bell_draw(key_list[10], (FF, D), FF ** -0.5, 0.125)
    cotangent = bell_draw(key_list[11], (SEQS, SLOTS, D), 1.0, 6.0, ((0, 4), (1, 8)))
    return dict(inputs=inputs, lengths=lengths, norm1_gain=norm1_gain, norm1_bias=norm1_bias, qkv_weight=qkv_weight, features=features, out_weight=out_weight, norm2_gain=norm2_gain, norm2_bias=norm2_bias, up_weight=up_weight, down_weight=down_weight, cotangent=cotangent)


EPS = 1e-05
FULL_PRECISION = lax.Precision.HIGHEST

@jax.custom_vjp
def low(v):
    return lax.optimization_barrier(v.astype(jnp.bfloat16)).astype(jnp.float32)

@jax.custom_vjp
def reduced_backward(v):
    return v

def low_keep(v):
    return (low(v), None)

def low_pass(kept, grad):
    return (grad,)

def back_keep(v):
    return (v, None)

def back_low(kept, grad):
    return (low(grad),)
low.defvjp(low_keep, low_pass)
reduced_backward.defvjp(back_keep, back_low)

def layer_norm(values, gain_vec, bias_vec):
    row_mean = lax.optimization_barrier(jnp.mean(values, axis=-1, keepdims=True))
    centred = values - row_mean
    inv_std = lax.rsqrt(lax.optimization_barrier(jnp.mean(centred * centred, axis=-1, keepdims=True)) + EPS)
    return centred * inv_std * gain_vec + bias_vec

def feature_map(rescaled_input, random_features):
    feature_projection = reduced_backward(jnp.einsum('oiex,esx->oies', rescaled_input, random_features, precision=FULL_PRECISION))
    feat_count = random_features.shape[1]
    return jnp.exp(feature_projection - 0.5 * lax.optimization_barrier(jnp.sum(rescaled_input * rescaled_input, axis=-1, keepdims=True))) * feat_count ** (-0.5)

def block_one(row_data, seq_length, params, random_features):
    gain_one, bias_one, qkv_w, out_w, gain_two, bias_two, up_w, down_w = params
    head_count, feat_count, head_size = random_features.shape
    total_rows, model_width = row_data.shape
    live_rows = (jnp.arange(total_rows, dtype=jnp.int32) < seq_length).astype(jnp.float32)[:, None]
    shrink = head_size ** (-0.25)
    normed_in = low(layer_norm(row_data, gain_one, bias_one))
    qkv = reduced_backward(jnp.dot(normed_in, qkv_w, precision=FULL_PRECISION))
    split = qkv.reshape(N_SEQ, STRETCH, 3, head_count, head_size)
    queries = low(shrink * split[:, :, 0])
    keys_low = low(shrink * split[:, :, 1])
    values_low = low(split[:, :, 2])
    query_low = low(feature_map(queries, random_features))
    key_live = live_rows.reshape(N_SEQ, STRETCH, 1, 1)
    key_low = low(feature_map(keys_low, random_features) * key_live)
    delta_state = reduced_backward(jnp.einsum('njhm,njhd->nhmd', key_low, values_low, precision=FULL_PRECISION))
    delta_sum = lax.optimization_barrier(jnp.sum(key_low, axis=1))
    prefix_state = jnp.concatenate([jnp.zeros_like(delta_state[:1]), jnp.cumsum(delta_state, axis=0)[:-1]], axis=0)
    prefix_sum = jnp.concatenate([jnp.zeros_like(delta_sum[:1]), jnp.cumsum(delta_sum, axis=0)[:-1]], axis=0)
    causal = jnp.tril(jnp.ones((STRETCH, STRETCH), dtype=bool))
    scores = reduced_backward(jnp.where(causal, jnp.einsum('nihm,njhm->nhij', query_low, key_low, precision=FULL_PRECISION), 0.0))
    numerator = reduced_backward(jnp.einsum('nihm,nhmd->nihd', query_low, low(prefix_state), precision=FULL_PRECISION) + jnp.einsum('nhij,njhd->nihd', low(scores), values_low, precision=FULL_PRECISION))
    denominator = jnp.einsum('nihm,nhm->nih', query_low, prefix_sum, precision=FULL_PRECISION) + jnp.transpose(lax.optimization_barrier(jnp.sum(scores, axis=-1)), (0, 2, 1))
    attention = (numerator / denominator[..., None]).reshape(total_rows, model_width)
    branch = reduced_backward(jnp.dot(low(attention), out_w, precision=FULL_PRECISION))
    middle = row_data + live_rows * branch
    normed_mid = low(layer_norm(middle, gain_two, bias_two))
    up_proj = reduced_backward(jnp.dot(normed_mid, up_w, precision=FULL_PRECISION))
    activated = low(jax.nn.gelu(up_proj, approximate=True))
    ffn_branch = reduced_backward(jnp.dot(activated, down_w, precision=FULL_PRECISION))
    return middle + live_rows * ffn_branch

def reference(inputs, lengths, norm1_gain, norm1_bias, qkv_weight, features, out_weight, norm2_gain, norm2_bias, up_weight, down_weight, cotangent):
    random_features = features.astype(jnp.float32)
    params = (norm1_gain.astype(jnp.float32), norm1_bias.astype(jnp.float32), qkv_weight.astype(jnp.float32), out_weight.astype(jnp.float32), norm2_gain.astype(jnp.float32), norm2_bias.astype(jnp.float32), up_weight.astype(jnp.float32), down_weight.astype(jnp.float32))

    def forward(row_data, weights):

        def one_sequence(unused_carry, packed):
            return (unused_carry, jax.checkpoint(block_one)(packed[0], packed[1], weights, random_features))
        return lax.scan(one_sequence, jnp.float32(0.0), (row_data, lengths))[1]
    block_sum, pullback = jax.vjp(forward, inputs.astype(jnp.float32), params)
    input_grad, grads = pullback(cotangent.astype(jnp.float32))
    return (block_sum.astype(jnp.bfloat16), input_grad, grads[0], grads[1], grads[2], grads[3], grads[4], grads[5], grads[6], grads[7])
```

```python
import functools

import jax
import jax.numpy as jnp
from jax import lax
from jax.sharding import Mesh, PartitionSpec as P

EPS = 1e-05
FULL_PRECISION = lax.Precision.HIGHEST


class Slice32:
    axes = ("z", "y", "x", "c")
    rows = P(("x", "c"), ("z", "y"), None)
    lens = P(("x", "c"))
    swap = {
        "c": ("c", [(0, 1), (1, 0)]),
        "x": ("x", [(0, 1), (1, 0)]),
        "y": ("y", [(0, 1), (1, 0)]),
        "z1": ("z", [(0, 1), (1, 0), (2, 3), (3, 2)]),
        "z2": ("z", [(0, 2), (2, 0), (1, 3), (3, 1)]),
    }

    def position(self):
        return lax.axis_index("z") * 2 + lax.axis_index("y")

    def bit(self, step):
        if step == "z1":
            return lax.axis_index("z") % 2
        if step == "z2":
            return lax.axis_index("z") // 2
        return lax.axis_index(step)

    def exchange(self, part, step):
        axis, pairs = self.swap[step]
        return lax.ppermute(part, axis, pairs)

    def carry(self, halves, reverse):
        y = lax.axis_index("y")
        keep = lax.dynamic_index_in_dim(halves, y, 0, keepdims=False)
        give = lax.dynamic_index_in_dim(halves, 1 - y, 0, keepdims=False)
        got = self.exchange(give, "y")
        total = keep + got
        hops = [(3, 2), (2, 1), (1, 0)] if reverse else [(0, 1), (1, 2), (2, 3)]
        out, before = total, None
        for n, hop in enumerate(hops):
            arrived = lax.ppermute(out, "z", [hop])
            before = arrived if before is None else before + arrived
            out = arrived + total
        first = y == (1 if reverse else 0)
        mine = before + jnp.where(first, 0.0, got)
        other = self.exchange(before + jnp.where(first, keep, 0.0), "y")
        pair = jnp.stack([mine, other])
        return jnp.where(y == 0, pair, pair[::-1])

    def split(self, part, step):
        half = part.shape[0] // 2
        bit = self.bit(step)
        keep = lax.dynamic_slice_in_dim(part, bit * half, half, 0)
        give = lax.dynamic_slice_in_dim(part, (1 - bit) * half, half, 0)
        return keep + self.exchange(give, step)

    def join(self, part, step):
        other = self.exchange(part, step)
        first = self.bit(step) == 0
        return jnp.concatenate([jnp.where(first, part, other), jnp.where(first, other, part)], 0)

    def total(self, part, order):
        for step in order:
            part = self.split(part, step)
        for step in order[::-1]:
            part = self.join(part, step)
        return part

    def total_small(self, part):
        for step in ("c", "x", "y", "z1", "z2"):
            part = part + self.exchange(part, step)
        return part


class AnySlice:
    axes = ("seq", "batch")
    rows = P("batch", "seq", None)
    lens = P("batch")

    def position(self):
        return lax.axis_index("seq")

    def carry(self, halves, reverse):
        size = lax.axis_size("seq")

        def shift(part, by):
            pairs = [(i, i + by) for i in range(size - by)]
            return lax.ppermute(part, "seq", [(b, a) for a, b in pairs] if reverse else pairs)

        out, by = shift(halves, 1), 1
        while by < size:
            out, by = out + shift(out, by), by * 2
        return out

    def total(self, part, order):
        return lax.psum(part, ("seq", "batch"))

    def total_small(self, part):
        return lax.psum(part, ("seq", "batch"))


def carried_in(comm, state, total, reverse):
    seqs, heads, feats, size = state.shape
    lanes = 512
    rows = heads * feats * size // lanes // 2
    extra = heads * feats // lanes // 2
    states, sums = [], []
    for s in range(seqs):
        halves = jnp.concatenate(
            [
                state[s].reshape(2, rows, lanes),
                total[s].reshape(2, extra, lanes),
                jnp.zeros((2, -extra % 8, lanes), jnp.float32),
            ],
            axis=1,
        )
        halves = comm.carry(halves, reverse)
        states.append(halves[:, :rows].reshape(heads, feats, size))
        sums.append(halves[:, rows : rows + extra].reshape(heads, feats))
    return jnp.stack(states), jnp.stack(sums)


def layer_norm(values, gain_vec, bias_vec):
    row_mean = jnp.mean(values, axis=-1, keepdims=True)
    centred = values - row_mean
    inv_std = lax.rsqrt(jnp.mean(centred * centred, axis=-1, keepdims=True) + EPS)
    normed = centred * inv_std
    return (normed * gain_vec + bias_vec, normed, inv_std)


def norm_back(grad_out, normed, inv_std, gain_vec):
    scaled_grad = grad_out * gain_vec
    grad_in = inv_std * (
        scaled_grad
        - jnp.mean(scaled_grad, axis=-1, keepdims=True)
        - normed * jnp.mean(scaled_grad * normed, axis=-1, keepdims=True)
    )
    return (grad_in, jnp.sum(grad_out * normed, axis=(0, 1)), jnp.sum(grad_out, axis=(0, 1)))


def feature_map(rescaled_input, random_features):
    feature_projection = jnp.einsum(
        "kbvr,vxr->kbvx", rescaled_input, random_features, preferred_element_type=jnp.float32
    )
    norm_part = jnp.sum(jnp.square(rescaled_input.astype(jnp.float32)), axis=-1, keepdims=True)
    return jnp.exp(feature_projection - 0.5 * norm_part) * random_features.shape[1] ** (-0.5)


def body(
    comm,
    inputs,
    lengths,
    norm1_gain,
    norm1_bias,
    qkv_weight,
    features,
    out_weight,
    norm2_gain,
    norm2_bias,
    up_weight,
    down_weight,
    cotangent,
):
    seq_count, stretch_rows, model_width = inputs.shape
    head_count, feat_count, head_size = features.shape
    shrink = head_size ** (-0.25)
    first_row = comm.position() * stretch_rows
    positions = first_row + jnp.arange(stretch_rows, dtype=jnp.int32)
    live_rows = (positions[None, :] < lengths[:, None]).astype(jnp.float32)[..., None]
    row_data = inputs.astype(jnp.float32)
    normed_f, normed1, inv1 = layer_norm(row_data, norm1_gain, norm1_bias)
    normed_in = normed_f.astype(jnp.bfloat16)
    qkv = jnp.einsum("scd,de->sce", normed_in, qkv_weight, preferred_element_type=jnp.float32)
    split = qkv.reshape(seq_count, stretch_rows, 3, head_count, head_size)
    queries = (shrink * split[:, :, 0]).astype(jnp.bfloat16)
    keys_low = (shrink * split[:, :, 1]).astype(jnp.bfloat16)
    values_low = split[:, :, 2].astype(jnp.bfloat16)
    query_map = feature_map(queries, features)
    key_map = feature_map(keys_low, features) * live_rows[..., None]
    query_low = query_map.astype(jnp.bfloat16)
    key_low = key_map.astype(jnp.bfloat16)
    causal = jnp.tril(jnp.ones((stretch_rows, stretch_rows), dtype=bool))
    scores = jnp.where(
        causal,
        jnp.einsum("sihm,sjhm->shij", query_low, key_low, preferred_element_type=jnp.float32),
        0.0,
    )
    scores_low = scores.astype(jnp.bfloat16)
    delta_state = jnp.einsum(
        "sjhm,sjhd->shmd", key_low, values_low, preferred_element_type=jnp.float32
    )
    delta_sum = jnp.sum(key_low.astype(jnp.float32), axis=1)
    prefix_state, prefix_sum = carried_in(comm, delta_state, delta_sum, False)
    state_low = prefix_state.astype(jnp.bfloat16)
    numerator = jnp.einsum(
        "sihm,shmd->sihd", query_low, state_low, preferred_element_type=jnp.float32
    ) + jnp.einsum("shij,sjhd->sihd", scores_low, values_low, preferred_element_type=jnp.float32)
    denominator = jnp.einsum(
        "sihm,shm->sih",
        query_low,
        prefix_sum,
        preferred_element_type=jnp.float32,
        precision=FULL_PRECISION,
    ) + jnp.transpose(jnp.sum(scores, axis=-1), (0, 2, 1))
    attention = numerator / denominator[..., None]
    attention_low = attention.reshape(seq_count, stretch_rows, model_width).astype(jnp.bfloat16)
    branch = jnp.einsum(
        "sce,ed->scd", attention_low, out_weight, preferred_element_type=jnp.float32
    )
    middle = row_data + live_rows * branch
    normed_g, normed2, inv2 = layer_norm(middle, norm2_gain, norm2_bias)
    normed_mid = normed_g.astype(jnp.bfloat16)
    up_proj = jnp.einsum("scd,df->scf", normed_mid, up_weight, preferred_element_type=jnp.float32)
    activated, gelu_back = jax.vjp(lambda values: jax.nn.gelu(values, approximate=True), up_proj)
    activated_low = activated.astype(jnp.bfloat16)
    ffn_branch = jnp.einsum(
        "scf,fd->scd", activated_low, down_weight, preferred_element_type=jnp.float32
    )
    block_out = (middle + live_rows * ffn_branch).astype(jnp.bfloat16)
    grad_out = cotangent.astype(jnp.float32)
    grad_ffn = (live_rows * grad_out).astype(jnp.bfloat16)
    down_grad = jnp.einsum(
        "scf,scd->fd", activated_low, grad_ffn, preferred_element_type=jnp.float32
    )
    grad_act = jnp.einsum("scd,fd->scf", grad_ffn, down_weight, preferred_element_type=jnp.float32)
    grad_up = gelu_back(grad_act)[0].astype(jnp.bfloat16)
    up_grad = jnp.einsum("scd,scf->df", normed_mid, grad_up, preferred_element_type=jnp.float32)
    grad_norm2 = jnp.einsum("scf,df->scd", grad_up, up_weight, preferred_element_type=jnp.float32)
    back_two, gain2_grad, bias2_grad = norm_back(grad_norm2, normed2, inv2, norm2_gain)
    grad_mid = grad_out + back_two
    grad_branch = (live_rows * grad_mid).astype(jnp.bfloat16)
    outw_grad = jnp.einsum(
        "sce,scd->ed", attention_low, grad_branch, preferred_element_type=jnp.float32
    )
    grad_attn = jnp.einsum(
        "scd,ed->sce", grad_branch, out_weight, preferred_element_type=jnp.float32
    )
    grad_attn = grad_attn.reshape(seq_count, stretch_rows, head_count, head_size)
    grad_num = (grad_attn / denominator[..., None]).astype(jnp.bfloat16)
    grad_den = -jnp.sum(grad_attn * attention, axis=-1) / denominator
    grad_scores = jnp.where(
        causal,
        jnp.einsum("sihd,sjhd->shij", grad_num, values_low, preferred_element_type=jnp.float32)
        + jnp.transpose(grad_den, (0, 2, 1))[..., None],
        0.0,
    ).astype(jnp.bfloat16)
    grad_state = jnp.einsum(
        "sihm,sihd->shmd", query_low, grad_num, preferred_element_type=jnp.float32
    )
    grad_sum = jnp.einsum(
        "sihm,sih->shm",
        query_low,
        grad_den,
        preferred_element_type=jnp.float32,
        precision=FULL_PRECISION,
    )
    later_state, later_sum = carried_in(comm, grad_state, grad_sum, True)
    later_low = later_state.astype(jnp.bfloat16)
    grad_pq = (
        jnp.einsum("sihd,shmd->sihm", grad_num, state_low, preferred_element_type=jnp.float32)
        + jnp.einsum("shij,sjhm->sihm", grad_scores, key_low, preferred_element_type=jnp.float32)
        + grad_den[..., None] * prefix_sum[:, None]
    )
    grad_pk = (
        jnp.einsum("shij,sihm->sjhm", grad_scores, query_low, preferred_element_type=jnp.float32)
        + jnp.einsum("sjhd,shmd->sjhm", values_low, later_low, preferred_element_type=jnp.float32)
        + later_sum[:, None]
    )
    grad_vv = jnp.einsum(
        "shij,sihd->sjhd", scores_low, grad_num, preferred_element_type=jnp.float32
    ) + jnp.einsum("sjhm,shmd->sjhd", key_low, later_low, preferred_element_type=jnp.float32)
    exponent_query = grad_pq * query_map
    exponent_key = grad_pk * key_map
    grad_qs = jnp.einsum(
        "koer,erw->koew",
        exponent_query.astype(jnp.bfloat16),
        features,
        preferred_element_type=jnp.float32,
    ) - queries * jnp.sum(exponent_query, axis=-1, keepdims=True)
    grad_ks = jnp.einsum(
        "koer,erw->koew",
        exponent_key.astype(jnp.bfloat16),
        features,
        preferred_element_type=jnp.float32,
    ) - keys_low * jnp.sum(exponent_key, axis=-1, keepdims=True)
    grad_qkv = jnp.stack([shrink * grad_qs, shrink * grad_ks, grad_vv], axis=2)
    grad_qkv = grad_qkv.reshape(seq_count, stretch_rows, 3 * model_width).astype(jnp.bfloat16)
    qkv_grad = jnp.einsum("scd,sce->de", normed_in, grad_qkv, preferred_element_type=jnp.float32)
    grad_norm1 = jnp.einsum("sce,de->scd", grad_qkv, qkv_weight, preferred_element_type=jnp.float32)
    back_one, gain1_grad, bias1_grad = norm_back(grad_norm1, normed1, inv1, norm1_gain)
    input_grad = grad_mid + back_one
    up_grad = comm.total(up_grad, ("c", "x", "y", "z1", "z2"))
    down_grad = comm.total(down_grad, ("c", "y", "x", "z1", "z2"))
    outw_grad = comm.total(outw_grad, ("c", "x", "y", "z1", "z2"))
    qkv_grad = comm.total(qkv_grad, ("c", "y", "x", "z1", "z2"))
    small = comm.total_small(jnp.stack([gain1_grad, bias1_grad, gain2_grad, bias2_grad]))
    gain1_grad, bias1_grad, gain2_grad, bias2_grad = small[0], small[1], small[2], small[3]
    return (
        block_out,
        input_grad,
        gain1_grad,
        bias1_grad,
        qkv_grad,
        outw_grad,
        gain2_grad,
        bias2_grad,
        up_grad,
        down_grad,
    )


def solution(mesh):
    comm = AnySlice()
    if dict(mesh.shape) == {"seq": 8, "batch": 4}:
        comm = Slice32()
        mesh = Mesh(mesh.devices.reshape(4, 2, 2, 2), comm.axes)
    return jax.shard_map(
        functools.partial(body, comm),
        mesh=mesh,
        in_specs=(comm.rows, comm.lens) + (P(),) * 9 + (comm.rows,),
        out_specs=(comm.rows, comm.rows) + (P(),) * 8,
        check_vma=False,
    )
```

```python
import functools

import jax
import jax.numpy as jnp
from jax import lax
from jax.experimental import pallas as pl
from jax.experimental.pallas import tpu as pltpu
from jax.sharding import Mesh, PartitionSpec as P

EPS = 1e-05
SHRINK = 64 ** (-0.25)
SCALE = 256 ** (-0.5)


class Slice32:
    axes = ("z", "y", "x", "c")
    rows = P(("x", "c"), ("z", "y"), None)
    lens = P(("x", "c"))
    swap = {
        "c": ("c", [(0, 1), (1, 0)]),
        "x": ("x", [(0, 1), (1, 0)]),
        "y": ("y", [(0, 1), (1, 0)]),
        "z1": ("z", [(0, 1), (1, 0), (2, 3), (3, 2)]),
        "z2": ("z", [(0, 2), (2, 0), (1, 3), (3, 1)]),
    }

    def position(self):
        return lax.axis_index("z") * 2 + lax.axis_index("y")

    def bit(self, step):
        if step == "z1":
            return lax.axis_index("z") % 2
        if step == "z2":
            return lax.axis_index("z") // 2
        return lax.axis_index(step)

    def exchange(self, part, step):
        axis, pairs = self.swap[step]
        return lax.ppermute(part, axis, pairs)

    def carry(self, halves, reverse):
        y = lax.axis_index("y")
        keep = lax.dynamic_index_in_dim(halves, y, 0, keepdims=False)
        give = lax.dynamic_index_in_dim(halves, 1 - y, 0, keepdims=False)
        got = self.exchange(give, "y")
        total = keep + got
        hops = [(3, 2), (2, 1), (1, 0)] if reverse else [(0, 1), (1, 2), (2, 3)]
        out, before = total, None
        for n, hop in enumerate(hops):
            arrived = lax.ppermute(out, "z", [hop])
            before = arrived if before is None else before + arrived
            out = arrived + total
        first = y == (1 if reverse else 0)
        mine = before + jnp.where(first, 0.0, got)
        other = self.exchange(before + jnp.where(first, keep, 0.0), "y")
        pair = jnp.stack([mine, other])
        return jnp.where(y == 0, pair, pair[::-1])

    def split(self, part, step):
        half = part.shape[0] // 2
        bit = self.bit(step)
        keep = lax.dynamic_slice_in_dim(part, bit * half, half, 0)
        give = lax.dynamic_slice_in_dim(part, (1 - bit) * half, half, 0)
        return keep + self.exchange(give, step)

    def join(self, part, step):
        other = self.exchange(part, step)
        first = self.bit(step) == 0
        return jnp.concatenate([jnp.where(first, part, other), jnp.where(first, other, part)], 0)

    def total(self, part, order):
        for step in order:
            part = self.split(part, step)
        for step in order[::-1]:
            part = self.join(part, step)
        return part

    def total_small(self, part):
        for step in ("c", "x", "y", "z1", "z2"):
            part = part + self.exchange(part, step)
        return part


class AnySlice:
    axes = ("seq", "batch")
    rows = P("batch", "seq", None)
    lens = P("batch")

    def position(self):
        return lax.axis_index("seq")

    def carry(self, halves, reverse):
        size = lax.axis_size("seq")

        def shift(part, by):
            pairs = [(i, i + by) for i in range(size - by)]
            return lax.ppermute(part, "seq", [(b, a) for a, b in pairs] if reverse else pairs)

        out, by = shift(halves, 1), 1
        while by < size:
            out, by = out + shift(out, by), by * 2
        return out

    def total(self, part, order):
        return lax.psum(part, ("seq", "batch"))

    def total_small(self, part):
        return lax.psum(part, ("seq", "batch"))


LANES = 128
BF = jnp.bfloat16
F32 = jnp.float32


def mm(a, b):
    return jnp.dot(a, b, preferred_element_type=F32)


def mm_t(a, b):
    return lax.dot_general(a, b, (((1,), (1,)), ((), ())), preferred_element_type=F32)


def lanes_of(width):
    return lax.broadcasted_iota(jnp.int32, (1, width), 1)


def head_of(width):
    return (lanes_of(width) % LANES) // 64


def live_of(meta, s, rows):
    at = lax.broadcasted_iota(jnp.int32, (rows, 1), 0) + meta[0]
    return (at < meta[1 + s]).astype(F32)


def norm(values, gain, bias):
    mu = jnp.mean(values, axis=-1, keepdims=True)
    centred = values - mu
    inv = lax.rsqrt(jnp.mean(centred * centred, axis=-1, keepdims=True) + EPS)
    xhat = centred * inv
    return xhat * gain + bias, xhat, inv


def norm_grad(e, xhat, inv, gain):
    eg = e * gain
    return inv * (
        eg
        - jnp.mean(eg, axis=-1, keepdims=True)
        - xhat * jnp.mean(eg * xhat, axis=-1, keepdims=True)
    )


def two_rows(first, second):
    row = lax.broadcasted_iota(jnp.int32, (8, first.shape[1]), 0)
    return jnp.where(row == 0, first, jnp.where(row == 1, second, 0.0))


def map_kernel(s, meta, x, gain, bias, wq, wk, wv, fx, h1, qs, ks, vv, pq, pk, xs):
    p = pl.program_id(0)
    rows = x.shape[1]

    @pl.when(p == 0)
    def _():
        h1[...] = norm(x[0].astype(F32), gain[...], bias[...])[0].astype(BF)

    w = jnp.concatenate([wq[...], wk[...], wv[...]], axis=1)
    qkv = mm(h1[...], w)
    q = (SHRINK * qkv[:, :LANES]).astype(BF)
    k = (SHRINK * qkv[:, LANES : 2 * LANES]).astype(BF)
    v = qkv[:, 2 * LANES :].astype(BF)
    qs[...], ks[...], vv[...] = q, k, v

    def phi(u):
        sq = jnp.square(u.astype(F32))
        hi = sq.astype(BF)
        lo = (sq - hi.astype(F32)).astype(BF)
        return jnp.exp(mm_t(jnp.concatenate([u, hi, lo], axis=1), fx[0])) * SCALE

    pq[...] = phi(q).astype(BF)
    phk = (phi(k) * live_of(meta, s, rows)).astype(BF)
    pk[...] = phk
    lhs = jnp.concatenate([v.T, jnp.ones((16, rows), BF)], axis=0)
    ds = mm(lhs, phk)
    at = pl.multiple_of((p % 2) * 64, 64)
    xs[0, pl.ds(at, 64), :256] = ds[:64, :256]
    xs[0, pl.ds(at, 64), 256:] = ds[64:128, 256:]
    row = lax.broadcasted_iota(jnp.int32, (8, 512), 0)
    z = ds[128:129]

    @pl.when(p % 2 == 0)
    def _():
        xs[0, 128:136] = jnp.where(row == 0, z, 0.0)

    @pl.when(p % 2 == 1)
    def _():
        xs[0, 128:136] = jnp.where(row == 1, z, xs[0, 128:136])


def below(rows, cols, shift):
    i = lax.broadcasted_iota(jnp.int32, (rows, cols), 0) + shift
    return lax.broadcasted_iota(jnp.int32, (rows, cols), 1) <= i


def local_kernel(pq, pk, vv, nd):
    rows = pq.shape[0]
    half = rows // 2
    v = vv[...]
    values = jnp.concatenate([v, jnp.ones_like(v)], axis=1)
    head = head_of(2 * LANES)
    top, low = None, None
    for h in range(2):
        cols = slice(256 * h, 256 * h + 256)
        mine = jnp.where(head == h, values, jnp.zeros_like(values))
        a0 = mm_t(pq[:half, cols], pk[:half, cols])
        a0 = jnp.where(below(half, half, 0), a0, 0.0).astype(BF)
        a1 = mm_t(pq[half:, cols], pk[:, cols])
        a1 = jnp.where(below(half, rows, half), a1, 0.0).astype(BF)
        t, l = mm(a0, mine[:half]), mm(a1, mine)
        top, low = (t, l) if h == 0 else (top + t, low + l)
    nd[:half] = top
    nd[half:] = low


def gelu_parts(u):
    c0, c1 = 0.7978845608028654, 0.044715
    sq = u * u
    t = jnp.tanh(u * (c0 + (c0 * c1) * sq))
    half_up = 0.5 + 0.5 * t
    slope = half_up + (0.5 * u) * (1.0 - t * t) * (c0 + (3.0 * c0 * c1) * sq)
    return u * half_up, slope


def state_t(xs, p):
    at = (p % 2) * 64
    return xs[p // 2, at : at + 64, :], xs[p // 2, 128 + p % 2 : 129 + p % 2, :]


def middle_kernel(
    s, meta, x, dy, pq, nd, xs, gain, bias, wo, wup, wdown,
    out, dx1, dx, a_low, db, h2, df, gl, du, gs, ng,
    x1, xhat, inv, f, dh2, den,
):
    c = pl.program_id(0)
    rows = x.shape[1]
    live = live_of(meta, s, rows)
    col = lanes_of(512)

    @pl.when(c == 0)
    def _():
        for p in range(4):
            st, z = state_t(xs, p)
            zero = jnp.zeros_like(st)
            zb = jnp.broadcast_to(z, st.shape)
            rhs = jnp.concatenate(
                [
                    jnp.where(col < 256, st, zero),
                    jnp.where(col >= 256, st, zero),
                    jnp.where(col < 256, zb, zero),
                    jnp.where(col >= 256, zb, zero),
                ],
                axis=0,
            ).astype(BF)
            both = mm_t(pq[:, 512 * p : 512 * p + 512], rhs) + nd[:, 256 * p : 256 * p + 256]
            lanes = slice(LANES * p, LANES * p + LANES)
            den[:, lanes] = both[:, LANES:]
            f[:, lanes] = both[:, :LANES] / both[:, LANES:]
        a_low[...] = f[...].astype(BF)
        mid = x[0].astype(F32) + live * mm(a_low[...], wo[...])
        x1[...] = mid
        h, xh, iv = norm(mid, gain[...], bias[...])
        h2[...] = h.astype(BF)
        xhat[...] = xh
        inv[...] = jnp.broadcast_to(iv, inv.shape)
        df[...] = (live * dy[0].astype(F32)).astype(BF)

    g, slope = gelu_parts(mm(h2[...], wup[...]))
    g = g.astype(BF)
    gl[...] = g
    d = (slope * mm_t(df[...], wdown[...])).astype(BF)
    du[...] = d
    part = mm(g, wdown[...])
    back = mm_t(d, wup[...])

    @pl.when(c == 0)
    def _():
        x1[...] += live * part
        dh2[...] = back

    @pl.when(c > 0)
    def _():
        x1[...] += live * part
        dh2[...] += back

    @pl.when(c == pl.num_programs(0) - 1)
    def _():
        out[...] = x1[...].astype(BF)
        e = dh2[...]
        xh = xhat[...]
        ng[...] = two_rows(
            jnp.sum(e * xh, axis=0, keepdims=True), jnp.sum(e, axis=0, keepdims=True)
        )
        g1 = dy[0].astype(F32) + norm_grad(e, xh, inv[:, :1], gain[...])
        dx1[...] = g1
        db[...] = (live * g1).astype(BF)
        da = mm_t(db[...], wo[...])
        block = jnp.where(
            lax.broadcasted_iota(jnp.int32, (2 * LANES, LANES), 0) % LANES // 64
            == lax.broadcasted_iota(jnp.int32, (2 * LANES, LANES), 1) // 64,
            -1.0,
            0.0,
        ).astype(BF)
        slot = lanes_of(LANES) % 64
        for p in range(4):
            lanes = slice(LANES * p, LANES * p + LANES)
            dn = da[:, lanes] / den[:, lanes]
            w = dn * f[:, lanes]
            hi = w.astype(BF)
            lo = (w - hi.astype(F32)).astype(BF)
            dd = mm(jnp.concatenate([hi, lo], axis=1), block)
            hi = dd.astype(BF).astype(F32)
            lo = dd - hi
            two = jnp.where((slot == 0) | (slot == 2), hi, jnp.where(slot == 1, lo, 0.0))
            both = jnp.concatenate([dn.astype(BF), two.astype(BF)], axis=1)
            dx[:, 256 * p : 256 * p + 256] = both
            g = mm(both.T, pq[:, 512 * p : 512 * p + 512])
            at = (p % 2) * 64
            gs[p // 2, at : at + 64, :] = jnp.where(col < 256, g[:64], g[64:128])
            z = jnp.where(col < 256, g[128:129] + g[129:130], g[192:193] + g[193:194])
            if p % 2 == 0:
                first = z
            else:
                gs[p // 2, 128:136, :] = two_rows(first, z)


def inner_kernel(qs, ks, vv, pq, pk, dx, xs, fx, dq, dkl, dvl):
    p = pl.program_id(0)
    rows = pq.shape[0]
    half = rows // 2
    col = lanes_of(512)
    slot = lanes_of(LANES) % 64
    head = head_of(2 * LANES)
    ones = jnp.broadcast_to(jnp.where(slot < 2, 1.0, 0.0), (rows, LANES)).astype(BF)
    v1 = jnp.concatenate([vv[...], ones], axis=1)
    st = xs[0, pl.ds(pl.multiple_of((p % 2) * 64, 64), 64), :]
    zs = xs[0, 128:136, :]
    z = jnp.where(p % 2 == 0, zs[0:1], zs[1:2])
    zh = z.astype(BF).astype(F32)
    zl = z - zh
    zero = jnp.zeros_like(st)
    row = lax.broadcasted_iota(jnp.int32, (64, 512), 0)
    zr = jnp.where(row < 2, zh, jnp.where(row == 2, zl, 0.0))
    rhs = jnp.concatenate(
        [
            jnp.where(col < 256, st, zero),
            jnp.where(col >= 256, st, zero),
            jnp.where(col < 256, zr, zero),
            jnp.where(col >= 256, zr, zero),
        ],
        axis=0,
    ).astype(BF)
    d = dx[...]
    far = mm(d, rhs)
    eqs, eks = [], []
    top, low = None, None
    for h in range(2):
        cols = slice(256 * h, 256 * h + 256)
        mine = jnp.where(head == h, d, jnp.zeros_like(d))
        q, k = pq[:, cols], pk[:, cols]
        a0 = jnp.where(below(half, half, 0), mm_t(mine[:half], v1[:half]), 0.0).astype(BF)
        a1 = jnp.where(below(half, rows, half), mm_t(mine[half:], v1), 0.0).astype(BF)
        dpq = jnp.concatenate([mm(a0, k[:half]), mm(a1, k)], axis=0) + far[:, cols]
        eqs.append((dpq * q.astype(F32)).astype(BF))
        i0 = lax.broadcasted_iota(jnp.int32, (half, rows), 1)
        up0 = i0 >= lax.broadcasted_iota(jnp.int32, (half, rows), 0)
        up1 = up0[:, :half]
        b0 = jnp.where(up0, mm_t(v1[:half], mine), 0.0).astype(BF)
        b1 = jnp.where(up1, mm_t(v1[half:], mine[half:]), 0.0).astype(BF)
        dpk = jnp.concatenate([mm(b0, q), mm(b1, q[half:])], axis=0)
        eks.append((dpk * k.astype(F32)).astype(BF))
        c0 = jnp.where(up0, mm_t(k[:half], q), 0.0).astype(BF)
        c1 = jnp.where(up1, mm_t(k[half:], q[half:]), 0.0).astype(BF)
        t, l = mm(c0, mine[:, :LANES]), mm(c1, mine[half:, :LANES])
        top, low = (t, l) if h == 0 else (top + t, low + l)
    fw = fx[0, :, : 2 * LANES]
    r = mm(jnp.concatenate(eqs, axis=1), fw)
    dq[...] = (SHRINK * (r[:, :LANES] + 2.0 * qs[...].astype(F32) * r[:, LANES:])).astype(BF)
    r = mm(jnp.concatenate(eks, axis=1), fw)
    dkl[...] = r[:, :LANES] + 2.0 * ks[...].astype(F32) * r[:, LANES:]
    dvl[:half] = top
    dvl[half:] = low


def last_kernel(
    s, x, dx1, gain, ks, vv, pk, rs, fx, dq, dkl, dvl, wq, wk, wv,
    grad, dk, dv, ng, dh1,
):
    p = pl.program_id(0)
    rows = pk.shape[0]
    col = lanes_of(512)
    slot = lanes_of(LANES) % 64
    ones = jnp.broadcast_to(jnp.where(slot < 2, 1.0, 0.0), (rows, LANES)).astype(BF)
    v1 = jnp.concatenate([vv[...], ones], axis=1)
    st = rs[0, pl.ds(pl.multiple_of((p % 2) * 64, 64), 64), :]
    zs = rs[0, 128:136, :]
    z = jnp.where(p % 2 == 0, zs[0:1], zs[1:2])
    zh = z.astype(BF).astype(F32)
    zl = z - zh
    zero = jnp.zeros_like(st)
    row = lax.broadcasted_iota(jnp.int32, (64, 512), 0)
    zr = jnp.where(row == 0, zh, jnp.where(row == 1, zl, 0.0))
    rhs = jnp.concatenate(
        [
            jnp.where(col < 256, st, zero),
            jnp.where(col >= 256, st, zero),
            jnp.where(col < 256, zr, zero),
            jnp.where(col >= 256, zr, zero),
        ],
        axis=0,
    ).astype(BF)
    dpk = mm(v1, rhs)
    ek = (dpk * pk[...].astype(F32)).astype(BF)
    r = mm(ek, fx[0, :, : 2 * LANES])
    k = SHRINK * (dkl[...] + r[:, :LANES] + 2.0 * ks[...].astype(F32) * r[:, LANES:])
    k = k.astype(BF)
    v = (dvl[...] + mm_t(pk[...], rhs[:LANES])).astype(BF)
    dk[...], dv[...] = k, v
    w = jnp.concatenate([wq[...], wk[...], wv[...]], axis=1)
    part = mm_t(jnp.concatenate([dq[...], k, v], axis=1), w)

    @pl.when(p == 0)
    def _():
        dh1[...] = part

    @pl.when(p > 0)
    def _():
        dh1[...] += part

    @pl.when(p == pl.num_programs(0) - 1)
    def _():
        _, xh, inv = norm(x[0].astype(F32), gain[...], gain[...])
        e = dh1[...]
        ng[...] = two_rows(
            jnp.sum(e * xh, axis=0, keepdims=True), jnp.sum(e, axis=0, keepdims=True)
        )
        grad[...] = dx1[...] + norm_grad(e, xh, inv, gain[...])


def weight_kernel(a0, a1, b0, b1, out):
    out[...] = mm(a0[...].T, b0[...]) + mm(a1[...].T, b1[...])


def params(limit=60):
    return pltpu.CompilerParams(vmem_limit_bytes=limit * 2**20)


def full(shape):
    return pl.BlockSpec(shape, lambda p, n=len(shape): (0,) * n)


def of_seq(s, shape):
    return pl.BlockSpec((1,) + shape, lambda p: (s, 0, 0))


def cols(rows, width, first=0):
    return pl.BlockSpec((rows, width), lambda p: (0, first + p))


SMEM = pl.BlockSpec(memory_space=pltpu.SMEM)
HALF = pl.BlockSpec((1, 136, 512), lambda p: (p // 2, 0, 0))
PAIR = pl.BlockSpec((1, 512, 384), lambda p: (p, 0, 0))


def arr(shape, dtype):
    return jax.ShapeDtypeStruct(shape, dtype)


def call(kernel, grid, ins, outs, scratch=(), flops=0, nbytes=0):
    return pl.pallas_call(
        kernel,
        grid=(grid,),
        in_specs=ins,
        out_specs=[o[0] for o in outs],
        out_shape=[arr(*o[1:]) for o in outs],
        scratch_shapes=list(scratch),
        compiler_params=params(),
        cost_estimate=pl.CostEstimate(flops=flops, bytes_accessed=nbytes, transcendentals=0),
    )


def weight_grad(a, b, over_a):
    m, n, rows = a[0].shape[1], b[0].shape[1], a[0].shape[0]
    grid = (m if over_a else n) // 512 if (m if over_a else n) > 512 else 1
    am, bn = (m // grid, n) if over_a else (m, n // grid)
    index_a = (lambda p: (0, p)) if over_a else (lambda p: (0, 0))
    index_b = (lambda p: (0, 0)) if over_a else (lambda p: (0, p))
    index_o = (lambda p: (p, 0)) if over_a else (lambda p: (0, p))
    sa, sb = pl.BlockSpec((rows, am), index_a), pl.BlockSpec((rows, bn), index_b)
    return call(
        weight_kernel, grid, [sa, sa, sb, sb],
        [(pl.BlockSpec((am, bn), index_o), (m, n), F32)],
        flops=4 * rows * m * n, nbytes=4 * m * n + 4 * rows * (m + n),
    )(a[0], a[1], b[0], b[1])[0]


def feature_blocks(features):
    pairs = features.shape[0] // 2
    f = features.reshape(pairs, 2, 256, 64)
    half = jnp.full((pairs, 256, 64), -0.5, BF)
    zero = jnp.zeros((pairs, 256, 64), BF)
    top = jnp.concatenate([f[:, 0], zero, half, zero, half, zero], axis=2)
    low = jnp.concatenate([zero, f[:, 1], zero, half, zero, half], axis=2)
    return jnp.concatenate([top, low], axis=1)


def body(
    comm,
    inputs,
    lengths,
    norm1_gain,
    norm1_bias,
    qkv_weight,
    features,
    out_weight,
    norm2_gain,
    norm2_bias,
    up_weight,
    down_weight,
    cotangent,
):
    seqs, rows, width = inputs.shape
    wide = up_weight.shape[1]
    first_row = (comm.position() * rows).astype(jnp.int32)
    meta = jnp.concatenate([first_row[None], lengths])
    fx = feature_blocks(features)
    g1, n1, g2, n2 = (v[None] for v in (norm1_gain, norm1_bias, norm2_gain, norm2_bias))
    vec = full((1, width))
    act = cols(rows, LANES)
    big = cols(rows, 512)
    xs_out = (HALF, (2, 136, 512), F32)
    maps, locals_, state = [], [], []
    for s in range(seqs):
        outs = call(
            functools.partial(map_kernel, s), 4,
            [SMEM, of_seq(s, (rows, width)), vec, vec]
            + [cols(width, LANES, 4 * n) for n in range(3)] + [PAIR],
            [(full((rows, width)), (rows, width), BF)]
            + [(act, (rows, width), BF)] * 3
            + [(big, (rows, 2048), BF)] * 2 + [xs_out],
            flops=rows * 4_800_000, nbytes=12 * 2**20,
        )(meta, inputs, g1, n1, qkv_weight, qkv_weight, qkv_weight, fx)
        maps.append(outs)
    state = [comm.carry(m[6], False) for m in maps]
    for s in range(seqs):
        h1, qs, ks, vv, pq, pk, _ = maps[s]
        locals_.append(
            call(
                local_kernel, 4, [big, big, act],
                [(cols(rows, 256), (rows, 1024), F32)],
                flops=rows * 6_000_000, nbytes=7 * 2**20,
            )(pq, pk, vv)[0]
        )
    mids = []
    for s in range(seqs):
        pq = maps[s][4]
        mids.append(
            call(
                functools.partial(middle_kernel, s), wide // 512,
                [SMEM, of_seq(s, (rows, width)), of_seq(s, (rows, width)), full((rows, 2048)),
                 full((rows, 1024)), full((2, 136, 512)), vec, vec, full((width, width)),
                 cols(width, 512), pl.BlockSpec((512, width), lambda p: (p, 0))],
                [(full((rows, width)), (rows, width), BF),
                 (full((rows, width)), (rows, width), F32),
                 (full((rows, 1024)), (rows, 1024), BF),
                 (full((rows, width)), (rows, width), BF),
                 (full((rows, width)), (rows, width), BF),
                 (full((rows, width)), (rows, width), BF),
                 (full((rows, width)), (rows, width), BF),
                 (cols(rows, 512), (rows, wide), BF),
                 (cols(rows, 512), (rows, wide), BF),
                 (full((2, 136, 512)), (2, 136, 512), F32),
                 (full((8, width)), (8, width), F32)],
                scratch=[pltpu.VMEM((rows, width), F32), pltpu.VMEM((rows, width), F32),
                         pltpu.VMEM((rows, LANES), F32)]
                + [pltpu.VMEM((rows, width), F32)] * 3,
                flops=rows * 11_000_000, nbytes=24 * 2**20,
            )(meta, inputs, cotangent, pq, locals_[s], state[s], g2, n2, out_weight,
              up_weight, down_weight)
        )
    out, dx1, dx, a_low, db, h2, df, gl, du, gs, ng2 = zip(*mids)
    later = [comm.carry(g, True) for g in gs]
    down_grad = weight_grad(gl, df, True)
    up_grad = weight_grad(h2, du, False)
    outw_grad = weight_grad(a_low, db, True)
    up_grad = comm.total(up_grad, ("c", "x", "y", "z1", "z2"))
    down_grad = comm.total(down_grad, ("c", "y", "x", "z1", "z2"))
    outw_grad = comm.total(outw_grad, ("c", "x", "y", "z1", "z2"))
    inner = []
    for s in range(seqs):
        h1, qs, ks, vv, pq, pk, _ = maps[s]
        inner.append(
            call(
                inner_kernel, 4, [act, act, act, big, big, cols(rows, 256), HALF, PAIR],
                [(act, (rows, width), BF), (act, (rows, width), F32), (act, (rows, width), F32)],
                flops=rows * 20_000_000, nbytes=11 * 2**20,
            )(qs, ks, vv, pq, pk, dx[s], state[s], fx)
        )
    lasts = []
    for s in range(seqs):
        h1, qs, ks, vv, pq, pk, _ = maps[s]
        dq, dkl, dvl = inner[s]
        lasts.append(
            call(
                functools.partial(last_kernel, s), 4,
                [of_seq(s, (rows, width)), full((rows, width)), vec, act, act, big, HALF, PAIR,
                 act, act, act] + [cols(width, LANES, 4 * n) for n in range(3)],
                [(full((rows, width)), (rows, width), F32), (act, (rows, width), BF),
                 (act, (rows, width), BF), (full((8, width)), (8, width), F32)],
                scratch=[pltpu.VMEM((rows, width), F32)],
                flops=rows * 6_000_000, nbytes=11 * 2**20,
            )(inputs, dx1[s], g1, ks, vv, pk, later[s], fx, dq, dkl, dvl,
              qkv_weight, qkv_weight, qkv_weight)
        )
    grad, dk, dv, ng1 = zip(*lasts)
    h1 = [m[0] for m in maps]
    dq = [i[0] for i in inner]
    qkv_grad = jnp.concatenate(
        [weight_grad(h1, d, True) for d in (dq, dk, dv)], axis=1
    )
    qkv_grad = comm.total(qkv_grad, ("c", "y", "x", "z1", "z2"))
    small = jnp.concatenate([(ng1[0] + ng1[1])[:2], (ng2[0] + ng2[1])[:2]], axis=0)
    small = comm.total_small(small)
    return (
        jnp.stack(out),
        jnp.stack(grad),
        small[0],
        small[1],
        qkv_grad,
        outw_grad,
        small[2],
        small[3],
        up_grad,
        down_grad,
    )


def solution(mesh):
    comm = AnySlice()
    if dict(mesh.shape) == {"seq": 8, "batch": 4}:
        comm = Slice32()
        mesh = Mesh(mesh.devices.reshape(4, 2, 2, 2), comm.axes)
    return jax.shard_map(
        functools.partial(body, comm),
        mesh=mesh,
        in_specs=(comm.rows, comm.lens) + (P(),) * 9 + (comm.rows,),
        out_specs=(comm.rows, comm.rows) + (P(),) * 8,
        check_vma=False,
    )
```

```python
import functools

import jax
import jax.numpy as jnp
from jax import lax
from jax.experimental import pallas as pl
from jax.experimental.pallas import tpu as pltpu
from jax.sharding import Mesh, PartitionSpec as P

EPS = 1e-05
SHRINK = 64 ** (-0.25)
SCALE = 256 ** (-0.5)


class Slice32:
    axes = ("z", "y", "x", "c")
    rows = P(("x", "c"), ("z", "y"), None)
    lens = P(("x", "c"))
    swaps = {
        "c": ("c", [(0, 1), (1, 0)]),
        "x": ("x", [(0, 1), (1, 0)]),
        "y": ("y", [(0, 1), (1, 0)]),
        "z1": ("z", [(0, 1), (1, 0), (2, 3), (3, 2)]),
        "z2": ("z", [(0, 2), (2, 0), (1, 3), (3, 1)]),
    }

    def position(self):
        return lax.axis_index("z") * 2 + lax.axis_index("y")

    def bits(self):
        z = lax.axis_index("z")
        at = [lax.axis_index(a) for a in "cxy"] + [z % 2, z // 2]
        return jnp.stack(at).astype(jnp.int32)

    def swap(self, part, axis):
        name, pairs = self.swaps[axis]
        return lax.ppermute(part, name, pairs)

    def whole_sum(self, part):
        return lax.psum(part, self.axes)

    def carry(self, keep, give, bits, reverse):
        after = yield
        got = self.swap(give, "y")
        after = yield give
        total = simple(add_kernel, after, keep, got)
        hops = [(3, 2), (2, 1), (1, 0)] if reverse else [(0, 1), (1, 2), (2, 3)]
        out, arrived = total, []
        for hop in hops:
            arrived.append(lax.ppermute(out, "z", [hop]))
            after = yield out
            if len(arrived) < 3:
                out = simple(add_kernel, after, total, arrived[-1])
        mine, send = call(
            functools.partial(close_kernel, reverse), 1, [SMEM] + [full(keep.shape)] * 5,
            [(full(keep.shape), keep.shape, F32)] * 2, flops=keep.size, nbytes=28 * keep.size,
        )(bits, keep, got, *arrived, after=after)
        other = self.swap(send, "y")
        yield send
        yield mine, other

    ways = {"x": 1, "y": 2, "z1": 3, "z2": 4}

    def sums(self, give, keep, bits, shapes, order):
        if order is None:
            return self.halves_sum(give, keep, bits, shapes)
        return self.chain_sum(give, keep, bits, shapes, order)

    def chain_sum(self, give, keep, bits, shapes, order):
        after = yield
        got = self.swap(give, "c")
        after = yield give
        rows, wide = give.shape
        part = keep()
        for axis in order:
            half = part.shape[0] // 2
            spec = (full((half, wide)), (half, wide), F32)
            give, part = call(
                functools.partial(fold_kernel, (self.ways[axis],), 2), 1,
                [SMEM] + [full(part.shape)] * 2, [spec] * 2, nbytes=16 * part.size,
            )(bits, part, got, after=after)
            got = self.swap(give, axis)
            after = yield give
        part = simple(add_kernel, after, part, got)
        got = self.swap(part, order[-1])
        after = yield part
        for n in range(len(order) - 1, 0, -1):
            (part,) = self.join((self.ways[order[n]],), bits, (part, got), after)
            got = self.swap(part, order[n - 1])
            after = yield part
        (part,) = self.join((self.ways[order[0]],), bits, (part, got), after)
        got = self.swap(part, "c")
        after = yield part
        yield call(
            last_join_kernel, 1, [SMEM] + [full((rows, wide))] * 2,
            [(full(s), s, F32) for s in shapes], nbytes=16 * rows * wide,
        )(bits, part, got, after=after)

    def halves_sum(self, give, keep, bits, shapes):
        after = yield
        got = self.swap(give, "c")
        after = yield give
        rows, wide = give.shape

        def fold(ways, parts, after, count):
            size = parts[0].shape[0] // count
            shape = (size, wide)
            outs = [(full(shape), shape, F32)] * (4 if count == 4 else 2 * len(ways))
            return call(
                functools.partial(fold_kernel, ways, count), 1,
                [SMEM] + [full(p.shape) for p in parts], outs,
                flops=parts[0].size, nbytes=12 * parts[0].size,
            )(bits, *parts, after=after)

        give_a, give_b, keep_a, keep_b = fold((1, 2), (keep(), got), after, 4)
        got_a, got_b = self.swap(give_a, "x"), self.swap(give_b, "y")
        after = yield give_a
        give_a, give_b, keep_a, keep_b = fold((2, 1), (keep_a, got_a, keep_b, got_b), after, 2)
        got_a, got_b = self.swap(give_a, "y"), self.swap(give_b, "x")
        after = yield give_a
        both = rows // 4
        part = (full((both // 2, wide)), (both // 2, wide), F32)
        ins = [SMEM] + [full((both // 2, wide))] * 4
        give, keep = call(merge_kernel, 1, ins, [part] * 2, nbytes=24 * both * wide)(
            bits, keep_a, got_a, keep_b, got_b, after=after
        )
        got = self.swap(give, "z1")
        after = yield give
        give, keep = fold((4,), (keep, got), after, 2)
        got = self.swap(give, "z2")
        after = yield give
        one = simple(add_kernel, after, keep, got)
        got = self.swap(one, "z2")
        after = yield one
        (two,) = self.join((4,), bits, (one, got), after)
        got = self.swap(two, "z1")
        after = yield two
        (four,) = self.join((3,), bits, (two, got), after)
        a, b = four[: both // 2], four[both // 2 :]
        got_a, got_b = self.swap(a, "y"), self.swap(b, "x")
        after = yield a
        a, b = self.join((2, 1), bits, (a, got_a, b, got_b), after)
        got_a, got_b = self.swap(a, "x"), self.swap(b, "y")
        after = yield a
        part = call(
            functools.partial(join_kernel, (1, 2), True), 1,
            [SMEM] + [full(a.shape)] * 4, [(full((rows, wide)), (rows, wide), F32)],
            nbytes=8 * rows * wide,
        )(bits, a, got_a, b, got_b, after=after)[0]
        got = self.swap(part, "c")
        after = yield part
        yield call(
            last_join_kernel, 1, [SMEM] + [full((rows, wide))] * 2,
            [(full(s), s, F32) for s in shapes], nbytes=16 * rows * wide,
        )(bits, part, got, after=after)

    def join(self, ways, bits, parts, after):
        rows, wide = parts[0].shape
        out = (full((2 * rows, wide)), (2 * rows, wide), F32)
        return call(
            functools.partial(join_kernel, ways, False), 1,
            [SMEM] + [full(p.shape) for p in parts], [out] * len(ways),
            nbytes=16 * rows * wide,
        )(bits, *parts, after=after)


class AnySlice:
    axes = ("seq", "batch")
    rows = P("batch", "seq", None)
    lens = P("batch")

    def position(self):
        return lax.axis_index("seq")

    def bits(self):
        return jnp.zeros((5,), jnp.int32)

    def whole_sum(self, part):
        return lax.psum(part, self.axes)

    def carry(self, keep, give, bits, reverse):
        size = lax.axis_size("seq")

        def shift(part, by):
            pairs = [(i, i + by) for i in range(size - by)]
            return lax.ppermute(part, "seq", [(b, a) for a, b in pairs] if reverse else pairs)

        for _ in range(6):
            yield keep
        out, by = shift(jnp.stack([keep, give]), 1), 1
        while by < size:
            out, by = out + shift(out, by), by * 2
        yield out[0], out[1]

    def sums(self, give, keep, bits, shapes, order):
        for _ in range(11):
            yield give
        part = lax.psum(jnp.concatenate([keep(), give], axis=0), self.axes)
        outs, at = [], 0
        for shape in shapes:
            outs.append(part[:, at : at + shape[1]])
            at += shape[1]
        yield outs


LANES = 128
BF = jnp.bfloat16
F32 = jnp.float32


def mm(a, b):
    return jnp.dot(a, b, preferred_element_type=F32)


def mm_t(a, b):
    return lax.dot_general(a, b, (((1,), (1,)), ((), ())), preferred_element_type=F32)


def lanes_of(width):
    return lax.broadcasted_iota(jnp.int32, (1, width), 1)


def head_of(width):
    return (lanes_of(width) % LANES) // 64


def live_of(meta, s, rows):
    at = lax.broadcasted_iota(jnp.int32, (rows, 1), 0) + meta[0]
    return (at < meta[1 + s]).astype(F32)


def norm(values, gain, bias):
    mu = jnp.mean(values, axis=-1, keepdims=True)
    centred = values - mu
    inv = lax.rsqrt(jnp.mean(centred * centred, axis=-1, keepdims=True) + EPS)
    xhat = centred * inv
    return xhat * gain + bias, xhat, inv


def norm_grad(e, xhat, inv, gain):
    eg = e * gain
    return inv * (
        eg
        - jnp.mean(eg, axis=-1, keepdims=True)
        - xhat * jnp.mean(eg * xhat, axis=-1, keepdims=True)
    )


def blocks_of(f):
    shape = (f.shape[0], LANES)
    own = lax.broadcasted_iota(jnp.int32, shape, 0) // 256 == head_of(LANES)
    diagonal = jnp.where(own, jnp.concatenate([f, f], axis=1), jnp.zeros(shape, BF))
    half = jnp.where(own, -0.5, 0.0).astype(BF)
    return jnp.concatenate([diagonal, half], axis=1)


def two_rows(first, second):
    row = lax.broadcasted_iota(jnp.int32, (8, first.shape[1]), 0)
    return jnp.where(row == 0, first, jnp.where(row == 1, second, 0.0))


def map_kernel(
    s, meta, bits, x, gain, bias, wq, wk, wv, fx, h1, qs, ks, vv, pq, pk, keep, give
):
    p = pl.program_id(0)
    rows = x.shape[1]

    @pl.when(p == 0)
    def _():
        h1[...] = norm(x[0].astype(F32), gain[...], bias[...])[0].astype(BF)

    w = jnp.concatenate([wq[...], wk[...], wv[...]], axis=1)
    qkv = mm(h1[...], w)
    q = (SHRINK * qkv[:, :LANES]).astype(BF)
    k = (SHRINK * qkv[:, LANES : 2 * LANES]).astype(BF)
    v = qkv[:, 2 * LANES :].astype(BF)
    qs[...], ks[...], vv[...] = q, k, v

    fw = blocks_of(fx[0])
    fw = jnp.concatenate([fw, fw[:, LANES:]], axis=1)

    def phi(u):
        sq = jnp.square(u.astype(F32))
        hi = sq.astype(BF)
        lo = (sq - hi.astype(F32)).astype(BF)
        return jnp.exp(mm_t(jnp.concatenate([u, hi, lo], axis=1), fw)) * SCALE

    pq[...] = phi(q).astype(BF)
    phk = (phi(k) * live_of(meta, s, rows)).astype(BF)
    pk[...] = phk
    lhs = jnp.concatenate([v.T, jnp.ones((16, rows), BF)], axis=0)
    ds = mm(lhs, phk)
    for near, xs in ((True, keep), (False, give)):

        @pl.when((p // 2 == bits[2]) == near)
        def _():
            put_state(xs, 2 * (p % 2), ds[:64, :256], ds[128:129, :256])
            put_state(xs, 2 * (p % 2) + 1, ds[64:128, 256:], ds[128:129, 256:])


def put_state(xs, at, state, total):
    xs[at, :64] = state
    xs[at, 64:] = jnp.broadcast_to(total, (8, 256))


def add_kernel(*refs):
    *parts, out = refs
    total = parts[0][...]
    for part in parts[1:]:
        total = total + part[...]
    out[...] = total


def close_kernel(reverse, bits, keep, got, first, second, third, mine, send):
    before = (first[...] + second[...]) + third[...]
    early = (bits[2] == (1 if reverse else 0)).astype(F32)
    mine[...] = before + (1.0 - early) * got[...]
    send[...] = before + early * keep[...]


def fold_kernel(ways, count, bits, *refs):
    if count == 4:
        part, got, *outs = refs
        size = part.shape[0] // 4
        for n, way in enumerate(ways):
            bit = bits[way]
            for out, side in ((outs[n], 1 - bit), (outs[2 + n], bit)):
                at = pl.ds(pl.multiple_of((2 * n + side) * size, 8), size)
                out[...] = part[at, :] + got[at, :]
        return
    pairs = len(ways)
    for n, way in enumerate(ways):
        part, got = refs[2 * n], refs[2 * n + 1]
        outs = refs[2 * pairs :]
        size, bit = part.shape[0] // 2, bits[way]
        for out, side in ((outs[n], 1 - bit), (outs[pairs + n], bit)):
            at = pl.ds(pl.multiple_of(side * size, 8), size)
            out[...] = part[at, :] + got[at, :]


def merge_kernel(bits, part_a, got_a, part_b, got_b, give, keep):
    first = bits[3] == 0
    a, b = part_a[...] + got_a[...], part_b[...] + got_b[...]
    keep[...] = jnp.where(first, a, b)
    give[...] = jnp.where(first, b, a)


def join_kernel(ways, one, bits, *refs):
    outs = refs[2 * len(ways) :]
    for n, way in enumerate(ways):
        part, got = refs[2 * n], refs[2 * n + 1]
        size, bit = part.shape[0], bits[way]
        out, base = (outs[0], 2 * n * size) if one else (outs[n], 0)
        out[pl.ds(pl.multiple_of(base + bit * size, 8), size), :] = part[...]
        out[pl.ds(pl.multiple_of(base + (1 - bit) * size, 8), size), :] = got[...]


def last_join_kernel(bits, part, got, *outs):
    size, at = part.shape[0], 0
    for out in outs:
        wide = out.shape[1]
        for ref, side in ((part, bits[0]), (got, 1 - bits[0])):
            out[pl.ds(pl.multiple_of(side * size, 8), size), :] = ref[:, at : at + wide]
        at += wide


def below(rows, cols, shift):
    i = lax.broadcasted_iota(jnp.int32, (rows, cols), 0) + shift
    return lax.broadcasted_iota(jnp.int32, (rows, cols), 1) <= i


def local_kernel(pq, pk, vv, nd):
    rows = pq.shape[0]
    half = rows // 2
    v = vv[...]
    values = jnp.concatenate([v, jnp.ones_like(v)], axis=1)
    head = head_of(2 * LANES)
    top, low = None, None
    for h in range(2):
        cols = slice(256 * h, 256 * h + 256)
        mine = jnp.where(head == h, values, jnp.zeros_like(values))
        a0 = mm_t(pq[:half, cols], pk[:half, cols])
        a0 = jnp.where(below(half, half, 0), a0, 0.0).astype(BF)
        a1 = mm_t(pq[half:, cols], pk[:, cols])
        a1 = jnp.where(below(half, rows, half), a1, 0.0).astype(BF)
        t, l = mm(a0, mine[:half]), mm(a1, mine)
        top, low = (t, l) if h == 0 else (top + t, low + l)
    nd[:half] = top
    nd[half:] = low


def gelu_parts(u):
    c0, c1 = 0.7978845608028654, 0.044715
    sq = u * u
    t = jnp.tanh(u * (c0 + (c0 * c1) * sq))
    half_up = 0.5 + 0.5 * t
    slope = half_up + (0.5 * u) * (1.0 - t * t) * (c0 + (3.0 * c0 * c1) * sq)
    return u * half_up, slope


def state_of(mine, other, near, first):
    two = [jnp.where(near, mine[first + h], other[first + h]) for h in range(2)]
    st = jnp.concatenate([t[:64] for t in two], axis=1)
    return st, jnp.concatenate([t[64:65] for t in two], axis=1)


def middle_kernel(
    s, meta, bits, x, dy, pq, nd, mine, other, gain, bias, wo, wup, wdown,
    out, dx1, dx, a_low, db, h2, df, gl, du, gs_keep, gs_give, ng,
    x1, xhat, inv, f, dh2, den,
):
    c = pl.program_id(0)
    rows = x.shape[1]
    live = live_of(meta, s, rows)
    col = lanes_of(512)

    @pl.when(c == 0)
    def _():
        for p in range(4):
            st, z = state_of(mine, other, bits[2] == p // 2, 2 * (p % 2))
            zero = jnp.zeros_like(st)
            zb = jnp.broadcast_to(z, st.shape)
            rhs = jnp.concatenate(
                [
                    jnp.where(col < 256, st, zero),
                    jnp.where(col >= 256, st, zero),
                    jnp.where(col < 256, zb, zero),
                    jnp.where(col >= 256, zb, zero),
                ],
                axis=0,
            ).astype(BF)
            both = mm_t(pq[:, 512 * p : 512 * p + 512], rhs) + nd[:, 256 * p : 256 * p + 256]
            lanes = slice(LANES * p, LANES * p + LANES)
            den[:, lanes] = both[:, LANES:]
            f[:, lanes] = both[:, :LANES] / both[:, LANES:]
        a_low[...] = f[...].astype(BF)
        mid = x[0].astype(F32) + live * mm(a_low[...], wo[...])
        x1[...] = mid
        h, xh, iv = norm(mid, gain[...], bias[...])
        h2[...] = h.astype(BF)
        xhat[...] = xh
        inv[...] = jnp.broadcast_to(iv, inv.shape)
        df[...] = (live * dy[0].astype(F32)).astype(BF)

    g, slope = gelu_parts(mm(h2[...], wup[...]))
    g = g.astype(BF)
    gl[...] = g
    d = (slope * mm_t(df[...], wdown[...])).astype(BF)
    du[...] = d
    part = mm(g, wdown[...])
    back = mm_t(d, wup[...])

    @pl.when(c == 0)
    def _():
        x1[...] += live * part
        dh2[...] = back

    @pl.when(c > 0)
    def _():
        x1[...] += live * part
        dh2[...] += back

    @pl.when(c == pl.num_programs(0) - 1)
    def _():
        out[...] = x1[...].astype(BF)
        e = dh2[...]
        xh = xhat[...]
        ng[...] = two_rows(
            jnp.sum(e * xh, axis=0, keepdims=True), jnp.sum(e, axis=0, keepdims=True)
        )
        g1 = dy[0].astype(F32) + norm_grad(e, xh, inv[:, :1], gain[...])
        dx1[...] = g1
        db[...] = (live * g1).astype(BF)
        da = mm_t(db[...], wo[...])
        block = jnp.where(
            lax.broadcasted_iota(jnp.int32, (2 * LANES, LANES), 0) % LANES // 64
            == lax.broadcasted_iota(jnp.int32, (2 * LANES, LANES), 1) // 64,
            -1.0,
            0.0,
        ).astype(BF)
        slot = lanes_of(LANES) % 64
        for p in range(4):
            lanes = slice(LANES * p, LANES * p + LANES)
            dn = da[:, lanes] / den[:, lanes]
            w = dn * f[:, lanes]
            hi = w.astype(BF)
            lo = (w - hi.astype(F32)).astype(BF)
            dd = mm(jnp.concatenate([hi, lo], axis=1), block)
            hi = dd.astype(BF).astype(F32)
            lo = dd - hi
            two = jnp.where((slot == 0) | (slot == 2), hi, jnp.where(slot == 1, lo, 0.0))
            both = jnp.concatenate([dn.astype(BF), two.astype(BF)], axis=1)
            dx[:, 256 * p : 256 * p + 256] = both
            g = mm(both.T, pq[:, 512 * p : 512 * p + 512])
            for near, gs in ((True, gs_keep), (False, gs_give)):

                @pl.when((bits[2] == p // 2) == near)
                def _(gs=gs, g=g):
                    for h in range(2):
                        side, at = slice(256 * h, 256 * h + 256), 128 + 64 * h
                        z = g[at : at + 1, side] + g[at + 1 : at + 2, side]
                        put_state(gs, 2 * (p % 2) + h, g[64 * h : 64 * h + 64, side], z)


def inner_kernel(bits, qs, ks, vv, pq, pk, dx, mine, other, fx, dq, dkl, dvl):
    p = pl.program_id(0)
    rows = pq.shape[0]
    half = rows // 2
    col = lanes_of(512)
    slot = lanes_of(LANES) % 64
    head = head_of(2 * LANES)
    ones = jnp.broadcast_to(jnp.where(slot < 2, 1.0, 0.0), (rows, LANES)).astype(BF)
    v1 = jnp.concatenate([vv[...], ones], axis=1)
    st, z = state_of(mine, other, bits[2] == p // 2, 0)
    zh = z.astype(BF).astype(F32)
    zl = z - zh
    zero = jnp.zeros_like(st)
    row = lax.broadcasted_iota(jnp.int32, (64, 512), 0)
    zr = jnp.where(row < 2, zh, jnp.where(row == 2, zl, 0.0))
    rhs = jnp.concatenate(
        [
            jnp.where(col < 256, st, zero),
            jnp.where(col >= 256, st, zero),
            jnp.where(col < 256, zr, zero),
            jnp.where(col >= 256, zr, zero),
        ],
        axis=0,
    ).astype(BF)
    d = dx[...]
    far = mm(d, rhs)
    eqs, eks = [], []
    top, low = None, None
    for h in range(2):
        cols = slice(256 * h, 256 * h + 256)
        own = jnp.where(head == h, d, jnp.zeros_like(d))
        q, k = pq[:, cols], pk[:, cols]
        a0 = jnp.where(below(half, half, 0), mm_t(own[:half], v1[:half]), 0.0).astype(BF)
        a1 = jnp.where(below(half, rows, half), mm_t(own[half:], v1), 0.0).astype(BF)
        dpq = jnp.concatenate([mm(a0, k[:half]), mm(a1, k)], axis=0) + far[:, cols]
        eqs.append((dpq * q.astype(F32)).astype(BF))
        i0 = lax.broadcasted_iota(jnp.int32, (half, rows), 1)
        up0 = i0 >= lax.broadcasted_iota(jnp.int32, (half, rows), 0)
        up1 = up0[:, :half]
        b0 = jnp.where(up0, mm_t(v1[:half], own), 0.0).astype(BF)
        b1 = jnp.where(up1, mm_t(v1[half:], own[half:]), 0.0).astype(BF)
        dpk = jnp.concatenate([mm(b0, q), mm(b1, q[half:])], axis=0)
        eks.append((dpk * k.astype(F32)).astype(BF))
        c0 = jnp.where(up0, mm_t(k[:half], q), 0.0).astype(BF)
        c1 = jnp.where(up1, mm_t(k[half:], q[half:]), 0.0).astype(BF)
        t, l = mm(c0, own[:, :LANES]), mm(c1, own[half:, :LANES])
        top, low = (t, l) if h == 0 else (top + t, low + l)
    fw = blocks_of(fx[0])
    r = mm(jnp.concatenate(eqs, axis=1), fw)
    dq[...] = (SHRINK * (r[:, :LANES] + 2.0 * qs[...].astype(F32) * r[:, LANES:])).astype(BF)
    r = mm(jnp.concatenate(eks, axis=1), fw)
    dkl[...] = r[:, :LANES] + 2.0 * ks[...].astype(F32) * r[:, LANES:]
    dvl[:half] = top
    dvl[half:] = low


def last_kernel(
    s, bits, x, dx1, gain, ks, vv, pk, mine, other, fx, dq, dkl, dvl, wq, wk, wv,
    grad, dk, dv, ng, dh1,
):
    p = pl.program_id(0)
    rows = pk.shape[0]
    col = lanes_of(512)
    slot = lanes_of(LANES) % 64
    ones = jnp.broadcast_to(jnp.where(slot < 2, 1.0, 0.0), (rows, LANES)).astype(BF)
    v1 = jnp.concatenate([vv[...], ones], axis=1)
    st, z = state_of(mine, other, bits[2] == p // 2, 0)
    zh = z.astype(BF).astype(F32)
    zl = z - zh
    zero = jnp.zeros_like(st)
    row = lax.broadcasted_iota(jnp.int32, (64, 512), 0)
    zr = jnp.where(row == 0, zh, jnp.where(row == 1, zl, 0.0))
    rhs = jnp.concatenate(
        [
            jnp.where(col < 256, st, zero),
            jnp.where(col >= 256, st, zero),
            jnp.where(col < 256, zr, zero),
            jnp.where(col >= 256, zr, zero),
        ],
        axis=0,
    ).astype(BF)
    dpk = mm(v1, rhs)
    ek = (dpk * pk[...].astype(F32)).astype(BF)
    r = mm(ek, blocks_of(fx[0]))
    k = SHRINK * (dkl[...] + r[:, :LANES] + 2.0 * ks[...].astype(F32) * r[:, LANES:])
    k = k.astype(BF)
    v = (dvl[...] + mm_t(pk[...], rhs[:LANES])).astype(BF)
    dk[...], dv[...] = k, v
    w = jnp.concatenate([wq[...], wk[...], wv[...]], axis=1)
    part = mm_t(jnp.concatenate([dq[...], k, v], axis=1), w)

    @pl.when(p == 0)
    def _():
        dh1[...] = part

    @pl.when(p > 0)
    def _():
        dh1[...] += part

    @pl.when(p == pl.num_programs(0) - 1)
    def _():
        _, xh, inv = norm(x[0].astype(F32), gain[...], gain[...])
        e = dh1[...]
        ng[...] = two_rows(
            jnp.sum(e * xh, axis=0, keepdims=True), jnp.sum(e, axis=0, keepdims=True)
        )
        grad[...] = dx1[...] + norm_grad(e, xh, inv, gain[...])


def weight_kernel(c, a0, a1, b0, b1, out):
    out[...] = mm(a0[...].T, b0[...]) + mm(a1[...].T, b1[...])


def late_kernel(c, a0, a1, b0, b1, b2, b3, b4, b5, n0, n1, n2, n3, o0, o1, d0, d1, out):
    a = jnp.concatenate([a0[...].T, a1[...].T], axis=1)
    for n, (first, second) in enumerate(((b0, b1), (b2, b3), (b4, b5))):
        both = jnp.concatenate([first[...], second[...]], axis=0)
        out[:, 512 * n : 512 * n + 512] = mm(a, both)
    out[:, 1536:2048] = mm(o0[...].T, d0[...]) + mm(o1[...].T, d1[...])
    sums = [n0[...] + n1[...], n2[...] + n3[...]]
    out[:, 2048:] = jnp.concatenate(sums + [jnp.zeros((112, out.shape[0]), F32)], axis=0).T


def params(limit=36):
    return pltpu.CompilerParams(vmem_limit_bytes=limit * 2**20)


def full(shape):
    return pl.BlockSpec(shape, lambda p, n=len(shape): (0,) * n)


def of_seq(s, shape):
    return pl.BlockSpec((1,) + shape, lambda p: (s, 0, 0))


def cols(rows, width, first=0):
    return pl.BlockSpec((rows, width), lambda p: (0, first + p))


SMEM = pl.BlockSpec(memory_space=pltpu.SMEM)
HEADS = pl.BlockSpec((2, 72, 256), lambda p: (p % 2, 0, 0))
PAIR = pl.BlockSpec((1, 512, 64), lambda p: (p, 0, 0))


def arr(shape, dtype):
    return jax.ShapeDtypeStruct(shape, dtype)


ANY = pl.BlockSpec(memory_space=pl.ANY)


def call(kernel, grid, ins, outs, scratch=(), flops=0, nbytes=0, scalars=0):
    def run(*args, after=()):
        count, waits = len(ins) + scalars, len(after)

        def waiting(*refs):
            kernel(*refs[:count], *refs[count + waits :])

        return pl.pallas_call(
            waiting,
            grid_spec=pltpu.PrefetchScalarGridSpec(
                num_scalar_prefetch=scalars,
                grid=(grid,),
                in_specs=list(ins) + [ANY] * waits,
                out_specs=[o[0] for o in outs],
                scratch_shapes=list(scratch),
            ),
            out_shape=[arr(*o[1:]) for o in outs],
            compiler_params=params(),
            cost_estimate=pl.CostEstimate(flops=flops, bytes_accessed=nbytes, transcendentals=0),
        )(*args, *after)

    return run


def simple(kernel, after, *parts):
    spec = full(parts[0].shape)
    return call(
        kernel, 1, [spec] * len(parts), [(spec, parts[0].shape, F32)],
        flops=parts[0].size, nbytes=12 * parts[0].size,
    )(*parts, after=after)[0]


def half_of(give):
    return (lambda c: 1 - c[0]) if give else (lambda c: c[0])


def whole(shape):
    return pl.BlockSpec(shape, lambda p, c: (0,) * len(shape))


def up_weights(give, bits, h2, du, after=()):
    rows, n = du[0].shape
    m = h2[0].shape[1] // 2
    at = half_of(give)
    sa = pl.BlockSpec((rows, m), lambda p, c: (0, at(c)))
    sb = pl.BlockSpec((rows, 512), lambda p, c: (0, p))
    return call(
        weight_kernel, n // 512, [sa, sa, sb, sb],
        [(pl.BlockSpec((m, 512), lambda p, c: (0, p)), (m, n), F32)],
        flops=4 * rows * m * n, nbytes=4 * m * n + 4 * rows * n, scalars=1,
    )(bits, *h2, *du, after=after)[0]


def down_weights(give, bits, gl, df, after=()):
    rows, n = df[0].shape
    m = gl[0].shape[1] // 2
    at, grid = half_of(give), m // 512
    sa = pl.BlockSpec((rows, 512), lambda p, c: (0, grid * at(c) + p))
    sb = whole((rows, n))
    return call(
        weight_kernel, grid, [sa, sa, sb, sb],
        [(pl.BlockSpec((512, n), lambda p, c: (p, 0)), (m, n), F32)],
        flops=4 * rows * m * n, nbytes=4 * m * n + 4 * rows * m, scalars=1,
    )(bits, *gl, *df, after=after)[0]


def late_weights(give, bits, h1, dq, dk, dv, ng1, ng2, a, db, after=()):
    rows, n = dk[0].shape
    m = n // 2
    at = half_of(give)
    sa, sb = pl.BlockSpec((rows, m), lambda p, c: (0, at(c))), whole((rows, n))
    sn = pl.BlockSpec((8, m), lambda p, c: (0, at(c)))
    wide = 4 * n + LANES
    return call(
        late_kernel, 1, [sa] * 2 + [sb] * 6 + [sn] * 4 + [sa] * 2 + [sb] * 2,
        [(whole((m, wide)), (m, wide), F32)],
        flops=16 * rows * m * n, nbytes=16 * m * n + 16 * rows * n, scalars=1,
    )(bits, *h1, *dq, *dk, *dv, *ng1, *ng2, *a, *db, after=after)[0]


ORDER = (
    "M0", "f", "M1", "f", "g", "A0", "f", "g", "A1", "f", "g", "f", "g", "N0", "g", "p", "N1",
    "p", "q", "Gu", "u", "Ku", "Gd", "p", "q", "d", "Kd", "u", "I0", "p", "q", "d", "I1",
    "p", "q", "u", "L0", "q", "d", "L1", "Gk", "k", "Kk", "u", "d", "k", "u", "d", "k",
    "u", "d", "k", "u", "d", "k", "u", "d", "k", "u", "d", "k", "u", "d", "k", "k", "k",
)


def body(
    comm,
    inputs,
    lengths,
    norm1_gain,
    norm1_bias,
    qkv_weight,
    features,
    out_weight,
    norm2_gain,
    norm2_bias,
    up_weight,
    down_weight,
    cotangent,
):
    seqs, rows, width = inputs.shape
    wide = up_weight.shape[1]
    first_row = (comm.position() * rows).astype(jnp.int32)
    meta = jnp.concatenate([first_row[None], lengths])
    fx = features.reshape(4, 512, 64)
    bits = comm.bits()
    g1, n1, g2, n2 = (v[None] for v in (norm1_gain, norm1_bias, norm2_gain, norm2_bias))
    vec = full((1, width))
    act = cols(rows, LANES)
    big = cols(rows, 512)
    heads = (4, 72, 256)
    states = [(full(heads), heads, F32)] * 2

    def maps_of(s, after):
        return call(
            functools.partial(map_kernel, s), 4,
            [SMEM, SMEM, of_seq(s, (rows, width)), vec, vec]
            + [cols(width, LANES, 4 * n) for n in range(3)] + [PAIR],
            [(full((rows, width)), (rows, width), BF)]
            + [(act, (rows, width), BF)] * 3
            + [(big, (rows, 2048), BF)] * 2 + states,
            flops=rows * 4_800_000, nbytes=12 * 2**20,
        )(meta, bits, inputs, g1, n1, qkv_weight, qkv_weight, qkv_weight, fx, after=after)

    def locals_of(s, after):
        _, _, _, vv, pq, pk, _, _ = maps[s]
        return call(
            local_kernel, 4, [big, big, act],
            [(cols(rows, 256), (rows, 1024), F32)],
            flops=rows * 6_000_000, nbytes=7 * 2**20,
        )(pq, pk, vv, after=after)[0]

    def middle_of(s, prefix, after):
        pq = maps[s][4]
        return call(
                functools.partial(middle_kernel, s), wide // 512,
                [SMEM, SMEM, of_seq(s, (rows, width)), of_seq(s, (rows, width)), full((rows, 2048)),
                 full((rows, 1024)), full(heads), full(heads), vec, vec, full((width, width)),
                 cols(width, 512), pl.BlockSpec((512, width), lambda p: (p, 0))],
                [(full((rows, width)), (rows, width), BF),
                 (full((rows, width)), (rows, width), F32),
                 (full((rows, 1024)), (rows, 1024), BF),
                 (full((rows, width)), (rows, width), BF),
                 (full((rows, width)), (rows, width), BF),
                 (full((rows, width)), (rows, width), BF),
                 (full((rows, width)), (rows, width), BF),
                 (cols(rows, 512), (rows, wide), BF),
                 (cols(rows, 512), (rows, wide), BF),
                 *states,
                 (full((8, width)), (8, width), F32)],
                scratch=[pltpu.VMEM((rows, width), F32), pltpu.VMEM((rows, width), F32),
                         pltpu.VMEM((rows, LANES), F32)]
                + [pltpu.VMEM((rows, width), F32)] * 3,
                flops=rows * 11_000_000, nbytes=24 * 2**20,
            )(meta, bits, inputs, cotangent, pq, locals_[s], *prefix, g2, n2, out_weight,
              up_weight, down_weight, after=after)

    def inner(s, after):
        _, qs, ks, vv, pq, pk, _, _ = maps[s]
        return call(
            inner_kernel, 4,
            [SMEM, act, act, act, big, big, cols(rows, 256), HEADS, HEADS, PAIR],
            [(act, (rows, width), BF), (act, (rows, width), F32), (act, (rows, width), F32)],
            flops=rows * 20_000_000, nbytes=11 * 2**20,
        )(bits, qs, ks, vv, pq, pk, mids[s][2], *state[s], fx, after=after)

    def last(s, later, after):
        _, qs, ks, vv, pq, pk, _, _ = maps[s]
        return call(
            functools.partial(last_kernel, s), 4,
            [SMEM, of_seq(s, (rows, width)), full((rows, width)), vec, act, act, big, HEADS, HEADS,
             PAIR,
             act, act, act] + [cols(width, LANES, 4 * n) for n in range(3)],
            [(full((rows, width)), (rows, width), F32), (act, (rows, width), BF),
             (act, (rows, width), BF), (full((8, width)), (8, width), F32)],
            scratch=[pltpu.VMEM((rows, width), F32)],
            flops=rows * 6_000_000, nbytes=11 * 2**20,
        )(bits, inputs, mids[s][1], g1, ks, vv, pk, *later, fx, *inners[s],
          qkv_weight, qkv_weight, qkv_weight, after=after)

    maps, locals_, mids, state, inners, lasts, kept, flows = {}, {}, {}, {}, {}, {}, {}, {}

    def of_mids(*index):
        return [[mids[s][n] for s in range(seqs)] for n in index]

    def weights(name, give, after):
        if name == "u":
            return up_weights(give, bits, *of_mids(5, 8), after=after)
        if name == "d":
            return down_weights(give, bits, *of_mids(7, 6), after=after)
        h1 = [maps[s][0] for s in range(seqs)]
        dq = [inners[s][0] for s in range(seqs)]
        dk, dv, ng1 = ([lasts[s][n] for s in range(seqs)] for n in (1, 2, 3))
        return late_weights(give, bits, h1, dq, dk, dv, ng1, *of_mids(11, 3, 4), after=after)

    shapes = {
        "u": ((width, wide),),
        "d": ((wide, width),),
        "k": ((width, 3 * width), (width, width), (width, LANES)),
    }
    orders = {"u": ("x", "y", "z1", "z2"), "d": ("y", "x", "z1", "z2"), "k": None}

    def play(items, token):
        for item in items:
            after = () if token is None else (token,)
            kind, name = item[0], item[-1]
            s = int(name) if name in "01" else None
            if kind == "M":
                maps[s] = maps_of(s, after)
                token = maps[s][7]
                flows["fg"[s]] = comm.carry(maps[s][6], token, bits, False)
                next(flows["fg"[s]])
            elif kind == "A":
                token = locals_[s] = locals_of(s, after)
            elif kind == "N":
                state[s] = next(flows["fg"[s]])
                mids[s] = middle_of(s, state[s], after)
                token = mids[s][10]
                flows["pq"[s]] = comm.carry(mids[s][9], token, bits, True)
                next(flows["pq"[s]])
            elif kind == "I":
                inners[s] = inner(s, after)
                token = inners[s][1]
            elif kind == "L":
                lasts[s] = last(s, next(flows["pq"[s]]), after)
                token = lasts[s][0]
            elif kind == "G":
                token = weights(name, True, after)
                flows[name] = comm.sums(
                    token, functools.partial(kept.get, name), bits, shapes[name], orders[name]
                )
                next(flows[name])
            elif kind == "K":
                token = kept[name] = weights(name, False, after)
            else:
                token = flows[name].send(after)
        return token

    end = (play(ORDER, None),)
    (up_grad,), (down_grad,) = flows["u"].send(end), flows["d"].send(end)
    qkv_grad, outw_grad, small = flows["k"].send(end)
    small = small[:, :16].T
    grad = jnp.stack([lasts[s][0] for s in range(seqs)])
    out = [mids[s][0] for s in range(seqs)]
    return (
        jnp.stack(out),
        grad,
        small[0],
        small[1],
        qkv_grad,
        outw_grad,
        small[8],
        small[9],
        up_grad,
        down_grad,
    )


def solution(mesh):
    comm = AnySlice()
    if dict(mesh.shape) == {"seq": 8, "batch": 4}:
        comm = Slice32()
        mesh = Mesh(mesh.devices.reshape(4, 2, 2, 2), comm.axes)
    return jax.shard_map(
        functools.partial(body, comm),
        mesh=mesh,
        in_specs=(comm.rows, comm.lens) + (P(),) * 9 + (comm.rows,),
        out_specs=(comm.rows, comm.rows) + (P(),) * 8,
        check_vma=False,
    )
```

```python
import functools

import jax
import jax.numpy as jnp
from jax import lax
from jax.experimental import pallas as pl
from jax.experimental.pallas import tpu as pltpu
from jax.sharding import Mesh, PartitionSpec as P

EPS = 1e-05
SHRINK = 64 ** (-0.25)
SCALE = 256 ** (-0.5)


class Slice32:
    axes = ("z", "y", "x", "c")
    rows = P(("x", "c"), ("z", "y"), None)
    lens = P(("x", "c"))
    swaps = {
        "c": ("c", [(0, 1), (1, 0)]),
        "x": ("x", [(0, 1), (1, 0)]),
        "y": ("y", [(0, 1), (1, 0)]),
        "z1": ("z", [(0, 1), (1, 0), (2, 3), (3, 2)]),
        "z2": ("z", [(0, 2), (2, 0), (1, 3), (3, 1)]),
    }

    def position(self):
        return lax.axis_index("z") * 2 + lax.axis_index("y")

    def bits(self):
        z = lax.axis_index("z")
        at = [lax.axis_index(a) for a in "cxy"] + [z % 2, z // 2]
        return jnp.stack(at).astype(jnp.int32)

    def swap(self, part, axis):
        name, pairs = self.swaps[axis]
        return lax.ppermute(part, name, pairs)

    def whole_sum(self, part):
        return lax.psum(part, self.axes)

    def carry(self, keep, give, bits, reverse):
        after = yield
        got = self.swap(give, "y")
        after = yield give
        total = simple(add_kernel, after, keep, got)
        hops = [(3, 2), (2, 1), (1, 0)] if reverse else [(0, 1), (1, 2), (2, 3)]
        out, arrived = total, []
        for hop in hops:
            arrived.append(lax.ppermute(out, "z", [hop]))
            after = yield out
            if len(arrived) < 3:
                out = simple(add_kernel, after, total, arrived[-1])
        mine, send = call(
            functools.partial(close_kernel, reverse), 1, [SMEM] + [full(keep.shape)] * 5,
            [(full(keep.shape), keep.shape, F32)] * 2, flops=keep.size, nbytes=28 * keep.size,
        )(bits, keep, got, *arrived, after=after)
        other = self.swap(send, "y")
        yield send
        yield mine, other

    def sums(self, give, keep, bits, shapes):
        after = yield
        got = self.swap(give, "c")
        after = yield give
        rows, wide = give.shape

        def fold(ways, parts, after, count):
            size = parts[0].shape[0] // count
            shape = (size, wide)
            outs = [(full(shape), shape, F32)] * (4 if count == 4 else 2 * len(ways))
            return call(
                functools.partial(fold_kernel, ways, count), 1,
                [SMEM] + [full(p.shape) for p in parts], outs,
                flops=parts[0].size, nbytes=12 * parts[0].size,
            )(bits, *parts, after=after)

        give_a, give_b, keep_a, keep_b = fold((1, 2), (keep(), got), after, 4)
        got_a, got_b = self.swap(give_a, "x"), self.swap(give_b, "y")
        after = yield give_a
        give_a, give_b, keep_a, keep_b = fold((2, 1), (keep_a, got_a, keep_b, got_b), after, 2)
        got_a, got_b = self.swap(give_a, "y"), self.swap(give_b, "x")
        after = yield give_a
        both = rows // 4
        part = (full((both // 2, wide)), (both // 2, wide), F32)
        ins = [SMEM] + [full((both // 2, wide))] * 4
        give, keep = call(merge_kernel, 1, ins, [part] * 2, nbytes=24 * both * wide)(
            bits, keep_a, got_a, keep_b, got_b, after=after
        )
        got = self.swap(give, "z1")
        after = yield give
        give, keep = fold((4,), (keep, got), after, 2)
        got = self.swap(give, "z2")
        after = yield give
        one = simple(add_kernel, after, keep, got)
        got = self.swap(one, "z2")
        after = yield one
        (two,) = self.join((4,), bits, (one, got), after)
        got = self.swap(two, "z1")
        after = yield two
        (four,) = self.join((3,), bits, (two, got), after)
        a, b = four[: both // 2], four[both // 2 :]
        got_a, got_b = self.swap(a, "y"), self.swap(b, "x")
        after = yield a
        a, b = self.join((2, 1), bits, (a, got_a, b, got_b), after)
        got_a, got_b = self.swap(a, "x"), self.swap(b, "y")
        after = yield a
        part = call(
            functools.partial(join_kernel, (1, 2), True), 1,
            [SMEM] + [full(a.shape)] * 4, [(full((rows, wide)), (rows, wide), F32)],
            nbytes=8 * rows * wide,
        )(bits, a, got_a, b, got_b, after=after)[0]
        got = self.swap(part, "c")
        after = yield part
        yield call(
            last_join_kernel, 1, [SMEM] + [full((rows, wide))] * 2,
            [(full(s), s, F32) for s in shapes], nbytes=16 * rows * wide,
        )(bits, part, got, after=after)

    def join(self, ways, bits, parts, after):
        rows, wide = parts[0].shape
        out = (full((2 * rows, wide)), (2 * rows, wide), F32)
        return call(
            functools.partial(join_kernel, ways, False), 1,
            [SMEM] + [full(p.shape) for p in parts], [out] * len(ways),
            nbytes=16 * rows * wide,
        )(bits, *parts, after=after)


class AnySlice:
    axes = ("seq", "batch")
    rows = P("batch", "seq", None)
    lens = P("batch")

    def position(self):
        return lax.axis_index("seq")

    def bits(self):
        return jnp.zeros((5,), jnp.int32)

    def whole_sum(self, part):
        return lax.psum(part, self.axes)

    def carry(self, keep, give, bits, reverse):
        size = lax.axis_size("seq")

        def shift(part, by):
            pairs = [(i, i + by) for i in range(size - by)]
            return lax.ppermute(part, "seq", [(b, a) for a, b in pairs] if reverse else pairs)

        for _ in range(6):
            yield keep
        out, by = shift(jnp.stack([keep, give]), 1), 1
        while by < size:
            out, by = out + shift(out, by), by * 2
        yield out[0], out[1]

    def sums(self, give, keep, bits, shapes):
        for _ in range(11):
            yield give
        part = lax.psum(jnp.concatenate([keep(), give], axis=0), self.axes)
        outs, at = [], 0
        for shape in shapes:
            outs.append(part[:, at : at + shape[1]])
            at += shape[1]
        yield outs


LANES = 128
BF = jnp.bfloat16
F32 = jnp.float32


def mm(a, b):
    return jnp.dot(a, b, preferred_element_type=F32)


def mm_t(a, b):
    return lax.dot_general(a, b, (((1,), (1,)), ((), ())), preferred_element_type=F32)


def lanes_of(width):
    return lax.broadcasted_iota(jnp.int32, (1, width), 1)


def head_of(width):
    return (lanes_of(width) % LANES) // 64


def live_of(meta, s, rows):
    at = lax.broadcasted_iota(jnp.int32, (rows, 1), 0) + meta[0]
    return (at < meta[1 + s]).astype(F32)


def norm(values, gain, bias):
    mu = jnp.mean(values, axis=-1, keepdims=True)
    centred = values - mu
    inv = lax.rsqrt(jnp.mean(centred * centred, axis=-1, keepdims=True) + EPS)
    xhat = centred * inv
    return xhat * gain + bias, xhat, inv


def norm_grad(e, xhat, inv, gain):
    eg = e * gain
    return inv * (
        eg
        - jnp.mean(eg, axis=-1, keepdims=True)
        - xhat * jnp.mean(eg * xhat, axis=-1, keepdims=True)
    )


def blocks_of(f):
    shape = (f.shape[0], LANES)
    own = lax.broadcasted_iota(jnp.int32, shape, 0) // 256 == head_of(LANES)
    diagonal = jnp.where(own, jnp.concatenate([f, f], axis=1), jnp.zeros(shape, BF))
    half = jnp.where(own, -0.5, 0.0).astype(BF)
    return jnp.concatenate([diagonal, half], axis=1)


def two_rows(first, second):
    row = lax.broadcasted_iota(jnp.int32, (8, first.shape[1]), 0)
    return jnp.where(row == 0, first, jnp.where(row == 1, second, 0.0))


def phi(u, f):
    fw = blocks_of(f)
    sq = jnp.square(u.astype(F32))
    hi = sq.astype(BF)
    lo = (sq - hi.astype(F32)).astype(BF)
    lhs = jnp.concatenate([u, hi, lo], axis=1)
    return jnp.exp(mm_t(lhs, jnp.concatenate([fw, fw[:, LANES:]], axis=1))) * SCALE


def map_kernel(s, meta, bits, x, gain, bias, wk, wv, fx, h1, ks, vv, pk, keep, give):
    p = pl.program_id(0)
    rows = x.shape[1]

    @pl.when(p == 0)
    def _():
        h1[...] = norm(x[0].astype(F32), gain[...], bias[...])[0].astype(BF)

    kv = mm(h1[...], jnp.concatenate([wk[...], wv[...]], axis=1))
    k = (SHRINK * kv[:, :LANES]).astype(BF)
    v = kv[:, LANES:].astype(BF)
    ks[...], vv[...] = k, v
    phk = (phi(k, fx[0]) * live_of(meta, s, rows)).astype(BF)
    pk[...] = phk
    ds = mm(jnp.concatenate([v.T, jnp.ones((16, rows), BF)], axis=0), phk)
    for near, xs in ((True, keep), (False, give)):

        @pl.when((p // 2 == bits[2]) == near)
        def _(xs=xs):
            put_state(xs, 2 * (p % 2), ds[:64, :256], ds[128:129, :256])
            put_state(xs, 2 * (p % 2) + 1, ds[64:128, 256:], ds[128:129, 256:])


def query_kernel(h1, wq, fx, qs, pq):
    q = (SHRINK * mm(h1[...], wq[...])).astype(BF)
    qs[...] = q
    pq[...] = phi(q, fx[0]).astype(BF)


def put_state(xs, at, state, total):
    xs[at, :64] = state
    xs[at, 64:] = jnp.broadcast_to(total, (8, 256))


def add_kernel(*refs):
    *parts, out = refs
    total = parts[0][...]
    for part in parts[1:]:
        total = total + part[...]
    out[...] = total


def close_kernel(reverse, bits, keep, got, first, second, third, mine, send):
    before = (first[...] + second[...]) + third[...]
    early = (bits[2] == (1 if reverse else 0)).astype(F32)
    mine[...] = before + (1.0 - early) * got[...]
    send[...] = before + early * keep[...]


def fold_kernel(ways, count, bits, *refs):
    if count == 4:
        part, got, *outs = refs
        size = part.shape[0] // 4
        for n, way in enumerate(ways):
            bit = bits[way]
            for out, side in ((outs[n], 1 - bit), (outs[2 + n], bit)):
                at = pl.ds(pl.multiple_of((2 * n + side) * size, 8), size)
                out[...] = part[at, :] + got[at, :]
        return
    pairs = len(ways)
    for n, way in enumerate(ways):
        part, got = refs[2 * n], refs[2 * n + 1]
        outs = refs[2 * pairs :]
        size, bit = part.shape[0] // 2, bits[way]
        for out, side in ((outs[n], 1 - bit), (outs[pairs + n], bit)):
            at = pl.ds(pl.multiple_of(side * size, 8), size)
            out[...] = part[at, :] + got[at, :]


def merge_kernel(bits, part_a, got_a, part_b, got_b, give, keep):
    first = bits[3] == 0
    a, b = part_a[...] + got_a[...], part_b[...] + got_b[...]
    keep[...] = jnp.where(first, a, b)
    give[...] = jnp.where(first, b, a)


def join_kernel(ways, one, bits, *refs):
    outs = refs[2 * len(ways) :]
    for n, way in enumerate(ways):
        part, got = refs[2 * n], refs[2 * n + 1]
        size, bit = part.shape[0], bits[way]
        out, base = (outs[0], 2 * n * size) if one else (outs[n], 0)
        out[pl.ds(pl.multiple_of(base + bit * size, 8), size), :] = part[...]
        out[pl.ds(pl.multiple_of(base + (1 - bit) * size, 8), size), :] = got[...]


def last_join_kernel(bits, part, got, *outs):
    size, at = part.shape[0], 0
    for out in outs:
        wide = out.shape[1]
        for ref, side in ((part, bits[0]), (got, 1 - bits[0])):
            out[pl.ds(pl.multiple_of(side * size, 8), size), :] = ref[:, at : at + wide]
        at += wide


def below(rows, cols, shift):
    i = lax.broadcasted_iota(jnp.int32, (rows, cols), 0) + shift
    return lax.broadcasted_iota(jnp.int32, (rows, cols), 1) <= i


def local_kernel(pq, pk, vv, nd):
    rows = pq.shape[0]
    half = rows // 2
    v = vv[...]
    values = jnp.concatenate([v, jnp.ones_like(v)], axis=1)
    head = head_of(2 * LANES)
    top, low = None, None
    for h in range(2):
        cols = slice(256 * h, 256 * h + 256)
        mine = jnp.where(head == h, values, jnp.zeros_like(values))
        a0 = mm_t(pq[:half, cols], pk[:half, cols])
        a0 = jnp.where(below(half, half, 0), a0, 0.0).astype(BF)
        a1 = mm_t(pq[half:, cols], pk[:, cols])
        a1 = jnp.where(below(half, rows, half), a1, 0.0).astype(BF)
        t, l = mm(a0, mine[:half]), mm(a1, mine)
        top, low = (t, l) if h == 0 else (top + t, low + l)
    nd[:half] = top
    nd[half:] = low


def gelu_parts(u):
    c0, c1 = 0.7978845608028654, 0.044715
    sq = u * u
    t = jnp.tanh(u * (c0 + (c0 * c1) * sq))
    half_up = 0.5 + 0.5 * t
    slope = half_up + (0.5 * u) * (1.0 - t * t) * (c0 + (3.0 * c0 * c1) * sq)
    return u * half_up, slope


def state_of(mine, other, near, first):
    two = [jnp.where(near, mine[first + h], other[first + h]) for h in range(2)]
    st = jnp.concatenate([t[:64] for t in two], axis=1)
    return st, jnp.concatenate([t[64:65] for t in two], axis=1)


def middle_kernel(
    s, meta, bits, x, dy, pq, nd, mine, other, gain, bias, wo, wup, wdown, *refs
):
    middle_body(s, meta, bits, x, dy, pq, nd, mine, other, gain, bias, wo, wup, wdown, *refs[-18:])


def middle_body(
    s, meta, bits, x, dy, pq, nd, mine, other, gain, bias, wo, wup, wdown,
    out, dx1, dx, a_low, db, h2, df, gl, du, gs_keep, gs_give, ng,
    x1, xhat, inv, f, dh2, den,
):
    c = pl.program_id(0)
    rows = x.shape[1]
    live = live_of(meta, s, rows)
    col = lanes_of(512)

    @pl.when(c == 0)
    def _():
        for p in range(4):
            st, z = state_of(mine, other, bits[2] == p // 2, 2 * (p % 2))
            zero = jnp.zeros_like(st)
            zb = jnp.broadcast_to(z, st.shape)
            rhs = jnp.concatenate(
                [
                    jnp.where(col < 256, st, zero),
                    jnp.where(col >= 256, st, zero),
                    jnp.where(col < 256, zb, zero),
                    jnp.where(col >= 256, zb, zero),
                ],
                axis=0,
            ).astype(BF)
            both = mm_t(pq[:, 512 * p : 512 * p + 512], rhs) + nd[:, 256 * p : 256 * p + 256]
            lanes = slice(LANES * p, LANES * p + LANES)
            den[:, lanes] = both[:, LANES:]
            f[:, lanes] = both[:, :LANES] / both[:, LANES:]
        a_low[...] = f[...].astype(BF)
        mid = x[0].astype(F32) + live * mm(a_low[...], wo[...])
        x1[...] = mid
        h, xh, iv = norm(mid, gain[...], bias[...])
        h2[...] = h.astype(BF)
        xhat[...] = xh
        inv[...] = jnp.broadcast_to(iv, inv.shape)
        df[...] = (live * dy[0].astype(F32)).astype(BF)

    g, slope = gelu_parts(mm(h2[...], wup[...]))
    g = g.astype(BF)
    gl[...] = g
    d = (slope * mm_t(df[...], wdown[...])).astype(BF)
    du[...] = d
    part = mm(g, wdown[...])
    back = mm_t(d, wup[...])

    @pl.when(c == 0)
    def _():
        x1[...] += live * part
        dh2[...] = back

    @pl.when(c > 0)
    def _():
        x1[...] += live * part
        dh2[...] += back

    @pl.when(c == pl.num_programs(0) - 1)
    def _():
        out[0] = x1[...].astype(BF)
        e = dh2[...]
        xh = xhat[...]
        ng[...] = two_rows(
            jnp.sum(e * xh, axis=0, keepdims=True), jnp.sum(e, axis=0, keepdims=True)
        )
        g1 = dy[0].astype(F32) + norm_grad(e, xh, inv[:, :1], gain[...])
        dx1[...] = g1
        db[...] = (live * g1).astype(BF)
        da = mm_t(db[...], wo[...])
        block = jnp.where(
            lax.broadcasted_iota(jnp.int32, (2 * LANES, LANES), 0) % LANES // 64
            == lax.broadcasted_iota(jnp.int32, (2 * LANES, LANES), 1) // 64,
            -1.0,
            0.0,
        ).astype(BF)
        slot = lanes_of(LANES) % 64
        for p in range(4):
            lanes = slice(LANES * p, LANES * p + LANES)
            dn = da[:, lanes] / den[:, lanes]
            w = dn * f[:, lanes]
            hi = w.astype(BF)
            lo = (w - hi.astype(F32)).astype(BF)
            dd = mm(jnp.concatenate([hi, lo], axis=1), block)
            hi = dd.astype(BF).astype(F32)
            lo = dd - hi
            two = jnp.where((slot == 0) | (slot == 2), hi, jnp.where(slot == 1, lo, 0.0))
            both = jnp.concatenate([dn.astype(BF), two.astype(BF)], axis=1)
            dx[:, 256 * p : 256 * p + 256] = both
            g = mm(both.T, pq[:, 512 * p : 512 * p + 512])
            for near, gs in ((True, gs_keep), (False, gs_give)):

                @pl.when((bits[2] == p // 2) == near)
                def _(gs=gs, g=g):
                    for h in range(2):
                        side, at = slice(256 * h, 256 * h + 256), 128 + 64 * h
                        z = g[at : at + 1, side] + g[at + 1 : at + 2, side]
                        put_state(gs, 2 * (p % 2) + h, g[64 * h : 64 * h + 64, side], z)


def inner_kernel(part, bits, qs, ks, vv, pq, pk, dx, mine, other, fx, *outs):
    p = pl.program_id(0) + 2 * part
    dq, dkl, dvl = outs[-3:]
    rows = pq.shape[0]
    half = rows // 2
    col = lanes_of(512)
    slot = lanes_of(LANES) % 64
    head = head_of(2 * LANES)
    ones = jnp.broadcast_to(jnp.where(slot < 2, 1.0, 0.0), (rows, LANES)).astype(BF)
    v1 = jnp.concatenate([vv[...], ones], axis=1)
    st, z = state_of(mine, other, bits[2] == p // 2, 0)
    zh = z.astype(BF).astype(F32)
    zl = z - zh
    zero = jnp.zeros_like(st)
    row = lax.broadcasted_iota(jnp.int32, (64, 512), 0)
    zr = jnp.where(row < 2, zh, jnp.where(row == 2, zl, 0.0))
    rhs = jnp.concatenate(
        [
            jnp.where(col < 256, st, zero),
            jnp.where(col >= 256, st, zero),
            jnp.where(col < 256, zr, zero),
            jnp.where(col >= 256, zr, zero),
        ],
        axis=0,
    ).astype(BF)
    d = dx[...]
    far = mm(d, rhs)
    eqs, eks = [], []
    top, low = None, None
    for h in range(2):
        cols = slice(256 * h, 256 * h + 256)
        own = jnp.where(head == h, d, jnp.zeros_like(d))
        q, k = pq[:, cols], pk[:, cols]
        a0 = jnp.where(below(half, half, 0), mm_t(own[:half], v1[:half]), 0.0).astype(BF)
        a1 = jnp.where(below(half, rows, half), mm_t(own[half:], v1), 0.0).astype(BF)
        dpq = jnp.concatenate([mm(a0, k[:half]), mm(a1, k)], axis=0) + far[:, cols]
        eqs.append((dpq * q.astype(F32)).astype(BF))
        i0 = lax.broadcasted_iota(jnp.int32, (half, rows), 1)
        up0 = i0 >= lax.broadcasted_iota(jnp.int32, (half, rows), 0)
        up1 = up0[:, :half]
        b0 = jnp.where(up0, mm_t(v1[:half], own), 0.0).astype(BF)
        b1 = jnp.where(up1, mm_t(v1[half:], own[half:]), 0.0).astype(BF)
        dpk = jnp.concatenate([mm(b0, q), mm(b1, q[half:])], axis=0)
        eks.append((dpk * k.astype(F32)).astype(BF))
        c0 = jnp.where(up0, mm_t(k[:half], q), 0.0).astype(BF)
        c1 = jnp.where(up1, mm_t(k[half:], q[half:]), 0.0).astype(BF)
        t, l = mm(c0, own[:, :LANES]), mm(c1, own[half:, :LANES])
        top, low = (t, l) if h == 0 else (top + t, low + l)
    fw = blocks_of(fx[0])
    r = mm(jnp.concatenate(eqs, axis=1), fw)
    dq[...] = (SHRINK * (r[:, :LANES] + 2.0 * qs[...].astype(F32) * r[:, LANES:])).astype(BF)
    r = mm(jnp.concatenate(eks, axis=1), fw)
    dkl[...] = r[:, :LANES] + 2.0 * ks[...].astype(F32) * r[:, LANES:]
    dvl[:half] = top
    dvl[half:] = low


def last_kernel(
    s, bits, x, dx1, gain, ks, vv, pk, mine, other, fx, dq, dkl, dvl, wq, wk, wv,
    *refs,
):
    grad, dk, dv, ng, dh1 = refs[-5:]
    p = pl.program_id(0)
    rows = pk.shape[0]
    col = lanes_of(512)
    slot = lanes_of(LANES) % 64
    ones = jnp.broadcast_to(jnp.where(slot < 2, 1.0, 0.0), (rows, LANES)).astype(BF)
    v1 = jnp.concatenate([vv[...], ones], axis=1)
    st, z = state_of(mine, other, bits[2] == p // 2, 0)
    zh = z.astype(BF).astype(F32)
    zl = z - zh
    zero = jnp.zeros_like(st)
    row = lax.broadcasted_iota(jnp.int32, (64, 512), 0)
    zr = jnp.where(row == 0, zh, jnp.where(row == 1, zl, 0.0))
    rhs = jnp.concatenate(
        [
            jnp.where(col < 256, st, zero),
            jnp.where(col >= 256, st, zero),
            jnp.where(col < 256, zr, zero),
            jnp.where(col >= 256, zr, zero),
        ],
        axis=0,
    ).astype(BF)
    dpk = mm(v1, rhs)
    ek = (dpk * pk[...].astype(F32)).astype(BF)
    r = mm(ek, blocks_of(fx[0]))
    k = SHRINK * (dkl[...] + r[:, :LANES] + 2.0 * ks[...].astype(F32) * r[:, LANES:])
    k = k.astype(BF)
    v = (dvl[...] + mm_t(pk[...], rhs[:LANES])).astype(BF)
    dk[...], dv[...] = k, v
    w = jnp.concatenate([wq[...], wk[...], wv[...]], axis=1)
    part = mm_t(jnp.concatenate([dq[...], k, v], axis=1), w)

    @pl.when(p == 0)
    def _():
        dh1[...] = part

    @pl.when(p > 0)
    def _():
        dh1[...] += part

    @pl.when(p == pl.num_programs(0) - 1)
    def _():
        _, xh, inv = norm(x[0].astype(F32), gain[...], gain[...])
        e = dh1[...]
        ng[...] = two_rows(
            jnp.sum(e * xh, axis=0, keepdims=True), jnp.sum(e, axis=0, keepdims=True)
        )
        grad[0] = dx1[...] + norm_grad(e, xh, inv, gain[...])


def block_kernel(g0, g1, f0, f1, h0, h1, u0, u1, down, up):
    p = pl.program_id(0)
    n = pl.num_programs(0) // 2

    @pl.when(p < n)
    def _():
        down[...] = mm(g0[...].T, f0[...]) + mm(g1[...].T, f1[...])

    @pl.when(p >= n)
    def _():
        up[...] = mm(h0[...].T, u0[...]) + mm(h1[...].T, u1[...])


def late_kernel(c, a0, a1, b0, b1, b2, b3, b4, b5, n0, n1, n2, n3, o0, o1, d0, d1, out):
    a = jnp.concatenate([a0[...].T, a1[...].T], axis=1)
    for n, (first, second) in enumerate(((b0, b1), (b2, b3), (b4, b5))):
        both = jnp.concatenate([first[...], second[...]], axis=0)
        out[:, 512 * n : 512 * n + 512] = mm(a, both)
    out[:, 1536:2048] = mm(o0[...].T, d0[...]) + mm(o1[...].T, d1[...])
    sums = [n0[...] + n1[...], n2[...] + n3[...]]
    out[:, 2048:] = jnp.concatenate(sums + [jnp.zeros((112, out.shape[0]), F32)], axis=0).T


def params(limit):
    return pltpu.CompilerParams(vmem_limit_bytes=limit * 2**20)


def full(shape):
    return pl.BlockSpec(shape, lambda p, n=len(shape): (0,) * n)


def of_seq(s, shape):
    return pl.BlockSpec((1,) + shape, lambda p: (s, 0, 0))


def cols(rows, width, first=0):
    return pl.BlockSpec((rows, width), lambda p: (0, first + p))


SMEM = pl.BlockSpec(memory_space=pltpu.SMEM)
HEADS = pl.BlockSpec((2, 72, 256), lambda p: (p % 2, 0, 0))
PAIR = pl.BlockSpec((1, 512, 64), lambda p: (p, 0, 0))


def arr(shape, dtype):
    return jax.ShapeDtypeStruct(shape, dtype)


ANY = pl.BlockSpec(memory_space=pl.ANY)


def call(
    kernel, grid, ins, outs, scratch=(), flops=0, nbytes=0, scalars=0, aliases={},
    grant=16,
):
    def run(*args, after=()):
        count, waits = len(ins) + scalars, len(after)

        def waiting(*refs):
            kernel(*refs[:count], *refs[count + waits :])

        return pl.pallas_call(
            waiting,
            grid_spec=pltpu.PrefetchScalarGridSpec(
                num_scalar_prefetch=scalars,
                grid=(grid,),
                in_specs=list(ins) + [ANY] * waits,
                out_specs=[o[0] for o in outs],
                scratch_shapes=list(scratch),
            ),
            out_shape=[arr(*o[1:]) for o in outs],
            compiler_params=params(grant),
            input_output_aliases=aliases,
            cost_estimate=pl.CostEstimate(flops=flops, bytes_accessed=nbytes, transcendentals=0),
        )(*args, *after)

    return run


def simple(kernel, after, *parts):
    spec = full(parts[0].shape)
    return call(
        kernel, 1, [spec] * len(parts), [(spec, parts[0].shape, F32)],
        flops=parts[0].size, nbytes=12 * parts[0].size,
    )(*parts, after=after)[0]


def half_of(give):
    return (lambda c: 1 - c[0]) if give else (lambda c: c[0])


def whole(shape):
    return pl.BlockSpec(shape, lambda p, c: (0,) * len(shape))


def block_weights(gl, df, h2, du, after=()):
    rows, width = df[0].shape
    wide = gl[0].shape[1]
    n = wide // 512
    one = full((rows, width))
    first = lambda p: jnp.minimum(p, n - 1)
    second = lambda p: jnp.maximum(p - n, 0)
    sg = pl.BlockSpec((rows, 512), lambda p: (0, first(p)))
    su = pl.BlockSpec((rows, 512), lambda p: (0, second(p)))
    return call(
        block_kernel, 2 * n, [sg, sg, one, one, one, one, su, su],
        [(pl.BlockSpec((512, width), lambda p: (first(p), 0)), (wide, width), F32),
         (pl.BlockSpec((width, 512), lambda p: (0, second(p))), (width, wide), F32)],
        flops=8 * rows * width * wide, nbytes=8 * width * wide + 8 * rows * wide,
    )(*gl, *df, *h2, *du, after=after)


def late_weights(give, bits, h1, dq, dk, dv, ng1, ng2, a, db, after=()):
    rows, n = dk[0].shape
    m = n // 2
    at = half_of(give)
    sa, sb = pl.BlockSpec((rows, m), lambda p, c: (0, at(c))), whole((rows, n))
    sn = pl.BlockSpec((8, m), lambda p, c: (0, at(c)))
    wide = 4 * n + LANES
    return call(
        late_kernel, 1, [sa] * 2 + [sb] * 6 + [sn] * 4 + [sa] * 2 + [sb] * 2,
        [(whole((m, wide)), (m, wide), F32)],
        flops=16 * rows * m * n, nbytes=16 * m * n + 16 * rows * n, scalars=1,
    )(bits, *h1, *dq, *dk, *dv, *ng1, *ng2, *a, *db, after=after)[0]


FRONT = (
    "M0", "f", "M1", "f", "g", "Q0", "f", "g", "Q1", "f", "g", "A0", "f", "g", "A1", "N0", "g",
    "p", "N1", "p", "q",
)
BACK = (
    "p", "q", "I0a", "p", "q", "I0b", "I1a", "p", "q", "I1b", "L0", "q", "L1", "Gk", "k", "Kk",
    "k", "k", "k", "k", "k", "k", "k", "k", "k", "Fk",
)


def body(
    comm,
    inputs,
    lengths,
    norm1_gain,
    norm1_bias,
    qkv_weight,
    features,
    out_weight,
    norm2_gain,
    norm2_bias,
    up_weight,
    down_weight,
    cotangent,
):
    seqs, rows, width = inputs.shape
    wide = up_weight.shape[1]
    first_row = (comm.position() * rows).astype(jnp.int32)
    meta = jnp.concatenate([first_row[None], lengths])
    fx = features.reshape(4, 512, 64)
    bits = comm.bits()
    g1, n1, g2, n2 = (v[None] for v in (norm1_gain, norm1_bias, norm2_gain, norm2_bias))
    vec = full((1, width))
    act = cols(rows, LANES)
    big = cols(rows, 512)
    heads = (4, 72, 256)
    states = [(full(heads), heads, F32)] * 2

    def maps_of(s, after):
        return call(
            functools.partial(map_kernel, s), 4,
            [SMEM, SMEM, of_seq(s, (rows, width)), vec, vec]
            + [cols(width, LANES, 4 * n) for n in (1, 2)] + [PAIR],
            [(full((rows, width)), (rows, width), BF)]
            + [(act, (rows, width), BF)] * 2
            + [(big, (rows, 2048), BF)] + states,
            flops=rows * 3_000_000, nbytes=8 * 2**20,
        )(meta, bits, inputs, g1, n1, qkv_weight, qkv_weight, fx, after=after)

    def queries_of(h1, after):
        return call(
            query_kernel, 4, [full((rows, width)), cols(width, LANES), PAIR],
            [(act, (rows, width), BF), (big, (rows, 2048), BF)],
            flops=rows * 1_800_000, nbytes=4 * 2**20,
        )(h1, qkv_weight, fx, after=after)

    def locals_of(s, after):
        _, _, _, vv, pq, pk = maps[s]
        return call(
            local_kernel, 4, [big, big, act],
            [(cols(rows, 256), (rows, 1024), F32)],
            flops=rows * 6_000_000, nbytes=7 * 2**20,
        )(pq, pk, vv, after=after)[0]

    def middle_of(s, prefix, after):
        pq = maps[s][4]
        return call(
                functools.partial(middle_kernel, s), wide // 512,
                [SMEM, SMEM, of_seq(s, (rows, width)), of_seq(s, (rows, width)), full((rows, 2048)),
                 full((rows, 1024)), full(heads), full(heads), vec, vec, full((width, width)),
                 cols(width, 512), pl.BlockSpec((512, width), lambda p: (p, 0))] + [ANY] * s,
                [(of_seq(s, (rows, width)), inputs.shape, BF),
                 (full((rows, width)), (rows, width), F32),
                 (full((rows, 1024)), (rows, 1024), BF),
                 (full((rows, width)), (rows, width), BF),
                 (full((rows, width)), (rows, width), BF),
                 (full((rows, width)), (rows, width), BF),
                 (full((rows, width)), (rows, width), BF),
                 (cols(rows, 512), (rows, wide), BF),
                 (cols(rows, 512), (rows, wide), BF),
                 *states,
                 (full((8, width)), (8, width), F32)],
                scratch=[pltpu.VMEM((rows, width), F32), pltpu.VMEM((rows, width), F32),
                         pltpu.VMEM((rows, LANES), F32)]
                + [pltpu.VMEM((rows, width), F32)] * 3,
                flops=rows * 11_000_000, nbytes=24 * 2**20, grant=24, aliases={13: 0} if s else {},
            )(meta, bits, inputs, cotangent, pq, locals_[s], *prefix, g2, n2, out_weight,
              up_weight, down_weight, *([mids[0][0]] if s else []), after=after)

    def inner(s, part, after):
        _, qs, ks, vv, pq, pk = maps[s]
        here = lambda wide: pl.BlockSpec((rows, wide), lambda p: (0, p + 2 * part))
        side = pl.BlockSpec((2, 72, 256), lambda p: (p % 2, 0, 0))
        fxs = pl.BlockSpec((1, 512, 64), lambda p: (p + 2 * part, 0, 0))
        act, big = here(LANES), here(512)
        earlier = tuple(inners[s]) if part else ()
        return call(
            functools.partial(inner_kernel, part), 2,
            [SMEM, act, act, act, big, big, here(256), side, side, fxs] + [ANY] * len(earlier),
            [(act, (rows, width), BF), (act, (rows, width), F32), (act, (rows, width), F32)],
            flops=rows * 10_000_000, nbytes=6 * 2**20,
            aliases={10 + n: n for n in range(len(earlier))},
        )(bits, qs, ks, vv, pq, pk, mids[s][2], *state[s], fx, *earlier, after=after)

    def last(s, later, after):
        _, qs, ks, vv, pq, pk = maps[s]
        return call(
            functools.partial(last_kernel, s), 4,
            [SMEM, of_seq(s, (rows, width)), full((rows, width)), vec, act, act, big, HEADS, HEADS,
             PAIR,
             act, act, act] + [cols(width, LANES, 4 * n) for n in range(3)] + [ANY] * s,
            [(of_seq(s, (rows, width)), inputs.shape, F32), (act, (rows, width), BF),
             (act, (rows, width), BF), (full((8, width)), (8, width), F32)],
            scratch=[pltpu.VMEM((rows, width), F32)],
            flops=rows * 6_000_000, nbytes=11 * 2**20, aliases={16: 0} if s else {},
        )(bits, inputs, mids[s][1], g1, ks, vv, pk, *later, fx, *inners[s],
          qkv_weight, qkv_weight, qkv_weight, *([lasts[0][0]] if s else []), after=after)

    maps, locals_, mids, state, inners, lasts, kept, flows = {}, {}, {}, {}, {}, {}, {}, {}
    ends = {}

    def of_mids(*index):
        return [[mids[s][n] for s in range(seqs)] for n in index]

    def weights(name, give, after):
        h1 = [maps[s][0] for s in range(seqs)]
        dq = [inners[s][0] for s in range(seqs)]
        dk, dv, ng1 = ([lasts[s][n] for s in range(seqs)] for n in (1, 2, 3))
        return late_weights(give, bits, h1, dq, dk, dv, ng1, *of_mids(11, 3, 4), after=after)

    shapes = ((width, 3 * width), (width, width), (width, LANES))

    def play(items, token):
        for item in items:
            after = () if token is None else (token,)
            kind, name = item[0], item[-1]
            s = int(item[1]) if item[1:2] in ("0", "1") else None
            if kind == "M":
                h1, ks, vv, pk, keep, token = maps_of(s, after)
                maps[s] = [h1, None, ks, vv, None, pk]
                flows["fg"[s]] = comm.carry(keep, token, bits, False)
                next(flows["fg"[s]])
            elif kind == "Q":
                maps[s][1], maps[s][4] = queries_of(maps[s][0], after)
                token = maps[s][1]
            elif kind == "A":
                token = locals_[s] = locals_of(s, after)
            elif kind == "N":
                state[s] = next(flows["fg"[s]])
                mids[s] = middle_of(s, state[s], after)
                token = mids[s][10]
                flows["pq"[s]] = comm.carry(mids[s][9], token, bits, True)
                next(flows["pq"[s]])
            elif kind == "I":
                inners[s] = inner(s, int(name == "b"), after)
                token = inners[s][1]
            elif kind == "L":
                lasts[s] = last(s, next(flows["pq"[s]]), after)
                token = lasts[s][0]
            elif kind == "G":
                token = weights(name, True, after)
                flows[name] = comm.sums(
                    token, functools.partial(kept.get, name), bits, shapes
                )
                next(flows[name])
            elif kind == "K":
                token = kept[name] = weights(name, False, after)
            elif kind == "F":
                ends[name] = flows[name].send(after)
                token = ends[name][0]
            else:
                token = flows[name].send(after)
        return token

    token = play(FRONT, None)
    parts = block_weights(*of_mids(7, 6, 5, 8), after=(token,))
    down_grad, up_grad = comm.whole_sum(tuple(parts))

    def rest():
        play(BACK, parts[1])
        qkv_grad, outw_grad, small = ends["k"]
        return qkv_grad, outw_grad, small[:, :16].T, lasts[seqs - 1][0]

    def nothing():
        shaped = [(width, 3 * width), (width, width), (16, width)]
        return *(jnp.zeros(s, F32) for s in shaped), cotangent.astype(F32)

    qkv_grad, outw_grad, small, grad = lax.cond(jnp.max(lengths) > 0, rest, nothing)
    out = mids[seqs - 1][0]
    return (
        out,
        grad,
        small[0],
        small[1],
        qkv_grad,
        outw_grad,
        small[8],
        small[9],
        up_grad,
        down_grad,
    )


def solution(mesh):
    comm = AnySlice()
    if dict(mesh.shape) == {"seq": 8, "batch": 4}:
        comm = Slice32()
        mesh = Mesh(mesh.devices.reshape(4, 2, 2, 2), comm.axes)
    return jax.shard_map(
        functools.partial(body, comm),
        mesh=mesh,
        in_specs=(comm.rows, comm.lens) + (P(),) * 9 + (comm.rows,),
        out_specs=(comm.rows, comm.rows) + (P(),) * 8,
        check_vma=False,
    )
```

```python
import functools

import jax
import jax.numpy as jnp
from jax import lax
from jax.experimental import pallas as pl
from jax.experimental.pallas import tpu as pltpu
from jax.sharding import Mesh, PartitionSpec as P

EPS = 1e-05
SHRINK = 64 ** (-0.25)
SCALE = 256 ** (-0.5)


class Slice32:
    axes = ("z", "y", "x", "c")
    rows = P(("x", "c"), ("z", "y"), None)
    lens = P(("x", "c"))
    swaps = {
        "c": ("c", [(0, 1), (1, 0)]),
        "x": ("x", [(0, 1), (1, 0)]),
        "y": ("y", [(0, 1), (1, 0)]),
        "z1": ("z", [(0, 1), (1, 0), (2, 3), (3, 2)]),
        "z2": ("z", [(0, 2), (2, 0), (1, 3), (3, 1)]),
    }

    def position(self):
        return lax.axis_index("z") * 2 + lax.axis_index("y")

    def bits(self):
        z = lax.axis_index("z")
        at = [lax.axis_index(a) for a in "cxy"] + [z % 2, z // 2]
        return jnp.stack(at).astype(jnp.int32)

    def swap(self, part, axis):
        name, pairs = self.swaps[axis]
        return lax.ppermute(part, name, pairs)

    def whole_sum(self, part):
        return lax.psum(part, self.axes)

    def carry(self, keep, give, bits, reverse):
        after = yield
        got = self.swap(give, "y")
        after = yield give
        total = simple(add_kernel, after, keep, got)
        hops = [(3, 2), (2, 1), (1, 0)] if reverse else [(0, 1), (1, 2), (2, 3)]
        out, arrived = total, []
        for hop in hops:
            arrived.append(lax.ppermute(out, "z", [hop]))
            after = yield out
            if len(arrived) < 3:
                out = simple(add_kernel, after, total, arrived[-1])
        mine, send = call(
            functools.partial(close_kernel, reverse), 1, [SMEM] + [full(keep.shape)] * 5,
            [(full(keep.shape), keep.shape, F32)] * 2, flops=keep.size, nbytes=28 * keep.size,
        )(bits, keep, got, *arrived, after=after)
        other = self.swap(send, "y")
        yield send
        yield mine, other

    def sums(self, give, keep, bits, shapes):
        after = yield
        got = self.swap(give, "c")
        after = yield give
        rows, wide = give.shape

        def fold(ways, parts, after, count):
            size = parts[0].shape[0] // count
            shape = (size, wide)
            outs = [(full(shape), shape, F32)] * (4 if count == 4 else 2 * len(ways))
            return call(
                functools.partial(fold_kernel, ways, count), 1,
                [SMEM] + [full(p.shape) for p in parts], outs,
                flops=parts[0].size, nbytes=12 * parts[0].size,
            )(bits, *parts, after=after)

        give_a, give_b, keep_a, keep_b = fold((1, 2), (keep(), got), after, 4)
        got_a, got_b = self.swap(give_a, "x"), self.swap(give_b, "y")
        after = yield give_a
        give_a, give_b, keep_a, keep_b = fold((2, 1), (keep_a, got_a, keep_b, got_b), after, 2)
        got_a, got_b = self.swap(give_a, "y"), self.swap(give_b, "x")
        after = yield give_a
        both = rows // 4
        part = (full((both // 2, wide)), (both // 2, wide), F32)
        ins = [SMEM] + [full((both // 2, wide))] * 4
        give, keep = call(merge_kernel, 1, ins, [part] * 2, nbytes=24 * both * wide)(
            bits, keep_a, got_a, keep_b, got_b, after=after
        )
        got = self.swap(give, "z1")
        after = yield give
        give, keep = fold((4,), (keep, got), after, 2)
        got = self.swap(give, "z2")
        after = yield give
        one = simple(add_kernel, after, keep, got)
        got = self.swap(one, "z2")
        after = yield one
        (two,) = self.join((4,), bits, (one, got), after)
        got = self.swap(two, "z1")
        after = yield two
        (four,) = self.join((3,), bits, (two, got), after)
        a, b = four[: both // 2], four[both // 2 :]
        got_a, got_b = self.swap(a, "y"), self.swap(b, "x")
        after = yield a
        a, b = self.join((2, 1), bits, (a, got_a, b, got_b), after)
        got_a, got_b = self.swap(a, "x"), self.swap(b, "y")
        after = yield a
        part = call(
            functools.partial(join_kernel, (1, 2), True), 1,
            [SMEM] + [full(a.shape)] * 4, [(full((rows, wide)), (rows, wide), F32)],
            nbytes=8 * rows * wide,
        )(bits, a, got_a, b, got_b, after=after)[0]
        got = self.swap(part, "c")
        after = yield part
        yield call(
            last_join_kernel, 1, [SMEM] + [full((rows, wide))] * 2,
            [(full(s), s, F32) for s in shapes], nbytes=16 * rows * wide,
        )(bits, part, got, after=after)

    def join(self, ways, bits, parts, after):
        rows, wide = parts[0].shape
        out = (full((2 * rows, wide)), (2 * rows, wide), F32)
        return call(
            functools.partial(join_kernel, ways, False), 1,
            [SMEM] + [full(p.shape) for p in parts], [out] * len(ways),
            nbytes=16 * rows * wide,
        )(bits, *parts, after=after)


class AnySlice:
    axes = ("seq", "batch")
    rows = P("batch", "seq", None)
    lens = P("batch")

    def position(self):
        return lax.axis_index("seq")

    def bits(self):
        return jnp.zeros((5,), jnp.int32)

    def whole_sum(self, part):
        return lax.psum(part, self.axes)

    def carry(self, keep, give, bits, reverse):
        size = lax.axis_size("seq")

        def shift(part, by):
            pairs = [(i, i + by) for i in range(size - by)]
            return lax.ppermute(part, "seq", [(b, a) for a, b in pairs] if reverse else pairs)

        for _ in range(6):
            yield keep
        out, by = shift(jnp.stack([keep, give]), 1), 1
        while by < size:
            out, by = out + shift(out, by), by * 2
        yield out[0], out[1]

    def sums(self, give, keep, bits, shapes):
        for _ in range(11):
            yield give
        part = lax.psum(jnp.concatenate([keep(), give], axis=0), self.axes)
        outs, at = [], 0
        for shape in shapes:
            outs.append(part[:, at : at + shape[1]])
            at += shape[1]
        yield outs


LANES = 128
BF = jnp.bfloat16
F32 = jnp.float32


def mm(a, b):
    return jnp.dot(a, b, preferred_element_type=F32)


def mm_t(a, b):
    return lax.dot_general(a, b, (((1,), (1,)), ((), ())), preferred_element_type=F32)


def lanes_of(width):
    return lax.broadcasted_iota(jnp.int32, (1, width), 1)


def head_of(width):
    return (lanes_of(width) % LANES) // 64


def live_of(meta, s, rows):
    at = lax.broadcasted_iota(jnp.int32, (rows, 1), 0) + meta[0]
    return (at < meta[1 + s]).astype(F32)


def norm(values, gain, bias):
    mu = jnp.mean(values, axis=-1, keepdims=True)
    centred = values - mu
    inv = lax.rsqrt(jnp.mean(centred * centred, axis=-1, keepdims=True) + EPS)
    xhat = centred * inv
    return xhat * gain + bias, xhat, inv


def norm_grad(e, xhat, inv, gain):
    eg = e * gain
    return inv * (
        eg
        - jnp.mean(eg, axis=-1, keepdims=True)
        - xhat * jnp.mean(eg * xhat, axis=-1, keepdims=True)
    )


def blocks_of(f):
    shape = (f.shape[0], LANES)
    own = lax.broadcasted_iota(jnp.int32, shape, 0) // 256 == head_of(LANES)
    diagonal = jnp.where(own, jnp.concatenate([f, f], axis=1), jnp.zeros(shape, BF))
    half = jnp.where(own, -0.5, 0.0).astype(BF)
    return jnp.concatenate([diagonal, half], axis=1)


def two_rows(first, second):
    row = lax.broadcasted_iota(jnp.int32, (8, first.shape[1]), 0)
    return jnp.where(row == 0, first, jnp.where(row == 1, second, 0.0))


def phi(u, f):
    fw = blocks_of(f)
    sq = jnp.square(u.astype(F32))
    hi = sq.astype(BF)
    lo = (sq - hi.astype(F32)).astype(BF)
    lhs = jnp.concatenate([u, hi, lo], axis=1)
    return jnp.exp(mm_t(lhs, jnp.concatenate([fw, fw[:, LANES:]], axis=1))) * SCALE


def map_kernel(s, meta, bits, x, gain, bias, wk, wv, fx, h1, ks, vv, pk, keep, give):
    p = pl.program_id(0)
    rows = x.shape[1]

    @pl.when(p == 0)
    def _():
        h1[...] = norm(x[0].astype(F32), gain[...], bias[...])[0].astype(BF)

    kv = mm(h1[...], jnp.concatenate([wk[...], wv[...]], axis=1))
    k = (SHRINK * kv[:, :LANES]).astype(BF)
    v = kv[:, LANES:].astype(BF)
    ks[...], vv[...] = k, v
    phk = (phi(k, fx[0]) * live_of(meta, s, rows)).astype(BF)
    pk[...] = phk
    ds = mm(jnp.concatenate([v.T, jnp.ones((16, rows), BF)], axis=0), phk)
    for near, xs in ((True, keep), (False, give)):

        @pl.when((p // 2 == bits[2]) == near)
        def _(xs=xs):
            put_state(xs, 2 * (p % 2), ds[:64, :256], ds[128:129, :256])
            put_state(xs, 2 * (p % 2) + 1, ds[64:128, 256:], ds[128:129, 256:])


def query_kernel(h1, wq, fx, qs, pq):
    q = (SHRINK * mm(h1[...], wq[...])).astype(BF)
    qs[...] = q
    pq[...] = phi(q, fx[0]).astype(BF)


def put_state(xs, at, state, total):
    xs[at, :64] = state
    xs[at, 64:] = jnp.broadcast_to(total, (8, 256))


def add_kernel(*refs):
    *parts, out = refs
    total = parts[0][...]
    for part in parts[1:]:
        total = total + part[...]
    out[...] = total


def close_kernel(reverse, bits, keep, got, first, second, third, mine, send):
    before = (first[...] + second[...]) + third[...]
    early = (bits[2] == (1 if reverse else 0)).astype(F32)
    mine[...] = before + (1.0 - early) * got[...]
    send[...] = before + early * keep[...]


def fold_kernel(ways, count, bits, *refs):
    if count == 4:
        part, got, *outs = refs
        size = part.shape[0] // 4
        for n, way in enumerate(ways):
            bit = bits[way]
            for out, side in ((outs[n], 1 - bit), (outs[2 + n], bit)):
                at = pl.ds(pl.multiple_of((2 * n + side) * size, 8), size)
                out[...] = part[at, :] + got[at, :]
        return
    pairs = len(ways)
    for n, way in enumerate(ways):
        part, got = refs[2 * n], refs[2 * n + 1]
        outs = refs[2 * pairs :]
        size, bit = part.shape[0] // 2, bits[way]
        for out, side in ((outs[n], 1 - bit), (outs[pairs + n], bit)):
            at = pl.ds(pl.multiple_of(side * size, 8), size)
            out[...] = part[at, :] + got[at, :]


def merge_kernel(bits, part_a, got_a, part_b, got_b, give, keep):
    first = bits[3] == 0
    a, b = part_a[...] + got_a[...], part_b[...] + got_b[...]
    keep[...] = jnp.where(first, a, b)
    give[...] = jnp.where(first, b, a)


def join_kernel(ways, one, bits, *refs):
    outs = refs[2 * len(ways) :]
    for n, way in enumerate(ways):
        part, got = refs[2 * n], refs[2 * n + 1]
        size, bit = part.shape[0], bits[way]
        out, base = (outs[0], 2 * n * size) if one else (outs[n], 0)
        out[pl.ds(pl.multiple_of(base + bit * size, 8), size), :] = part[...]
        out[pl.ds(pl.multiple_of(base + (1 - bit) * size, 8), size), :] = got[...]


def last_join_kernel(bits, part, got, *outs):
    size, at = part.shape[0], 0
    for out in outs:
        wide = out.shape[1]
        for ref, side in ((part, bits[0]), (got, 1 - bits[0])):
            out[pl.ds(pl.multiple_of(side * size, 8), size), :] = ref[:, at : at + wide]
        at += wide


def below(rows, cols, shift):
    i = lax.broadcasted_iota(jnp.int32, (rows, cols), 0) + shift
    return lax.broadcasted_iota(jnp.int32, (rows, cols), 1) <= i


def local_kernel(pq, pk, vv, nd):
    rows = pq.shape[0]
    half = rows // 2
    v = vv[...]
    values = jnp.concatenate([v, jnp.ones_like(v)], axis=1)
    head = head_of(2 * LANES)
    top, low = None, None
    for h in range(2):
        cols = slice(256 * h, 256 * h + 256)
        mine = jnp.where(head == h, values, jnp.zeros_like(values))
        a0 = mm_t(pq[:half, cols], pk[:half, cols])
        a0 = jnp.where(below(half, half, 0), a0, 0.0).astype(BF)
        a1 = mm_t(pq[half:, cols], pk[:, cols])
        a1 = jnp.where(below(half, rows, half), a1, 0.0).astype(BF)
        t, l = mm(a0, mine[:half]), mm(a1, mine)
        top, low = (t, l) if h == 0 else (top + t, low + l)
    nd[:half] = top
    nd[half:] = low


def gelu_parts(u):
    c0, c1 = 0.7978845608028654, 0.044715
    sq = u * u
    t = jnp.tanh(u * (c0 + (c0 * c1) * sq))
    half_up = 0.5 + 0.5 * t
    slope = half_up + (0.5 * u) * (1.0 - t * t) * (c0 + (3.0 * c0 * c1) * sq)
    return u * half_up, slope


def state_of(mine, other, near, first):
    two = [jnp.where(near, mine[first + h], other[first + h]) for h in range(2)]
    st = jnp.concatenate([t[:64] for t in two], axis=1)
    return st, jnp.concatenate([t[64:65] for t in two], axis=1)


def middle_kernel(
    s, meta, bits, x, dy, pq, nd, mine, other, gain, bias, wo, wup, wdown, *refs
):
    middle_body(s, meta, bits, x, dy, pq, nd, mine, other, gain, bias, wo, wup, wdown, *refs[-18:])


def middle_body(
    s, meta, bits, x, dy, pq, nd, mine, other, gain, bias, wo, wup, wdown,
    out, dx1, dx, a_low, db, h2, df, gl, du, gs_keep, gs_give, ng,
    x1, xhat, inv, f, dh2, den,
):
    c = pl.program_id(0)
    rows = x.shape[1]
    live = live_of(meta, s, rows)
    col = lanes_of(512)

    @pl.when(c == 0)
    def _():
        for p in range(4):
            st, z = state_of(mine, other, bits[2] == p // 2, 2 * (p % 2))
            zero = jnp.zeros_like(st)
            zb = jnp.broadcast_to(z, st.shape)
            rhs = jnp.concatenate(
                [
                    jnp.where(col < 256, st, zero),
                    jnp.where(col >= 256, st, zero),
                    jnp.where(col < 256, zb, zero),
                    jnp.where(col >= 256, zb, zero),
                ],
                axis=0,
            ).astype(BF)
            both = mm_t(pq[:, 512 * p : 512 * p + 512], rhs) + nd[:, 256 * p : 256 * p + 256]
            lanes = slice(LANES * p, LANES * p + LANES)
            den[:, lanes] = both[:, LANES:]
            f[:, lanes] = both[:, :LANES] / both[:, LANES:]
        a_low[...] = f[...].astype(BF)
        mid = x[0].astype(F32) + live * mm(a_low[...], wo[...])
        x1[...] = mid
        h, xh, iv = norm(mid, gain[...], bias[...])
        h2[...] = h.astype(BF)
        xhat[...] = xh
        inv[...] = jnp.broadcast_to(iv, inv.shape)
        df[...] = (live * dy[0].astype(F32)).astype(BF)

    g, slope = gelu_parts(mm(h2[...], wup[...]))
    g = g.astype(BF)
    gl[...] = g
    d = (slope * mm_t(df[...], wdown[...])).astype(BF)
    du[...] = d
    part = mm(g, wdown[...])
    back = mm_t(d, wup[...])

    @pl.when(c == 0)
    def _():
        x1[...] += live * part
        dh2[...] = back

    @pl.when(c > 0)
    def _():
        x1[...] += live * part
        dh2[...] += back

    @pl.when(c == pl.num_programs(0) - 1)
    def _():
        out[0] = x1[...].astype(BF)
        e = dh2[...]
        xh = xhat[...]
        ng[...] = two_rows(
            jnp.sum(e * xh, axis=0, keepdims=True), jnp.sum(e, axis=0, keepdims=True)
        )
        g1 = dy[0].astype(F32) + norm_grad(e, xh, inv[:, :1], gain[...])
        dx1[...] = g1
        db[...] = (live * g1).astype(BF)
        da = mm_t(db[...], wo[...])
        block = jnp.where(
            lax.broadcasted_iota(jnp.int32, (2 * LANES, LANES), 0) % LANES // 64
            == lax.broadcasted_iota(jnp.int32, (2 * LANES, LANES), 1) // 64,
            -1.0,
            0.0,
        ).astype(BF)
        slot = lanes_of(LANES) % 64
        for p in range(4):
            lanes = slice(LANES * p, LANES * p + LANES)
            dn = da[:, lanes] / den[:, lanes]
            w = dn * f[:, lanes]
            hi = w.astype(BF)
            lo = (w - hi.astype(F32)).astype(BF)
            dd = mm(jnp.concatenate([hi, lo], axis=1), block)
            hi = dd.astype(BF).astype(F32)
            lo = dd - hi
            two = jnp.where((slot == 0) | (slot == 2), hi, jnp.where(slot == 1, lo, 0.0))
            both = jnp.concatenate([dn.astype(BF), two.astype(BF)], axis=1)
            dx[:, 256 * p : 256 * p + 256] = both
            g = mm(both.T, pq[:, 512 * p : 512 * p + 512])
            for near, gs in ((True, gs_keep), (False, gs_give)):

                @pl.when((bits[2] == p // 2) == near)
                def _(gs=gs, g=g):
                    for h in range(2):
                        side, at = slice(256 * h, 256 * h + 256), 128 + 64 * h
                        z = g[at : at + 1, side] + g[at + 1 : at + 2, side]
                        put_state(gs, 2 * (p % 2) + h, g[64 * h : 64 * h + 64, side], z)


def inner_kernel(part, bits, qs, ks, vv, pq, pk, dx, mine, other, fx, *outs):
    p = pl.program_id(0) + 2 * part
    dq, dkl, dvl = outs[-3:]
    rows = pq.shape[0]
    half = rows // 2
    col = lanes_of(512)
    slot = lanes_of(LANES) % 64
    head = head_of(2 * LANES)
    ones = jnp.broadcast_to(jnp.where(slot < 2, 1.0, 0.0), (rows, LANES)).astype(BF)
    v1 = jnp.concatenate([vv[...], ones], axis=1)
    st, z = state_of(mine, other, bits[2] == p // 2, 0)
    zh = z.astype(BF).astype(F32)
    zl = z - zh
    zero = jnp.zeros_like(st)
    row = lax.broadcasted_iota(jnp.int32, (64, 512), 0)
    zr = jnp.where(row < 2, zh, jnp.where(row == 2, zl, 0.0))
    rhs = jnp.concatenate(
        [
            jnp.where(col < 256, st, zero),
            jnp.where(col >= 256, st, zero),
            jnp.where(col < 256, zr, zero),
            jnp.where(col >= 256, zr, zero),
        ],
        axis=0,
    ).astype(BF)
    d = dx[...]
    far = mm(d, rhs)
    eqs, eks = [], []
    top, low = None, None
    for h in range(2):
        cols = slice(256 * h, 256 * h + 256)
        own = jnp.where(head == h, d, jnp.zeros_like(d))
        q, k = pq[:, cols], pk[:, cols]
        a0 = jnp.where(below(half, half, 0), mm_t(own[:half], v1[:half]), 0.0).astype(BF)
        a1 = jnp.where(below(half, rows, half), mm_t(own[half:], v1), 0.0).astype(BF)
        dpq = jnp.concatenate([mm(a0, k[:half]), mm(a1, k)], axis=0) + far[:, cols]
        eqs.append((dpq * q.astype(F32)).astype(BF))
        i0 = lax.broadcasted_iota(jnp.int32, (half, rows), 1)
        up0 = i0 >= lax.broadcasted_iota(jnp.int32, (half, rows), 0)
        up1 = up0[:, :half]
        b0 = jnp.where(up0, mm_t(v1[:half], own), 0.0).astype(BF)
        b1 = jnp.where(up1, mm_t(v1[half:], own[half:]), 0.0).astype(BF)
        dpk = jnp.concatenate([mm(b0, q), mm(b1, q[half:])], axis=0)
        eks.append((dpk * k.astype(F32)).astype(BF))
        c0 = jnp.where(up0, mm_t(k[:half], q), 0.0).astype(BF)
        c1 = jnp.where(up1, mm_t(k[half:], q[half:]), 0.0).astype(BF)
        t, l = mm(c0, own[:, :LANES]), mm(c1, own[half:, :LANES])
        top, low = (t, l) if h == 0 else (top + t, low + l)
    fw = blocks_of(fx[0])
    r = mm(jnp.concatenate(eqs, axis=1), fw)
    dq[...] = (SHRINK * (r[:, :LANES] + 2.0 * qs[...].astype(F32) * r[:, LANES:])).astype(BF)
    r = mm(jnp.concatenate(eks, axis=1), fw)
    dkl[...] = r[:, :LANES] + 2.0 * ks[...].astype(F32) * r[:, LANES:]
    dvl[:half] = top
    dvl[half:] = low


def last_kernel(
    s, bits, x, dx1, gain, ks, vv, pk, mine, other, fx, dq, dkl, dvl, wq, wk, wv,
    *refs,
):
    grad, dk, dv, ng, dh1 = refs[-5:]
    p = pl.program_id(0)
    rows = pk.shape[0]
    col = lanes_of(512)
    slot = lanes_of(LANES) % 64
    ones = jnp.broadcast_to(jnp.where(slot < 2, 1.0, 0.0), (rows, LANES)).astype(BF)
    v1 = jnp.concatenate([vv[...], ones], axis=1)
    st, z = state_of(mine, other, bits[2] == p // 2, 0)
    zh = z.astype(BF).astype(F32)
    zl = z - zh
    zero = jnp.zeros_like(st)
    row = lax.broadcasted_iota(jnp.int32, (64, 512), 0)
    zr = jnp.where(row == 0, zh, jnp.where(row == 1, zl, 0.0))
    rhs = jnp.concatenate(
        [
            jnp.where(col < 256, st, zero),
            jnp.where(col >= 256, st, zero),
            jnp.where(col < 256, zr, zero),
            jnp.where(col >= 256, zr, zero),
        ],
        axis=0,
    ).astype(BF)
    dpk = mm(v1, rhs)
    ek = (dpk * pk[...].astype(F32)).astype(BF)
    r = mm(ek, blocks_of(fx[0]))
    k = SHRINK * (dkl[...] + r[:, :LANES] + 2.0 * ks[...].astype(F32) * r[:, LANES:])
    k = k.astype(BF)
    v = (dvl[...] + mm_t(pk[...], rhs[:LANES])).astype(BF)
    dk[...], dv[...] = k, v
    w = jnp.concatenate([wq[...], wk[...], wv[...]], axis=1)
    part = mm_t(jnp.concatenate([dq[...], k, v], axis=1), w)

    @pl.when(p == 0)
    def _():
        dh1[...] = part

    @pl.when(p > 0)
    def _():
        dh1[...] += part

    @pl.when(p == pl.num_programs(0) - 1)
    def _():
        _, xh, inv = norm(x[0].astype(F32), gain[...], gain[...])
        e = dh1[...]
        ng[...] = two_rows(
            jnp.sum(e * xh, axis=0, keepdims=True), jnp.sum(e, axis=0, keepdims=True)
        )
        grad[0] = dx1[...] + norm_grad(e, xh, inv, gain[...])


def block_kernel(g0, g1, f0, f1, h0, h1, u0, u1, down, up):
    p = pl.program_id(0)

    @pl.when(p < 4)
    def _():
        down[...] = mm(g0[...].T, f0[...]) + mm(g1[...].T, f1[...])

    @pl.when(p >= 4)
    def _():
        up[...] = mm(h0[...].T, u0[...]) + mm(h1[...].T, u1[...])


def early_kernel(c, a0, a1, b0, b1, a2, a3, b2, b3, out):
    out[:, :512] = mm(a0[...].T, b0[...]) + mm(a1[...].T, b1[...])
    out[:, 512:] = mm(a2[...].T, b2[...]) + mm(a3[...].T, b3[...])


def late_kernel(c, a0, a1, b0, b1, b2, b3, b4, b5, n0, n1, n2, n3, out):
    a = jnp.concatenate([a0[...].T, a1[...].T], axis=1)
    for n, (first, second) in enumerate(((b0, b1), (b2, b3), (b4, b5))):
        both = jnp.concatenate([first[...], second[...]], axis=0)
        out[:, 512 * n : 512 * n + 512] = mm(a, both)
    sums = [n0[...] + n1[...], n2[...] + n3[...]]
    out[:, 1536:] = jnp.concatenate(sums + [jnp.zeros((112, out.shape[0]), F32)], axis=0).T


def params(limit):
    return pltpu.CompilerParams(vmem_limit_bytes=limit * 2**20)


def full(shape):
    return pl.BlockSpec(shape, lambda p, n=len(shape): (0,) * n)


def of_seq(s, shape):
    return pl.BlockSpec((1,) + shape, lambda p: (s, 0, 0))


def cols(rows, width, first=0):
    return pl.BlockSpec((rows, width), lambda p: (0, first + p))


SMEM = pl.BlockSpec(memory_space=pltpu.SMEM)
HEADS = pl.BlockSpec((2, 72, 256), lambda p: (p % 2, 0, 0))
PAIR = pl.BlockSpec((1, 512, 64), lambda p: (p, 0, 0))


def arr(shape, dtype):
    return jax.ShapeDtypeStruct(shape, dtype)


ANY = pl.BlockSpec(memory_space=pl.ANY)


def call(
    kernel, grid, ins, outs, scratch=(), flops=0, nbytes=0, scalars=0, aliases={},
    grant=16,
):
    def run(*args, after=()):
        count, waits = len(ins) + scalars, len(after)

        def waiting(*refs):
            kernel(*refs[:count], *refs[count + waits :])

        return pl.pallas_call(
            waiting,
            grid_spec=pltpu.PrefetchScalarGridSpec(
                num_scalar_prefetch=scalars,
                grid=(grid,),
                in_specs=list(ins) + [ANY] * waits,
                out_specs=[o[0] for o in outs],
                scratch_shapes=list(scratch),
            ),
            out_shape=[arr(*o[1:]) for o in outs],
            compiler_params=params(grant),
            input_output_aliases=aliases,
            cost_estimate=pl.CostEstimate(flops=flops, bytes_accessed=nbytes, transcendentals=0),
        )(*args, *after)

    return run


def simple(kernel, after, *parts):
    spec = full(parts[0].shape)
    return call(
        kernel, 1, [spec] * len(parts), [(spec, parts[0].shape, F32)],
        flops=parts[0].size, nbytes=12 * parts[0].size,
    )(*parts, after=after)[0]


def half_of(give):
    return (lambda c: 1 - c[0]) if give else (lambda c: c[0])


def whole(shape):
    return pl.BlockSpec(shape, lambda p, c: (0,) * len(shape))


def block_weights(gl, df, h2, du, after=()):
    rows, width = df[0].shape
    wide = gl[0].shape[1]
    n = wide // 512
    one = full((rows, width))
    first = lambda p: jnp.minimum(p, n - 1)
    second = lambda p: jnp.maximum(p - n, 0)
    sg = pl.BlockSpec((rows, 512), lambda p: (0, first(p)))
    su = pl.BlockSpec((rows, 512), lambda p: (0, second(p)))
    return call(
        block_kernel, 2 * n - 1, [sg, sg, one, one, one, one, su, su],
        [(pl.BlockSpec((512, width), lambda p: (first(p), 0)), (wide, width), F32),
         (pl.BlockSpec((width, 512), lambda p: (0, second(p))), (width, wide - 512), F32)],
        flops=8 * rows * width * wide, nbytes=8 * width * wide + 8 * rows * wide,
    )(*gl, *df, *h2, *du, after=after)


def early_weights(give, bits, h2, du, a, db, after=()):
    rows, n = db[0].shape
    m = n // 2
    at, end = half_of(give), du[0].shape[1] // 512 - 1
    sa, sb = pl.BlockSpec((rows, m), lambda p, c: (0, at(c))), whole((rows, n))
    sd = pl.BlockSpec((rows, 512), lambda p, c: (0, end))
    return call(
        early_kernel, 1, [sa, sa, sd, sd, sa, sa, sb, sb],
        [(whole((m, 2 * n)), (m, 2 * n), F32)],
        flops=8 * rows * m * n, nbytes=8 * m * n + 8 * rows * n, scalars=1,
    )(bits, *h2, *du, *a, *db, after=after)[0]


def late_weights(give, bits, h1, dq, dk, dv, ng1, ng2, after=()):
    rows, n = dk[0].shape
    m = n // 2
    at = half_of(give)
    sa, sb = pl.BlockSpec((rows, m), lambda p, c: (0, at(c))), whole((rows, n))
    sn = pl.BlockSpec((8, m), lambda p, c: (0, at(c)))
    wide = 3 * n + LANES
    return call(
        late_kernel, 1, [sa] * 2 + [sb] * 6 + [sn] * 4, [(whole((m, wide)), (m, wide), F32)],
        flops=12 * rows * m * n, nbytes=12 * m * n + 12 * rows * n, scalars=1,
    )(bits, *h1, *dq, *dk, *dv, *ng1, *ng2, after=after)[0]


FRONT = (
    "M0", "f", "M1", "f", "g", "Q0", "f", "g", "Q1", "f", "g", "A0", "f", "g", "A1", "g", "N0",
    "p", "N1", "q", "p",
)
BACK = (
    "p", "q", "Ge", "e", "I0a", "Ke", "p", "q", "e", "I0b", "I1a", "p", "q", "e", "I1b", "e",
    "L0", "q", "e", "L1", "Gk", "k", "Kk", "e", "k", "e", "k", "e", "k", "e", "k", "e", "k", "Fe",
    "k", "k", "k", "k", "Fk",
)


def body(
    comm,
    inputs,
    lengths,
    norm1_gain,
    norm1_bias,
    qkv_weight,
    features,
    out_weight,
    norm2_gain,
    norm2_bias,
    up_weight,
    down_weight,
    cotangent,
):
    seqs, rows, width = inputs.shape
    wide = up_weight.shape[1]
    first_row = (comm.position() * rows).astype(jnp.int32)
    meta = jnp.concatenate([first_row[None], lengths])
    fx = features.reshape(4, 512, 64)
    bits = comm.bits()
    g1, n1, g2, n2 = (v[None] for v in (norm1_gain, norm1_bias, norm2_gain, norm2_bias))
    vec = full((1, width))
    act = cols(rows, LANES)
    big = cols(rows, 512)
    heads = (4, 72, 256)
    states = [(full(heads), heads, F32)] * 2

    def maps_of(s, after):
        return call(
            functools.partial(map_kernel, s), 4,
            [SMEM, SMEM, of_seq(s, (rows, width)), vec, vec]
            + [cols(width, LANES, 4 * n) for n in (1, 2)] + [PAIR],
            [(full((rows, width)), (rows, width), BF)]
            + [(act, (rows, width), BF)] * 2
            + [(big, (rows, 2048), BF)] + states,
            flops=rows * 3_000_000, nbytes=8 * 2**20,
        )(meta, bits, inputs, g1, n1, qkv_weight, qkv_weight, fx, after=after)

    def queries_of(h1, after):
        return call(
            query_kernel, 4, [full((rows, width)), cols(width, LANES), PAIR],
            [(act, (rows, width), BF), (big, (rows, 2048), BF)],
            flops=rows * 1_800_000, nbytes=4 * 2**20,
        )(h1, qkv_weight, fx, after=after)

    def locals_of(s, after):
        _, _, _, vv, pq, pk = maps[s]
        return call(
            local_kernel, 4, [big, big, act],
            [(cols(rows, 256), (rows, 1024), F32)],
            flops=rows * 6_000_000, nbytes=7 * 2**20,
        )(pq, pk, vv, after=after)[0]

    def middle_of(s, prefix, after):
        pq = maps[s][4]
        return call(
                functools.partial(middle_kernel, s), wide // 1024,
                [SMEM, SMEM, of_seq(s, (rows, width)), of_seq(s, (rows, width)), full((rows, 2048)),
                 full((rows, 1024)), full(heads), full(heads), vec, vec, full((width, width)),
                 cols(width, 1024), pl.BlockSpec((1024, width), lambda p: (p, 0))] + [ANY] * s,
                [(of_seq(s, (rows, width)), inputs.shape, BF),
                 (full((rows, width)), (rows, width), F32),
                 (full((rows, 1024)), (rows, 1024), BF),
                 (full((rows, width)), (rows, width), BF),
                 (full((rows, width)), (rows, width), BF),
                 (full((rows, width)), (rows, width), BF),
                 (full((rows, width)), (rows, width), BF),
                 (cols(rows, 1024), (rows, wide), BF),
                 (cols(rows, 1024), (rows, wide), BF),
                 *states,
                 (full((8, width)), (8, width), F32)],
                scratch=[pltpu.VMEM((rows, width), F32), pltpu.VMEM((rows, width), F32),
                         pltpu.VMEM((rows, LANES), F32)]
                + [pltpu.VMEM((rows, width), F32)] * 3,
                flops=rows * 11_000_000, nbytes=24 * 2**20, grant=30, aliases={13: 0} if s else {},
            )(meta, bits, inputs, cotangent, pq, locals_[s], *prefix, g2, n2, out_weight,
              up_weight, down_weight, *([mids[0][0]] if s else []), after=after)

    def inner(s, part, after):
        _, qs, ks, vv, pq, pk = maps[s]
        here = lambda wide: pl.BlockSpec((rows, wide), lambda p: (0, p + 2 * part))
        side = pl.BlockSpec((2, 72, 256), lambda p: (p % 2, 0, 0))
        fxs = pl.BlockSpec((1, 512, 64), lambda p: (p + 2 * part, 0, 0))
        act, big = here(LANES), here(512)
        earlier = tuple(inners[s]) if part else ()
        return call(
            functools.partial(inner_kernel, part), 2,
            [SMEM, act, act, act, big, big, here(256), side, side, fxs] + [ANY] * len(earlier),
            [(act, (rows, width), BF), (act, (rows, width), F32), (act, (rows, width), F32)],
            flops=rows * 10_000_000, nbytes=6 * 2**20,
            aliases={10 + n: n for n in range(len(earlier))},
        )(bits, qs, ks, vv, pq, pk, mids[s][2], *state[s], fx, *earlier, after=after)

    def last(s, later, after):
        _, qs, ks, vv, pq, pk = maps[s]
        return call(
            functools.partial(last_kernel, s), 4,
            [SMEM, of_seq(s, (rows, width)), full((rows, width)), vec, act, act, big, HEADS, HEADS,
             PAIR,
             act, act, act] + [cols(width, LANES, 4 * n) for n in range(3)] + [ANY] * s,
            [(of_seq(s, (rows, width)), inputs.shape, F32), (act, (rows, width), BF),
             (act, (rows, width), BF), (full((8, width)), (8, width), F32)],
            scratch=[pltpu.VMEM((rows, width), F32)],
            flops=rows * 6_000_000, nbytes=11 * 2**20, aliases={16: 0} if s else {},
        )(bits, inputs, mids[s][1], g1, ks, vv, pk, *later, fx, *inners[s],
          qkv_weight, qkv_weight, qkv_weight, *([lasts[0][0]] if s else []), after=after)

    maps, locals_, mids, state, inners, lasts, kept, flows = {}, {}, {}, {}, {}, {}, {}, {}
    ends = {}

    def of_mids(*index):
        return [[mids[s][n] for s in range(seqs)] for n in index]

    def weights(name, give, after):
        if name == "e":
            return early_weights(give, bits, *of_mids(5, 8, 3, 4), after=after)
        h1 = [maps[s][0] for s in range(seqs)]
        dq = [inners[s][0] for s in range(seqs)]
        dk, dv, ng1 = ([lasts[s][n] for s in range(seqs)] for n in (1, 2, 3))
        return late_weights(give, bits, h1, dq, dk, dv, ng1, *of_mids(11), after=after)

    shapes = {
        "e": ((width, 512), (width, width)),
        "k": ((width, 3 * width), (width, LANES)),
    }

    def play(items, token):
        for item in items:
            after = () if token is None else (token,)
            kind, name = item[0], item[-1]
            s = int(item[1]) if item[1:2] in ("0", "1") else None
            if kind == "M":
                h1, ks, vv, pk, keep, token = maps_of(s, after)
                maps[s] = [h1, None, ks, vv, None, pk]
                flows["fg"[s]] = comm.carry(keep, token, bits, False)
                next(flows["fg"[s]])
            elif kind == "Q":
                maps[s][1], maps[s][4] = queries_of(maps[s][0], after)
                token = maps[s][1]
            elif kind == "A":
                token = locals_[s] = locals_of(s, after)
            elif kind == "N":
                state[s] = next(flows["fg"[s]])
                mids[s] = middle_of(s, state[s], after)
                token = mids[s][10]
                flows["pq"[s]] = comm.carry(mids[s][9], token, bits, True)
                next(flows["pq"[s]])
            elif kind == "I":
                inners[s] = inner(s, int(name == "b"), after)
                token = inners[s][1]
            elif kind == "L":
                lasts[s] = last(s, next(flows["pq"[s]]), after)
                token = lasts[s][0]
            elif kind == "G":
                token = weights(name, True, after)
                flows[name] = comm.sums(
                    token, functools.partial(kept.get, name), bits, shapes[name]
                )
                next(flows[name])
            elif kind == "K":
                token = kept[name] = weights(name, False, after)
            elif kind == "F":
                ends[name] = flows[name].send(after)
                token = ends[name][0]
            else:
                token = flows[name].send(after)
        return token

    token = play(FRONT, None)
    parts = block_weights(*of_mids(7, 6, 5, 8), after=(token,))
    down_grad, up_grad = comm.whole_sum(tuple(parts))

    def rest():
        play(BACK, parts[1])
        qkv_grad, small = ends["k"]
        return *ends["e"], qkv_grad, small[:, :16].T, lasts[seqs - 1][0]

    def nothing():
        shaped = [(width, 512), (width, width), (width, 3 * width), (16, width)]
        return *(jnp.zeros(s, F32) for s in shaped), cotangent.astype(F32)

    up_end, outw_grad, qkv_grad, small, grad = lax.cond(jnp.max(lengths) > 0, rest, nothing)
    up_grad = jnp.concatenate([up_grad, up_end], axis=1)
    out = mids[seqs - 1][0]
    return (
        out,
        grad,
        small[0],
        small[1],
        qkv_grad,
        outw_grad,
        small[8],
        small[9],
        up_grad,
        down_grad,
    )


def solution(mesh):
    comm = AnySlice()
    if dict(mesh.shape) == {"seq": 8, "batch": 4}:
        comm = Slice32()
        mesh = Mesh(mesh.devices.reshape(4, 2, 2, 2), comm.axes)
    return jax.shard_map(
        functools.partial(body, comm),
        mesh=mesh,
        in_specs=(comm.rows, comm.lens) + (P(),) * 9 + (comm.rows,),
        out_specs=(comm.rows, comm.rows) + (P(),) * 8,
        check_vma=False,
    )
```

```python
import functools

import jax
import jax.numpy as jnp
from jax import lax
from jax.experimental import pallas as pl
from jax.experimental.pallas import tpu as pltpu
from jax.sharding import Mesh, PartitionSpec as P

EPS = 1e-05
SHRINK = 64 ** (-0.25)
SCALE = 256 ** (-0.5)


class Slice32:
    axes = ("z", "y", "x", "c")
    rows = P(("x", "c"), ("z", "y"), None)
    lens = P(("x", "c"))
    swaps = {
        "c": ("c", [(0, 1), (1, 0)]),
        "x": ("x", [(0, 1), (1, 0)]),
        "y": ("y", [(0, 1), (1, 0)]),
        "z1": ("z", [(0, 1), (1, 0), (2, 3), (3, 2)]),
        "z2": ("z", [(0, 2), (2, 0), (1, 3), (3, 1)]),
    }

    def late_rows(self, width):
        return width // 2

    def position(self):
        return lax.axis_index("z") * 2 + lax.axis_index("y")

    def bits(self):
        z = lax.axis_index("z")
        at = [lax.axis_index(a) for a in "cxy"] + [z % 2, z // 2]
        return jnp.stack(at).astype(jnp.int32)

    def swap(self, part, axis):
        name, pairs = self.swaps[axis]
        return lax.ppermute(part, name, pairs)

    def whole_sum(self, part):
        return lax.psum(part, self.axes)

    def carry(self, keep, give, bits, reverse):
        after = yield
        got = self.swap(give, "y")
        after = yield give
        total = simple(add_kernel, after, keep, got)
        hops = [(3, 2), (2, 1), (1, 0)] if reverse else [(0, 1), (1, 2), (2, 3)]
        out, arrived = total, []
        for hop in hops:
            arrived.append(lax.ppermute(out, "z", [hop]))
            after = yield out
            if len(arrived) < 3:
                out = simple(add_kernel, after, total, arrived[-1])
        mine, send = call(
            functools.partial(close_kernel, reverse), 1, [SMEM] + [full(keep.shape)] * 5,
            [(full(keep.shape), keep.shape, F32)] * 2, flops=keep.size, nbytes=28 * keep.size,
        )(bits, keep, got, *arrived, after=after)
        other = self.swap(send, "y")
        yield send
        yield mine, other

    def sums(self, give, keep, bits, shapes):
        after = yield
        got = self.swap(give, "c")
        after = yield give
        rows, wide = give.shape

        def fold(ways, parts, after, count):
            size = parts[0].shape[0] // count
            shape = (size, wide)
            outs = [(full(shape), shape, F32)] * (4 if count == 4 else 2 * len(ways))
            return call(
                functools.partial(fold_kernel, ways, count), 1,
                [SMEM] + [full(p.shape) for p in parts], outs,
                flops=parts[0].size, nbytes=12 * parts[0].size,
            )(bits, *parts, after=after)

        give_a, give_b, keep_a, keep_b = fold((1, 2), (keep(), got), after, 4)
        got_a, got_b = self.swap(give_a, "x"), self.swap(give_b, "y")
        after = yield give_a
        give_a, give_b, keep_a, keep_b = fold((2, 1), (keep_a, got_a, keep_b, got_b), after, 2)
        got_a, got_b = self.swap(give_a, "y"), self.swap(give_b, "x")
        after = yield give_a
        both = rows // 4
        part = (full((both // 2, wide)), (both // 2, wide), F32)
        ins = [SMEM] + [full((both // 2, wide))] * 4
        give, keep = call(merge_kernel, 1, ins, [part] * 2, nbytes=24 * both * wide)(
            bits, keep_a, got_a, keep_b, got_b, after=after
        )
        got = self.swap(give, "z1")
        after = yield give
        give, keep = fold((4,), (keep, got), after, 2)
        got = self.swap(give, "z2")
        after = yield give
        one = simple(add_kernel, after, keep, got)
        got = self.swap(one, "z2")
        after = yield one
        (two,) = self.join((4,), bits, (one, got), after)
        got = self.swap(two, "z1")
        after = yield two
        (four,) = self.join((3,), bits, (two, got), after)
        a, b = four[: both // 2], four[both // 2 :]
        got_a, got_b = self.swap(a, "y"), self.swap(b, "x")
        after = yield a
        a, b = self.join((2, 1), bits, (a, got_a, b, got_b), after)
        got_a, got_b = self.swap(a, "x"), self.swap(b, "y")
        after = yield a
        part = call(
            functools.partial(join_kernel, (1, 2), True), 1,
            [SMEM] + [full(a.shape)] * 4, [(full((rows, wide)), (rows, wide), F32)],
            nbytes=8 * rows * wide,
        )(bits, a, got_a, b, got_b, after=after)[0]
        yield part

    def close(self, part, bits, shapes, after=()):
        got = self.swap(part, "c")
        return call(
            last_join_kernel, 1, [SMEM] + [full(part.shape)] * 2,
            [(full(s), s, F32) for s in shapes], nbytes=16 * part.size,
        )(bits, part, got, after=after)

    def join(self, ways, bits, parts, after):
        rows, wide = parts[0].shape
        out = (full((2 * rows, wide)), (2 * rows, wide), F32)
        return call(
            functools.partial(join_kernel, ways, False), 1,
            [SMEM] + [full(p.shape) for p in parts], [out] * len(ways),
            nbytes=16 * rows * wide,
        )(bits, *parts, after=after)


class AnySlice:
    axes = ("seq", "batch")
    rows = P("batch", "seq", None)
    lens = P("batch")

    def late_rows(self, width):
        return width

    def position(self):
        return lax.axis_index("seq")

    def bits(self):
        return jnp.zeros((5,), jnp.int32)

    def whole_sum(self, part):
        return lax.psum(part, self.axes)

    def carry(self, keep, give, bits, reverse):
        size = lax.axis_size("seq")

        def shift(part, by):
            pairs = [(i, i + by) for i in range(size - by)]
            return lax.ppermute(part, "seq", [(b, a) for a, b in pairs] if reverse else pairs)

        for _ in range(6):
            yield keep
        out, by = shift(jnp.stack([keep, give]), 1), 1
        while by < size:
            out, by = out + shift(out, by), by * 2
        yield out[0], out[1]

    def sums(self, give, keep, bits, shapes):
        for _ in range(10):
            yield give
        yield jnp.concatenate([keep(), give], axis=0)

    def close(self, part, bits, shapes, after=()):
        part = lax.psum(part, self.axes)
        outs, at = [], 0
        for shape in shapes:
            outs.append(part[:, at : at + shape[1]])
            at += shape[1]
        return outs
LANES = 128
BF = jnp.bfloat16
F32 = jnp.float32


def mm(a, b):
    return jnp.dot(a, b, preferred_element_type=F32)


def mm_t(a, b):
    return lax.dot_general(a, b, (((1,), (1,)), ((), ())), preferred_element_type=F32)


def lanes_of(width):
    return lax.broadcasted_iota(jnp.int32, (1, width), 1)


def head_of(width):
    return (lanes_of(width) % LANES) // 64


def live_of(meta, s, rows):
    at = lax.broadcasted_iota(jnp.int32, (rows, 1), 0) + meta[0]
    return (at < meta[1 + s]).astype(F32)


def norm(values, gain, bias):
    mu = jnp.mean(values, axis=-1, keepdims=True)
    centred = values - mu
    inv = lax.rsqrt(jnp.mean(centred * centred, axis=-1, keepdims=True) + EPS)
    xhat = centred * inv
    return xhat * gain + bias, xhat, inv


def norm_grad(e, xhat, inv, gain):
    eg = e * gain
    return inv * (
        eg
        - jnp.mean(eg, axis=-1, keepdims=True)
        - xhat * jnp.mean(eg * xhat, axis=-1, keepdims=True)
    )


def blocks_of(f):
    shape = (f.shape[0], LANES)
    own = lax.broadcasted_iota(jnp.int32, shape, 0) // 256 == head_of(LANES)
    diagonal = jnp.where(own, jnp.concatenate([f, f], axis=1), jnp.zeros(shape, BF))
    half = jnp.where(own, -0.5, 0.0).astype(BF)
    return jnp.concatenate([diagonal, half], axis=1)


def two_rows(first, second):
    row = lax.broadcasted_iota(jnp.int32, (8, first.shape[1]), 0)
    return jnp.where(row == 0, first, jnp.where(row == 1, second, 0.0))


def phi(u, f):
    fw = blocks_of(f)
    sq = jnp.square(u.astype(F32))
    hi = sq.astype(BF)
    lo = (sq - hi.astype(F32)).astype(BF)
    lhs = jnp.concatenate([u, hi, lo], axis=1)
    return jnp.exp(mm_t(lhs, jnp.concatenate([fw, fw[:, LANES:]], axis=1))) * SCALE


def map_kernel(s, meta, bits, x, gain, bias, wk, wv, fx, h1, ks, vv, pk, keep, give):
    p = pl.program_id(0)
    rows = x.shape[1]

    @pl.when(p == 0)
    def _():
        h1[...] = norm(x[0].astype(F32), gain[...], bias[...])[0].astype(BF)

    kv = mm(h1[...], jnp.concatenate([wk[...], wv[...]], axis=1))
    k = (SHRINK * kv[:, :LANES]).astype(BF)
    v = kv[:, LANES:].astype(BF)
    ks[...], vv[...] = k, v
    phk = (phi(k, fx[0]) * live_of(meta, s, rows)).astype(BF)
    pk[...] = phk
    ds = mm(jnp.concatenate([v.T, jnp.ones((16, rows), BF)], axis=0), phk)
    for near, xs in ((True, keep), (False, give)):

        @pl.when((p // 2 == bits[2]) == near)
        def _(xs=xs):
            put_state(xs, 2 * (p % 2), ds[:64, :256], ds[128:129, :256])
            put_state(xs, 2 * (p % 2) + 1, ds[64:128, 256:], ds[128:129, 256:])


def query_kernel(h1, wq, fx, qs, pq):
    q = (SHRINK * mm(h1[...], wq[...])).astype(BF)
    qs[...] = q
    pq[...] = phi(q, fx[0]).astype(BF)


def put_state(xs, at, state, total):
    xs[at, :64] = state
    xs[at, 64:] = jnp.broadcast_to(total, (8, 256))


def add_kernel(*refs):
    *parts, out = refs
    total = parts[0][...]
    for part in parts[1:]:
        total = total + part[...]
    out[...] = total


def close_kernel(reverse, bits, keep, got, first, second, third, mine, send):
    before = (first[...] + second[...]) + third[...]
    early = (bits[2] == (1 if reverse else 0)).astype(F32)
    mine[...] = before + (1.0 - early) * got[...]
    send[...] = before + early * keep[...]


def fold_kernel(ways, count, bits, *refs):
    if count == 4:
        part, got, *outs = refs
        size = part.shape[0] // 4
        for n, way in enumerate(ways):
            bit = bits[way]
            for out, side in ((outs[n], 1 - bit), (outs[2 + n], bit)):
                at = pl.ds(pl.multiple_of((2 * n + side) * size, 8), size)
                out[...] = part[at, :] + got[at, :]
        return
    pairs = len(ways)
    for n, way in enumerate(ways):
        part, got = refs[2 * n], refs[2 * n + 1]
        outs = refs[2 * pairs :]
        size, bit = part.shape[0] // 2, bits[way]
        for out, side in ((outs[n], 1 - bit), (outs[pairs + n], bit)):
            at = pl.ds(pl.multiple_of(side * size, 8), size)
            out[...] = part[at, :] + got[at, :]


def merge_kernel(bits, part_a, got_a, part_b, got_b, give, keep):
    first = bits[3] == 0
    a, b = part_a[...] + got_a[...], part_b[...] + got_b[...]
    keep[...] = jnp.where(first, a, b)
    give[...] = jnp.where(first, b, a)


def join_kernel(ways, one, bits, *refs):
    outs = refs[2 * len(ways) :]
    for n, way in enumerate(ways):
        part, got = refs[2 * n], refs[2 * n + 1]
        size, bit = part.shape[0], bits[way]
        out, base = (outs[0], 2 * n * size) if one else (outs[n], 0)
        out[pl.ds(pl.multiple_of(base + bit * size, 8), size), :] = part[...]
        out[pl.ds(pl.multiple_of(base + (1 - bit) * size, 8), size), :] = got[...]


def last_join_kernel(bits, part, got, *outs):
    size, at = part.shape[0], 0
    for out in outs:
        wide = out.shape[1]
        for ref, side in ((part, bits[0]), (got, 1 - bits[0])):
            out[pl.ds(pl.multiple_of(side * size, 8), size), :] = ref[:, at : at + wide]
        at += wide


def below(rows, cols, shift):
    i = lax.broadcasted_iota(jnp.int32, (rows, cols), 0) + shift
    return lax.broadcasted_iota(jnp.int32, (rows, cols), 1) <= i


def local_kernel(pq, pk, vv, nd):
    rows = pq.shape[0]
    half = rows // 2
    v = vv[...]
    values = jnp.concatenate([v, jnp.ones_like(v)], axis=1)
    head = head_of(2 * LANES)
    top, low = None, None
    for h in range(2):
        cols = slice(256 * h, 256 * h + 256)
        mine = jnp.where(head == h, values, jnp.zeros_like(values))
        a0 = mm_t(pq[:half, cols], pk[:half, cols])
        a0 = jnp.where(below(half, half, 0), a0, 0.0).astype(BF)
        a1 = mm_t(pq[half:, cols], pk[:, cols])
        a1 = jnp.where(below(half, rows, half), a1, 0.0).astype(BF)
        t, l = mm(a0, mine[:half]), mm(a1, mine)
        top, low = (t, l) if h == 0 else (top + t, low + l)
    nd[:half] = top
    nd[half:] = low


def gelu_parts(u):
    c0, c1 = 0.7978845608028654, 0.044715
    sq = u * u
    t = jnp.tanh(u * (c0 + (c0 * c1) * sq))
    half_up = 0.5 + 0.5 * t
    slope = half_up + (0.5 * u) * (1.0 - t * t) * (c0 + (3.0 * c0 * c1) * sq)
    return u * half_up, slope


def state_of(mine, other, near, first):
    two = [jnp.where(near, mine[first + h], other[first + h]) for h in range(2)]
    st = jnp.concatenate([t[:64] for t in two], axis=1)
    return st, jnp.concatenate([t[64:65] for t in two], axis=1)


def middle_kernel(
    s, meta, bits, x, dy, pq, nd, mine, other, gain, bias, wo, wup, wdown, *refs
):
    middle_body(s, meta, bits, x, dy, pq, nd, mine, other, gain, bias, wo, wup, wdown, *refs[-18:])


def middle_body(
    s, meta, bits, x, dy, pq, nd, mine, other, gain, bias, wo, wup, wdown,
    out, dx1, dx, a_low, db, h2, df, gl, du, gs_keep, gs_give, ng,
    x1, xhat, inv, f, dh2, den,
):
    c = pl.program_id(0)
    rows = x.shape[1]
    live = live_of(meta, s, rows)
    col = lanes_of(512)

    @pl.when(c == 0)
    def _():
        for p in range(4):
            st, z = state_of(mine, other, bits[2] == p // 2, 2 * (p % 2))
            zero = jnp.zeros_like(st)
            zb = jnp.broadcast_to(z, st.shape)
            rhs = jnp.concatenate(
                [
                    jnp.where(col < 256, st, zero),
                    jnp.where(col >= 256, st, zero),
                    jnp.where(col < 256, zb, zero),
                    jnp.where(col >= 256, zb, zero),
                ],
                axis=0,
            ).astype(BF)
            both = mm_t(pq[:, 512 * p : 512 * p + 512], rhs) + nd[:, 256 * p : 256 * p + 256]
            lanes = slice(LANES * p, LANES * p + LANES)
            den[:, lanes] = both[:, LANES:]
            f[:, lanes] = both[:, :LANES] / both[:, LANES:]
        a_low[...] = f[...].astype(BF)
        mid = x[0].astype(F32) + live * mm(a_low[...], wo[...])
        x1[...] = mid
        h, xh, iv = norm(mid, gain[...], bias[...])
        h2[...] = h.astype(BF)
        xhat[...] = xh
        inv[...] = jnp.broadcast_to(iv, inv.shape)
        df[...] = (live * dy[0].astype(F32)).astype(BF)

    g, slope = gelu_parts(mm(h2[...], wup[...]))
    g = g.astype(BF)
    gl[...] = g
    d = (slope * mm_t(df[...], wdown[...])).astype(BF)
    du[...] = d
    part = mm(g, wdown[...])
    back = mm_t(d, wup[...])

    @pl.when(c == 0)
    def _():
        x1[...] += live * part
        dh2[...] = back

    @pl.when(c > 0)
    def _():
        x1[...] += live * part
        dh2[...] += back

    @pl.when(c == pl.num_programs(0) - 1)
    def _():
        out[0] = x1[...].astype(BF)
        e = dh2[...]
        xh = xhat[...]
        ng[...] = two_rows(
            jnp.sum(e * xh, axis=0, keepdims=True), jnp.sum(e, axis=0, keepdims=True)
        )
        g1 = dy[0].astype(F32) + norm_grad(e, xh, inv[:, :1], gain[...])
        dx1[...] = g1
        db[...] = (live * g1).astype(BF)
        da = mm_t(db[...], wo[...])
        block = jnp.where(
            lax.broadcasted_iota(jnp.int32, (2 * LANES, LANES), 0) % LANES // 64
            == lax.broadcasted_iota(jnp.int32, (2 * LANES, LANES), 1) // 64,
            -1.0,
            0.0,
        ).astype(BF)
        slot = lanes_of(LANES) % 64
        for p in range(4):
            lanes = slice(LANES * p, LANES * p + LANES)
            dn = da[:, lanes] / den[:, lanes]
            w = dn * f[:, lanes]
            hi = w.astype(BF)
            lo = (w - hi.astype(F32)).astype(BF)
            dd = mm(jnp.concatenate([hi, lo], axis=1), block)
            hi = dd.astype(BF).astype(F32)
            lo = dd - hi
            two = jnp.where((slot == 0) | (slot == 2), hi, jnp.where(slot == 1, lo, 0.0))
            both = jnp.concatenate([dn.astype(BF), two.astype(BF)], axis=1)
            dx[:, 256 * p : 256 * p + 256] = both
            g = mm(both.T, pq[:, 512 * p : 512 * p + 512])
            for near, gs in ((True, gs_keep), (False, gs_give)):

                @pl.when((bits[2] == p // 2) == near)
                def _(gs=gs, g=g):
                    for h in range(2):
                        side, at = slice(256 * h, 256 * h + 256), 128 + 64 * h
                        z = g[at : at + 1, side] + g[at + 1 : at + 2, side]
                        put_state(gs, 2 * (p % 2) + h, g[64 * h : 64 * h + 64, side], z)


def inner_kernel(part, bits, qs, ks, vv, pq, pk, dx, mine, other, fx, *outs):
    p = pl.program_id(0) + 2 * part
    dq, dkl, dvl = outs[-3:]
    rows = pq.shape[0]
    half = rows // 2
    col = lanes_of(512)
    slot = lanes_of(LANES) % 64
    head = head_of(2 * LANES)
    ones = jnp.broadcast_to(jnp.where(slot < 2, 1.0, 0.0), (rows, LANES)).astype(BF)
    v1 = jnp.concatenate([vv[...], ones], axis=1)
    st, z = state_of(mine, other, bits[2] == p // 2, 0)
    zh = z.astype(BF).astype(F32)
    zl = z - zh
    zero = jnp.zeros_like(st)
    row = lax.broadcasted_iota(jnp.int32, (64, 512), 0)
    zr = jnp.where(row < 2, zh, jnp.where(row == 2, zl, 0.0))
    rhs = jnp.concatenate(
        [
            jnp.where(col < 256, st, zero),
            jnp.where(col >= 256, st, zero),
            jnp.where(col < 256, zr, zero),
            jnp.where(col >= 256, zr, zero),
        ],
        axis=0,
    ).astype(BF)
    d = dx[...]
    far = mm(d, rhs)
    eqs, eks = [], []
    top, low = None, None
    for h in range(2):
        cols = slice(256 * h, 256 * h + 256)
        own = jnp.where(head == h, d, jnp.zeros_like(d))
        q, k = pq[:, cols], pk[:, cols]
        a0 = jnp.where(below(half, half, 0), mm_t(own[:half], v1[:half]), 0.0).astype(BF)
        a1 = jnp.where(below(half, rows, half), mm_t(own[half:], v1), 0.0).astype(BF)
        dpq = jnp.concatenate([mm(a0, k[:half]), mm(a1, k)], axis=0) + far[:, cols]
        eqs.append((dpq * q.astype(F32)).astype(BF))
        i0 = lax.broadcasted_iota(jnp.int32, (half, rows), 1)
        up0 = i0 >= lax.broadcasted_iota(jnp.int32, (half, rows), 0)
        up1 = up0[:, :half]
        b0 = jnp.where(up0, mm_t(v1[:half], own), 0.0).astype(BF)
        b1 = jnp.where(up1, mm_t(v1[half:], own[half:]), 0.0).astype(BF)
        dpk = jnp.concatenate([mm(b0, q), mm(b1, q[half:])], axis=0)
        eks.append((dpk * k.astype(F32)).astype(BF))
        c0 = jnp.where(up0, mm_t(k[:half], q), 0.0).astype(BF)
        c1 = jnp.where(up1, mm_t(k[half:], q[half:]), 0.0).astype(BF)
        t, l = mm(c0, own[:, :LANES]), mm(c1, own[half:, :LANES])
        top, low = (t, l) if h == 0 else (top + t, low + l)
    fw = blocks_of(fx[0])
    r = mm(jnp.concatenate(eqs, axis=1), fw)
    dq[...] = (SHRINK * (r[:, :LANES] + 2.0 * qs[...].astype(F32) * r[:, LANES:])).astype(BF)
    r = mm(jnp.concatenate(eks, axis=1), fw)
    dkl[...] = r[:, :LANES] + 2.0 * ks[...].astype(F32) * r[:, LANES:]
    dvl[:half] = top
    dvl[half:] = low


def last_kernel(
    s, bits, x, dx1, gain, ks, vv, pk, mine, other, fx, dq, dkl, dvl, wq, wk, wv,
    *refs,
):
    grad, dk, dv, ng, dh1 = refs[-5:]
    p = pl.program_id(0)
    rows = pk.shape[0]
    col = lanes_of(512)
    slot = lanes_of(LANES) % 64
    ones = jnp.broadcast_to(jnp.where(slot < 2, 1.0, 0.0), (rows, LANES)).astype(BF)
    v1 = jnp.concatenate([vv[...], ones], axis=1)
    st, z = state_of(mine, other, bits[2] == p // 2, 0)
    zh = z.astype(BF).astype(F32)
    zl = z - zh
    zero = jnp.zeros_like(st)
    row = lax.broadcasted_iota(jnp.int32, (64, 512), 0)
    zr = jnp.where(row == 0, zh, jnp.where(row == 1, zl, 0.0))
    rhs = jnp.concatenate(
        [
            jnp.where(col < 256, st, zero),
            jnp.where(col >= 256, st, zero),
            jnp.where(col < 256, zr, zero),
            jnp.where(col >= 256, zr, zero),
        ],
        axis=0,
    ).astype(BF)
    dpk = mm(v1, rhs)
    ek = (dpk * pk[...].astype(F32)).astype(BF)
    r = mm(ek, blocks_of(fx[0]))
    k = SHRINK * (dkl[...] + r[:, :LANES] + 2.0 * ks[...].astype(F32) * r[:, LANES:])
    k = k.astype(BF)
    v = (dvl[...] + mm_t(pk[...], rhs[:LANES])).astype(BF)
    dk[...], dv[...] = k, v
    w = jnp.concatenate([wq[...], wk[...], wv[...]], axis=1)
    part = mm_t(jnp.concatenate([dq[...], k, v], axis=1), w)

    @pl.when(p == 0)
    def _():
        dh1[...] = part

    @pl.when(p > 0)
    def _():
        dh1[...] += part

    @pl.when(p == pl.num_programs(0) - 1)
    def _():
        _, xh, inv = norm(x[0].astype(F32), gain[...], gain[...])
        e = dh1[...]
        ng[...] = two_rows(
            jnp.sum(e * xh, axis=0, keepdims=True), jnp.sum(e, axis=0, keepdims=True)
        )
        grad[0] = dx1[...] + norm_grad(e, xh, inv, gain[...])


def block_kernel(g0, g1, f0, f1, h0, h1, u0, u1, down, up):
    p = pl.program_id(0)

    @pl.when(p < 4)
    def _():
        down[...] = mm(g0[...].T, f0[...]) + mm(g1[...].T, f1[...])

    @pl.when(p >= 4)
    def _():
        up[...] = mm(h0[...].T, u0[...]) + mm(h1[...].T, u1[...])


def early_kernel(c, a0, a1, b0, b1, a2, a3, b2, b3, out):
    out[:, :512] = mm(a0[...].T, b0[...]) + mm(a1[...].T, b1[...])
    out[:, 512:] = mm(a2[...].T, b2[...]) + mm(a3[...].T, b3[...])


def late_kernel(c, a0, a1, b0, b1, b2, b3, b4, b5, n0, n1, n2, n3, out):
    a = jnp.concatenate([a0[...].T, a1[...].T], axis=1)
    for n, (first, second) in enumerate(((b0, b1), (b2, b3), (b4, b5))):
        both = jnp.concatenate([first[...], second[...]], axis=0)
        out[:, 512 * n : 512 * n + 512] = mm(a, both)
    sums = [n0[...] + n1[...], n2[...] + n3[...]]
    out[:, 1536:] = jnp.concatenate(sums + [jnp.zeros((112, out.shape[0]), F32)], axis=0).T


def params(limit):
    return pltpu.CompilerParams(vmem_limit_bytes=limit * 2**20)


def full(shape):
    return pl.BlockSpec(shape, lambda p, n=len(shape): (0,) * n)


def of_seq(s, shape):
    return pl.BlockSpec((1,) + shape, lambda p: (s, 0, 0))


def cols(rows, width, first=0):
    return pl.BlockSpec((rows, width), lambda p: (0, first + p))


SMEM = pl.BlockSpec(memory_space=pltpu.SMEM)
HEADS = pl.BlockSpec((2, 72, 256), lambda p: (p % 2, 0, 0))
PAIR = pl.BlockSpec((1, 512, 64), lambda p: (p, 0, 0))


def arr(shape, dtype):
    return jax.ShapeDtypeStruct(shape, dtype)


ANY = pl.BlockSpec(memory_space=pl.ANY)


def call(
    kernel, grid, ins, outs, scratch=(), flops=0, nbytes=0, scalars=0, aliases={},
    grant=16,
):
    def run(*args, after=()):
        count, waits = len(ins) + scalars, len(after)

        def waiting(*refs):
            kernel(*refs[:count], *refs[count + waits :])

        return pl.pallas_call(
            waiting,
            grid_spec=pltpu.PrefetchScalarGridSpec(
                num_scalar_prefetch=scalars,
                grid=(grid,),
                in_specs=list(ins) + [ANY] * waits,
                out_specs=[o[0] for o in outs],
                scratch_shapes=list(scratch),
            ),
            out_shape=[arr(*o[1:]) for o in outs],
            compiler_params=params(grant),
            input_output_aliases=aliases,
            cost_estimate=pl.CostEstimate(flops=flops, bytes_accessed=nbytes, transcendentals=0),
        )(*args, *after)

    return run


def simple(kernel, after, *parts):
    spec = full(parts[0].shape)
    return call(
        kernel, 1, [spec] * len(parts), [(spec, parts[0].shape, F32)],
        flops=parts[0].size, nbytes=12 * parts[0].size,
    )(*parts, after=after)[0]


def half_of(give):
    return (lambda c: 1 - c[0]) if give else (lambda c: c[0])


def whole(shape):
    return pl.BlockSpec(shape, lambda p, c: (0,) * len(shape))


def block_weights(gl, df, h2, du, after=()):
    rows, width = df[0].shape
    wide = gl[0].shape[1]
    n = wide // 512
    one = full((rows, width))
    first = lambda p: jnp.minimum(p, n - 1)
    second = lambda p: jnp.maximum(p - n, 0)
    sg = pl.BlockSpec((rows, 512), lambda p: (0, first(p)))
    su = pl.BlockSpec((rows, 512), lambda p: (0, second(p)))
    return call(
        block_kernel, 2 * n - 1, [sg, sg, one, one, one, one, su, su],
        [(pl.BlockSpec((512, width), lambda p: (first(p), 0)), (wide, width), F32),
         (pl.BlockSpec((width, 512), lambda p: (0, second(p))), (width, wide - 512), F32)],
        flops=8 * rows * width * wide, nbytes=8 * width * wide + 8 * rows * wide,
    )(*gl, *df, *h2, *du, after=after)


def early_weights(give, bits, h2, du, a, db, after=()):
    rows, n = db[0].shape
    m = n // 2
    at, end = half_of(give), du[0].shape[1] // 512 - 1
    sa, sb = pl.BlockSpec((rows, m), lambda p, c: (0, at(c))), whole((rows, n))
    sd = pl.BlockSpec((rows, 512), lambda p, c: (0, end))
    return call(
        early_kernel, 1, [sa, sa, sd, sd, sa, sa, sb, sb],
        [(whole((m, 2 * n)), (m, 2 * n), F32)],
        flops=8 * rows * m * n, nbytes=8 * m * n + 8 * rows * n, scalars=1,
    )(bits, *h2, *du, *a, *db, after=after)[0]


def late_weights(give, bits, h1, dq, dk, dv, ng1, ng2, after=()):
    rows, n = dk[0].shape
    m = n // 2
    at = half_of(give)
    sa, sb = pl.BlockSpec((rows, m), lambda p, c: (0, at(c))), whole((rows, n))
    sn = pl.BlockSpec((8, m), lambda p, c: (0, at(c)))
    wide = 3 * n + LANES
    return call(
        late_kernel, 1, [sa] * 2 + [sb] * 6 + [sn] * 4, [(whole((m, wide)), (m, wide), F32)],
        flops=12 * rows * m * n, nbytes=12 * m * n + 12 * rows * n, scalars=1,
    )(bits, *h1, *dq, *dk, *dv, *ng1, *ng2, after=after)[0]


FRONT = (
    "M0", "f", "M1", "f", "g", "Q0", "f", "g", "Q1", "f", "g", "A0", "f", "g", "A1", "g", "N0",
    "p", "N1", "q", "p",
)
BACK = (
    "p", "q", "Ge", "e", "I0a", "Ke", "p", "q", "e", "I0b", "I1a", "p", "q", "e", "I1b", "e",
    "L0", "q", "e", "L1", "Gk", "k", "Kk", "e", "k", "e", "k", "e", "k", "e", "k", "k", "Fe", "k",
    "k", "k", "Fk",
)


def body(
    comm,
    inputs,
    lengths,
    norm1_gain,
    norm1_bias,
    qkv_weight,
    features,
    out_weight,
    norm2_gain,
    norm2_bias,
    up_weight,
    down_weight,
    cotangent,
):
    seqs, rows, width = inputs.shape
    wide = up_weight.shape[1]
    first_row = (comm.position() * rows).astype(jnp.int32)
    meta = jnp.concatenate([first_row[None], lengths])
    fx = features.reshape(4, 512, 64)
    bits = comm.bits()
    g1, n1, g2, n2 = (v[None] for v in (norm1_gain, norm1_bias, norm2_gain, norm2_bias))
    vec = full((1, width))
    act = cols(rows, LANES)
    big = cols(rows, 512)
    heads = (4, 72, 256)
    states = [(full(heads), heads, F32)] * 2

    def maps_of(s, after):
        return call(
            functools.partial(map_kernel, s), 4,
            [SMEM, SMEM, of_seq(s, (rows, width)), vec, vec]
            + [cols(width, LANES, 4 * n) for n in (1, 2)] + [PAIR],
            [(full((rows, width)), (rows, width), BF)]
            + [(act, (rows, width), BF)] * 2
            + [(big, (rows, 2048), BF)] + states,
            flops=rows * 3_000_000, nbytes=8 * 2**20,
        )(meta, bits, inputs, g1, n1, qkv_weight, qkv_weight, fx, after=after)

    def queries_of(h1, after):
        return call(
            query_kernel, 4, [full((rows, width)), cols(width, LANES), PAIR],
            [(act, (rows, width), BF), (big, (rows, 2048), BF)],
            flops=rows * 1_800_000, nbytes=4 * 2**20,
        )(h1, qkv_weight, fx, after=after)

    def locals_of(s, after):
        _, _, _, vv, pq, pk = maps[s]
        return call(
            local_kernel, 4, [big, big, act],
            [(cols(rows, 256), (rows, 1024), F32)],
            flops=rows * 6_000_000, nbytes=7 * 2**20,
        )(pq, pk, vv, after=after)[0]

    def middle_of(s, prefix, after):
        pq = maps[s][4]
        return call(
                functools.partial(middle_kernel, s), wide // 1024,
                [SMEM, SMEM, of_seq(s, (rows, width)), of_seq(s, (rows, width)), full((rows, 2048)),
                 full((rows, 1024)), full(heads), full(heads), vec, vec, full((width, width)),
                 cols(width, 1024), pl.BlockSpec((1024, width), lambda p: (p, 0))] + [ANY] * s,
                [(of_seq(s, (rows, width)), inputs.shape, BF),
                 (full((rows, width)), (rows, width), F32),
                 (full((rows, 1024)), (rows, 1024), BF),
                 (full((rows, width)), (rows, width), BF),
                 (full((rows, width)), (rows, width), BF),
                 (full((rows, width)), (rows, width), BF),
                 (full((rows, width)), (rows, width), BF),
                 (cols(rows, 1024), (rows, wide), BF),
                 (cols(rows, 1024), (rows, wide), BF),
                 *states,
                 (full((8, width)), (8, width), F32)],
                scratch=[pltpu.VMEM((rows, width), F32), pltpu.VMEM((rows, width), F32),
                         pltpu.VMEM((rows, LANES), F32)]
                + [pltpu.VMEM((rows, width), F32)] * 3,
                flops=rows * 11_000_000, nbytes=24 * 2**20, grant=30, aliases={13: 0} if s else {},
            )(meta, bits, inputs, cotangent, pq, locals_[s], *prefix, g2, n2, out_weight,
              up_weight, down_weight, *([mids[0][0]] if s else []), after=after)

    def inner(s, part, after):
        _, qs, ks, vv, pq, pk = maps[s]
        here = lambda wide: pl.BlockSpec((rows, wide), lambda p: (0, p + 2 * part))
        side = pl.BlockSpec((2, 72, 256), lambda p: (p % 2, 0, 0))
        fxs = pl.BlockSpec((1, 512, 64), lambda p: (p + 2 * part, 0, 0))
        act, big = here(LANES), here(512)
        earlier = tuple(inners[s]) if part else ()
        return call(
            functools.partial(inner_kernel, part), 2,
            [SMEM, act, act, act, big, big, here(256), side, side, fxs] + [ANY] * len(earlier),
            [(act, (rows, width), BF), (act, (rows, width), F32), (act, (rows, width), F32)],
            flops=rows * 10_000_000, nbytes=6 * 2**20,
            aliases={10 + n: n for n in range(len(earlier))},
        )(bits, qs, ks, vv, pq, pk, mids[s][2], *state[s], fx, *earlier, after=after)

    def last(s, later, after):
        _, qs, ks, vv, pq, pk = maps[s]
        return call(
            functools.partial(last_kernel, s), 4,
            [SMEM, of_seq(s, (rows, width)), full((rows, width)), vec, act, act, big, HEADS, HEADS,
             PAIR,
             act, act, act] + [cols(width, LANES, 4 * n) for n in range(3)] + [ANY] * s,
            [(of_seq(s, (rows, width)), inputs.shape, F32), (act, (rows, width), BF),
             (act, (rows, width), BF), (full((8, width)), (8, width), F32)],
            scratch=[pltpu.VMEM((rows, width), F32)],
            flops=rows * 6_000_000, nbytes=11 * 2**20, aliases={16: 0} if s else {},
        )(bits, inputs, mids[s][1], g1, ks, vv, pk, *later, fx, *inners[s],
          qkv_weight, qkv_weight, qkv_weight, *([lasts[0][0]] if s else []), after=after)

    maps, locals_, mids, state, inners, lasts, kept, flows = {}, {}, {}, {}, {}, {}, {}, {}
    ends = {}

    def of_mids(*index):
        return [[mids[s][n] for s in range(seqs)] for n in index]

    def weights(name, give, after):
        if name == "e":
            return early_weights(give, bits, *of_mids(5, 8, 3, 4), after=after)
        h1 = [maps[s][0] for s in range(seqs)]
        dq = [inners[s][0] for s in range(seqs)]
        dk, dv, ng1 = ([lasts[s][n] for s in range(seqs)] for n in (1, 2, 3))
        return late_weights(give, bits, h1, dq, dk, dv, ng1, *of_mids(11), after=after)

    shapes = {
        "e": ((width, 512), (width, width)),
        "k": ((width, 3 * width), (width, LANES)),
    }

    def play(items, token):
        for item in items:
            after = () if token is None else (token,)
            kind, name = item[0], item[-1]
            s = int(item[1]) if item[1:2] in ("0", "1") else None
            if kind == "M":
                h1, ks, vv, pk, keep, token = maps_of(s, after)
                maps[s] = [h1, None, ks, vv, None, pk]
                flows["fg"[s]] = comm.carry(keep, token, bits, False)
                next(flows["fg"[s]])
            elif kind == "Q":
                maps[s][1], maps[s][4] = queries_of(maps[s][0], after)
                token = maps[s][1]
            elif kind == "A":
                token = locals_[s] = locals_of(s, after)
            elif kind == "N":
                state[s] = next(flows["fg"[s]])
                mids[s] = middle_of(s, state[s], after)
                token = mids[s][10]
                flows["pq"[s]] = comm.carry(mids[s][9], token, bits, True)
                next(flows["pq"[s]])
            elif kind == "I":
                inners[s] = inner(s, int(name == "b"), after)
                token = inners[s][1]
            elif kind == "L":
                lasts[s] = last(s, next(flows["pq"[s]]), after)
                token = lasts[s][0]
            elif kind == "G":
                token = weights(name, True, after)
                flows[name] = comm.sums(
                    token, functools.partial(kept.get, name), bits, shapes[name]
                )
                next(flows[name])
            elif kind == "K":
                token = kept[name] = weights(name, False, after)
            elif kind == "F":
                token = ends[name] = flows[name].send(after)
            else:
                token = flows[name].send(after)
        return token

    token = play(FRONT, None)
    parts = block_weights(*of_mids(7, 6, 5, 8), after=(token,))
    down_grad, up_grad = comm.whole_sum(tuple(parts))

    def rest():
        play(BACK, parts[1])
        up_end, outw_grad = comm.close(ends["e"], bits, shapes["e"])
        return up_end, outw_grad, ends["k"], lasts[seqs - 1][0]

    def nothing():
        shaped = [(width, 512), (width, width), (comm.late_rows(width), 3 * width + LANES)]
        return *(jnp.zeros(s, F32) for s in shaped), cotangent.astype(F32)

    up_end, outw_grad, late, grad = lax.cond(jnp.max(lengths) > 0, rest, nothing)
    up_grad = jnp.concatenate([up_grad, up_end], axis=1)
    qkv_grad, small = comm.close(late, bits, shapes["k"], after=(up_grad,))
    small = small[:, :16].T
    out = mids[seqs - 1][0]
    return (
        out,
        grad,
        small[0],
        small[1],
        qkv_grad,
        outw_grad,
        small[8],
        small[9],
        up_grad,
        down_grad,
    )


def solution(mesh):
    comm = AnySlice()
    if dict(mesh.shape) == {"seq": 8, "batch": 4}:
        comm = Slice32()
        mesh = Mesh(mesh.devices.reshape(4, 2, 2, 2), comm.axes)
    return jax.shard_map(
        functools.partial(body, comm),
        mesh=mesh,
        in_specs=(comm.rows, comm.lens) + (P(),) * 9 + (comm.rows,),
        out_specs=(comm.rows, comm.rows) + (P(),) * 8,
        check_vma=False,
    )
```

```python
import functools

import jax
import jax.numpy as jnp
from jax import lax
from jax.experimental import pallas as pl
from jax.experimental.pallas import tpu as pltpu
from jax.sharding import Mesh, PartitionSpec as P

EPS = 1e-05
SHRINK = 64 ** (-0.25)
SCALE = 256 ** (-0.5)


class Slice32:
    axes = ("z", "y", "x", "c")
    rows = P(("x", "c"), ("z", "y"), None)
    lens = P(("x", "c"))
    swaps = {
        "c": ("c", [(0, 1), (1, 0)]),
        "x": ("x", [(0, 1), (1, 0)]),
        "y": ("y", [(0, 1), (1, 0)]),
        "z1": ("z", [(0, 1), (1, 0), (2, 3), (3, 2)]),
        "z2": ("z", [(0, 2), (2, 0), (1, 3), (3, 1)]),
    }

    def late_rows(self, width):
        return width // 2

    def position(self):
        return lax.axis_index("z") * 2 + lax.axis_index("y")

    def bits(self):
        z = lax.axis_index("z")
        at = [lax.axis_index(a) for a in "cxy"] + [z % 2, z // 2]
        return jnp.stack(at).astype(jnp.int32)

    def swap(self, part, axis):
        name, pairs = self.swaps[axis]
        return lax.ppermute(part, name, pairs)

    def whole_sum(self, part):
        return lax.psum(part, self.axes)

    def carry(self, keep, give, bits, reverse):
        after = yield
        got = self.swap(give, "y")
        after = yield give
        total = simple(add_kernel, after, keep, got)
        hops = [(3, 2), (2, 1), (1, 0)] if reverse else [(0, 1), (1, 2), (2, 3)]
        out, arrived = total, []
        for hop in hops:
            arrived.append(lax.ppermute(out, "z", [hop]))
            after = yield out
            if len(arrived) < 3:
                out = simple(add_kernel, after, total, arrived[-1])
        mine, send = call(
            functools.partial(close_kernel, reverse), 1, [SMEM] + [full(keep.shape)] * 5,
            [(full(keep.shape), keep.shape, F32)] * 2, flops=keep.size, nbytes=28 * keep.size,
        )(bits, keep, got, *arrived, after=after)
        other = self.swap(send, "y")
        yield send
        yield mine, other

    def sums(self, give, keep, bits, shapes):
        after = yield
        got = self.swap(give, "c")
        after = yield give
        rows, wide = give.shape

        def fold(ways, parts, after, count):
            size = parts[0].shape[0] // count
            shape = (size, wide)
            outs = [(full(shape), shape, F32)] * (4 if count == 4 else 2 * len(ways))
            return call(
                functools.partial(fold_kernel, ways, count), 1,
                [SMEM] + [full(p.shape) for p in parts], outs,
                flops=parts[0].size, nbytes=12 * parts[0].size,
            )(bits, *parts, after=after)

        give_a, give_b, keep_a, keep_b = fold((1, 2), (keep(), got), after, 4)
        got_a, got_b = self.swap(give_a, "x"), self.swap(give_b, "y")
        after = yield give_a
        give_a, give_b, keep_a, keep_b = fold((2, 1), (keep_a, got_a, keep_b, got_b), after, 2)
        got_a, got_b = self.swap(give_a, "y"), self.swap(give_b, "x")
        after = yield give_a
        both = rows // 4
        part = (full((both // 2, wide)), (both // 2, wide), F32)
        ins = [SMEM] + [full((both // 2, wide))] * 4
        give, keep = call(merge_kernel, 1, ins, [part] * 2, nbytes=24 * both * wide)(
            bits, keep_a, got_a, keep_b, got_b, after=after
        )
        got = self.swap(give, "z1")
        after = yield give
        give, keep = fold((4,), (keep, got), after, 2)
        got = self.swap(give, "z2")
        after = yield give
        one = simple(add_kernel, after, keep, got)
        got = self.swap(one, "z2")
        after = yield one
        (two,) = self.join((4,), bits, (one, got), after)
        got = self.swap(two, "z1")
        after = yield two
        (four,) = self.join((3,), bits, (two, got), after)
        a, b = four[: both // 2], four[both // 2 :]
        got_a, got_b = self.swap(a, "y"), self.swap(b, "x")
        after = yield a
        a, b = self.join((2, 1), bits, (a, got_a, b, got_b), after)
        got_a, got_b = self.swap(a, "x"), self.swap(b, "y")
        after = yield a
        part = call(
            functools.partial(join_kernel, (1, 2), True), 1,
            [SMEM] + [full(a.shape)] * 4, [(full((rows, wide)), (rows, wide), F32)],
            nbytes=8 * rows * wide,
        )(bits, a, got_a, b, got_b, after=after)[0]
        yield part

    def close(self, part, bits, shapes, after=()):
        got = self.swap(part, "c")
        return call(
            last_join_kernel, 1, [SMEM] + [full(part.shape)] * 2,
            [(full(s), s, F32) for s in shapes], nbytes=16 * part.size,
        )(bits, part, got, after=after)

    def join(self, ways, bits, parts, after):
        rows, wide = parts[0].shape
        out = (full((2 * rows, wide)), (2 * rows, wide), F32)
        return call(
            functools.partial(join_kernel, ways, False), 1,
            [SMEM] + [full(p.shape) for p in parts], [out] * len(ways),
            nbytes=16 * rows * wide,
        )(bits, *parts, after=after)


class AnySlice:
    axes = ("seq", "batch")
    rows = P("batch", "seq", None)
    lens = P("batch")

    def late_rows(self, width):
        return width

    def position(self):
        return lax.axis_index("seq")

    def bits(self):
        return jnp.zeros((5,), jnp.int32)

    def whole_sum(self, part):
        return lax.psum(part, self.axes)

    def carry(self, keep, give, bits, reverse):
        size = lax.axis_size("seq")

        def shift(part, by):
            pairs = [(i, i + by) for i in range(size - by)]
            return lax.ppermute(part, "seq", [(b, a) for a, b in pairs] if reverse else pairs)

        for _ in range(6):
            yield keep
        out, by = shift(jnp.stack([keep, give]), 1), 1
        while by < size:
            out, by = out + shift(out, by), by * 2
        yield out[0], out[1]

    def sums(self, give, keep, bits, shapes):
        for _ in range(10):
            yield give
        yield jnp.concatenate([keep(), give], axis=0)

    def close(self, part, bits, shapes, after=()):
        part = lax.psum(part, self.axes)
        outs, at = [], 0
        for shape in shapes:
            outs.append(part[:, at : at + shape[1]])
            at += shape[1]
        return outs
LANES = 128
BF = jnp.bfloat16
F32 = jnp.float32


def mm(a, b):
    return jnp.dot(a, b, preferred_element_type=F32)


def mm_t(a, b):
    return lax.dot_general(a, b, (((1,), (1,)), ((), ())), preferred_element_type=F32)


def lanes_of(width):
    return lax.broadcasted_iota(jnp.int32, (1, width), 1)


def head_of(width):
    return (lanes_of(width) % LANES) // 64


def live_of(meta, s, rows):
    at = lax.broadcasted_iota(jnp.int32, (rows, 1), 0) + meta[0]
    return (at < meta[1 + s]).astype(F32)


def norm(values, gain, bias):
    mu = jnp.mean(values, axis=-1, keepdims=True)
    centred = values - mu
    inv = lax.rsqrt(jnp.mean(centred * centred, axis=-1, keepdims=True) + EPS)
    xhat = centred * inv
    return xhat * gain + bias, xhat, inv


def norm_grad(e, xhat, inv, gain):
    eg = e * gain
    return inv * (
        eg
        - jnp.mean(eg, axis=-1, keepdims=True)
        - xhat * jnp.mean(eg * xhat, axis=-1, keepdims=True)
    )


def blocks_of(f):
    shape = (f.shape[0], LANES)
    own = lax.broadcasted_iota(jnp.int32, shape, 0) // 256 == head_of(LANES)
    diagonal = jnp.where(own, jnp.concatenate([f, f], axis=1), jnp.zeros(shape, BF))
    half = jnp.where(own, -0.5, 0.0).astype(BF)
    return jnp.concatenate([diagonal, half], axis=1)


def two_rows(first, second):
    row = lax.broadcasted_iota(jnp.int32, (8, first.shape[1]), 0)
    return jnp.where(row == 0, first, jnp.where(row == 1, second, 0.0))


def phi(u, f):
    fw = blocks_of(f)
    sq = jnp.square(u.astype(F32))
    hi = sq.astype(BF)
    lo = (sq - hi.astype(F32)).astype(BF)
    lhs = jnp.concatenate([u, hi, lo], axis=1)
    return jnp.exp(mm_t(lhs, jnp.concatenate([fw, fw[:, LANES:]], axis=1))) * SCALE


def map_kernel(s, meta, bits, x, gain, bias, wk, wv, fx, h1, ks, vv, pk, keep, give):
    p = pl.program_id(0)
    rows = x.shape[1]

    @pl.when(p == 0)
    def _():
        h1[...] = norm(x[0].astype(F32), gain[...], bias[...])[0].astype(BF)

    kv = mm(h1[...], jnp.concatenate([wk[...], wv[...]], axis=1))
    k = (SHRINK * kv[:, :LANES]).astype(BF)
    v = kv[:, LANES:].astype(BF)
    ks[...], vv[...] = k, v
    phk = (phi(k, fx[0]) * live_of(meta, s, rows)).astype(BF)
    pk[...] = phk
    ds = mm(jnp.concatenate([v.T, jnp.ones((16, rows), BF)], axis=0), phk)
    for near, xs in ((True, keep), (False, give)):

        @pl.when((p // 2 == bits[2]) == near)
        def _(xs=xs):
            put_state(xs, 2 * (p % 2), ds[:64, :256], ds[128:129, :256])
            put_state(xs, 2 * (p % 2) + 1, ds[64:128, 256:], ds[128:129, 256:])


def query_kernel(h1, wq, fx, qs, pq):
    q = (SHRINK * mm(h1[...], wq[...])).astype(BF)
    qs[...] = q
    pq[...] = phi(q, fx[0]).astype(BF)


def put_state(xs, at, state, total):
    xs[at, :64] = state
    xs[at, 64:] = jnp.broadcast_to(total, (8, 256))


def add_kernel(*refs):
    *parts, out = refs
    total = parts[0][...]
    for part in parts[1:]:
        total = total + part[...]
    out[...] = total


def close_kernel(reverse, bits, keep, got, first, second, third, mine, send):
    before = (first[...] + second[...]) + third[...]
    early = (bits[2] == (1 if reverse else 0)).astype(F32)
    mine[...] = before + (1.0 - early) * got[...]
    send[...] = before + early * keep[...]


def fold_kernel(ways, count, bits, *refs):
    if count == 4:
        part, got, *outs = refs
        size = part.shape[0] // 4
        for n, way in enumerate(ways):
            bit = bits[way]
            for out, side in ((outs[n], 1 - bit), (outs[2 + n], bit)):
                at = pl.ds(pl.multiple_of((2 * n + side) * size, 8), size)
                out[...] = part[at, :] + got[at, :]
        return
    pairs = len(ways)
    for n, way in enumerate(ways):
        part, got = refs[2 * n], refs[2 * n + 1]
        outs = refs[2 * pairs :]
        size, bit = part.shape[0] // 2, bits[way]
        for out, side in ((outs[n], 1 - bit), (outs[pairs + n], bit)):
            at = pl.ds(pl.multiple_of(side * size, 8), size)
            out[...] = part[at, :] + got[at, :]


def merge_kernel(bits, part_a, got_a, part_b, got_b, give, keep):
    first = bits[3] == 0
    a, b = part_a[...] + got_a[...], part_b[...] + got_b[...]
    keep[...] = jnp.where(first, a, b)
    give[...] = jnp.where(first, b, a)


def join_kernel(ways, one, bits, *refs):
    outs = refs[2 * len(ways) :]
    for n, way in enumerate(ways):
        part, got = refs[2 * n], refs[2 * n + 1]
        size, bit = part.shape[0], bits[way]
        out, base = (outs[0], 2 * n * size) if one else (outs[n], 0)
        out[pl.ds(pl.multiple_of(base + bit * size, 8), size), :] = part[...]
        out[pl.ds(pl.multiple_of(base + (1 - bit) * size, 8), size), :] = got[...]


def last_join_kernel(bits, part, got, *outs):
    size, at = part.shape[0], 0
    for out in outs:
        wide = out.shape[1]
        for ref, side in ((part, bits[0]), (got, 1 - bits[0])):
            out[pl.ds(pl.multiple_of(side * size, 8), size), :] = ref[:, at : at + wide]
        at += wide


def below(rows, cols, shift):
    i = lax.broadcasted_iota(jnp.int32, (rows, cols), 0) + shift
    return lax.broadcasted_iota(jnp.int32, (rows, cols), 1) <= i


def local_kernel(pq, pk, vv, nd):
    rows = pq.shape[0]
    half = rows // 2
    v = vv[...]
    values = jnp.concatenate([v, jnp.ones_like(v)], axis=1)
    head = head_of(2 * LANES)
    top, low = None, None
    for h in range(2):
        cols = slice(256 * h, 256 * h + 256)
        mine = jnp.where(head == h, values, jnp.zeros_like(values))
        a0 = mm_t(pq[:half, cols], pk[:half, cols])
        a0 = jnp.where(below(half, half, 0), a0, 0.0).astype(BF)
        a1 = mm_t(pq[half:, cols], pk[:, cols])
        a1 = jnp.where(below(half, rows, half), a1, 0.0).astype(BF)
        t, l = mm(a0, mine[:half]), mm(a1, mine)
        top, low = (t, l) if h == 0 else (top + t, low + l)
    nd[:half] = top
    nd[half:] = low


def gelu_parts(u):
    c0, c1 = 0.7978845608028654, 0.044715
    sq = u * u
    t = jnp.tanh(u * (c0 + (c0 * c1) * sq))
    half_up = 0.5 + 0.5 * t
    slope = half_up + (0.5 * u) * (1.0 - t * t) * (c0 + (3.0 * c0 * c1) * sq)
    return u * half_up, slope


def state_of(mine, other, near, first):
    two = [jnp.where(near, mine[first + h], other[first + h]) for h in range(2)]
    st = jnp.concatenate([t[:64] for t in two], axis=1)
    return st, jnp.concatenate([t[64:65] for t in two], axis=1)


def middle_kernel(
    s, meta, bits, x, dy, pq, nd, mine, other, gain, bias, wo, wup, wdown, *refs
):
    middle_body(s, meta, bits, x, dy, pq, nd, mine, other, gain, bias, wo, wup, wdown, *refs[-18:])


def middle_body(
    s, meta, bits, x, dy, pq, nd, mine, other, gain, bias, wo, wup, wdown,
    out, dx1, dx, a_low, db, h2, df, gl, du, gs_keep, gs_give, ng,
    x1, xhat, inv, f, dh2, den,
):
    c = pl.program_id(0)
    rows = x.shape[1]
    live = live_of(meta, s, rows)
    col = lanes_of(512)

    @pl.when(c == 0)
    def _():
        for p in range(4):
            st, z = state_of(mine, other, bits[2] == p // 2, 2 * (p % 2))
            zero = jnp.zeros_like(st)
            zb = jnp.broadcast_to(z, st.shape)
            rhs = jnp.concatenate(
                [
                    jnp.where(col < 256, st, zero),
                    jnp.where(col >= 256, st, zero),
                    jnp.where(col < 256, zb, zero),
                    jnp.where(col >= 256, zb, zero),
                ],
                axis=0,
            ).astype(BF)
            both = mm_t(pq[:, 512 * p : 512 * p + 512], rhs) + nd[:, 256 * p : 256 * p + 256]
            lanes = slice(LANES * p, LANES * p + LANES)
            den[:, lanes] = both[:, LANES:]
            f[:, lanes] = both[:, :LANES] / both[:, LANES:]
        a_low[...] = f[...].astype(BF)
        mid = x[0].astype(F32) + live * mm(a_low[...], wo[...])
        x1[...] = mid
        h, xh, iv = norm(mid, gain[...], bias[...])
        h2[...] = h.astype(BF)
        xhat[...] = xh
        inv[...] = jnp.broadcast_to(iv, inv.shape)
        df[...] = (live * dy[0].astype(F32)).astype(BF)

    g, slope = gelu_parts(mm(h2[...], wup[...]))
    g = g.astype(BF)
    gl[...] = g
    d = (slope * mm_t(df[...], wdown[...])).astype(BF)
    du[...] = d
    part = mm(g, wdown[...])
    back = mm_t(d, wup[...])

    @pl.when(c == 0)
    def _():
        x1[...] += live * part
        dh2[...] = back

    @pl.when(c > 0)
    def _():
        x1[...] += live * part
        dh2[...] += back

    @pl.when(c == pl.num_programs(0) - 1)
    def _():
        out[0] = x1[...].astype(BF)
        e = dh2[...]
        xh = xhat[...]
        ng[...] = two_rows(
            jnp.sum(e * xh, axis=0, keepdims=True), jnp.sum(e, axis=0, keepdims=True)
        )
        g1 = dy[0].astype(F32) + norm_grad(e, xh, inv[:, :1], gain[...])
        dx1[...] = g1
        db[...] = (live * g1).astype(BF)
        da = mm_t(db[...], wo[...])
        block = jnp.where(
            lax.broadcasted_iota(jnp.int32, (2 * LANES, LANES), 0) % LANES // 64
            == lax.broadcasted_iota(jnp.int32, (2 * LANES, LANES), 1) // 64,
            -1.0,
            0.0,
        ).astype(BF)
        slot = lanes_of(LANES) % 64
        for p in range(4):
            lanes = slice(LANES * p, LANES * p + LANES)
            dn = da[:, lanes] / den[:, lanes]
            w = dn * f[:, lanes]
            hi = w.astype(BF)
            lo = (w - hi.astype(F32)).astype(BF)
            dd = mm(jnp.concatenate([hi, lo], axis=1), block)
            hi = dd.astype(BF).astype(F32)
            lo = dd - hi
            two = jnp.where((slot == 0) | (slot == 2), hi, jnp.where(slot == 1, lo, 0.0))
            both = jnp.concatenate([dn.astype(BF), two.astype(BF)], axis=1)
            dx[:, 256 * p : 256 * p + 256] = both
            g = mm(both.T, pq[:, 512 * p : 512 * p + 512])
            for near, gs in ((True, gs_keep), (False, gs_give)):

                @pl.when((bits[2] == p // 2) == near)
                def _(gs=gs, g=g):
                    for h in range(2):
                        side, at = slice(256 * h, 256 * h + 256), 128 + 64 * h
                        z = g[at : at + 1, side] + g[at + 1 : at + 2, side]
                        put_state(gs, 2 * (p % 2) + h, g[64 * h : 64 * h + 64, side], z)


def inner_kernel(part, bits, qs, ks, vv, pq, pk, dx, mine, other, fx, *outs):
    p = pl.program_id(0) + 2 * part
    dq, dkl, dvl = outs[-3:]
    rows = pq.shape[0]
    half = rows // 2
    col = lanes_of(512)
    slot = lanes_of(LANES) % 64
    head = head_of(2 * LANES)
    ones = jnp.broadcast_to(jnp.where(slot < 2, 1.0, 0.0), (rows, LANES)).astype(BF)
    v1 = jnp.concatenate([vv[...], ones], axis=1)
    st, z = state_of(mine, other, bits[2] == p // 2, 0)
    zh = z.astype(BF).astype(F32)
    zl = z - zh
    zero = jnp.zeros_like(st)
    row = lax.broadcasted_iota(jnp.int32, (64, 512), 0)
    zr = jnp.where(row < 2, zh, jnp.where(row == 2, zl, 0.0))
    rhs = jnp.concatenate(
        [
            jnp.where(col < 256, st, zero),
            jnp.where(col >= 256, st, zero),
            jnp.where(col < 256, zr, zero),
            jnp.where(col >= 256, zr, zero),
        ],
        axis=0,
    ).astype(BF)
    d = dx[...]
    far = mm(d, rhs)
    eqs, eks = [], []
    top, low = None, None
    for h in range(2):
        cols = slice(256 * h, 256 * h + 256)
        own = jnp.where(head == h, d, jnp.zeros_like(d))
        q, k = pq[:, cols], pk[:, cols]
        a0 = jnp.where(below(half, half, 0), mm_t(own[:half], v1[:half]), 0.0).astype(BF)
        a1 = jnp.where(below(half, rows, half), mm_t(own[half:], v1), 0.0).astype(BF)
        dpq = jnp.concatenate([mm(a0, k[:half]), mm(a1, k)], axis=0) + far[:, cols]
        eqs.append((dpq * q.astype(F32)).astype(BF))
        i0 = lax.broadcasted_iota(jnp.int32, (half, rows), 1)
        up0 = i0 >= lax.broadcasted_iota(jnp.int32, (half, rows), 0)
        up1 = up0[:, :half]
        b0 = jnp.where(up0, mm_t(v1[:half], own), 0.0).astype(BF)
        b1 = jnp.where(up1, mm_t(v1[half:], own[half:]), 0.0).astype(BF)
        dpk = jnp.concatenate([mm(b0, q), mm(b1, q[half:])], axis=0)
        eks.append((dpk * k.astype(F32)).astype(BF))
        c0 = jnp.where(up0, mm_t(k[:half], q), 0.0).astype(BF)
        c1 = jnp.where(up1, mm_t(k[half:], q[half:]), 0.0).astype(BF)
        t, l = mm(c0, own[:, :LANES]), mm(c1, own[half:, :LANES])
        top, low = (t, l) if h == 0 else (top + t, low + l)
    fw = blocks_of(fx[0])
    r = mm(jnp.concatenate(eqs, axis=1), fw)
    dq[...] = (SHRINK * (r[:, :LANES] + 2.0 * qs[...].astype(F32) * r[:, LANES:])).astype(BF)
    r = mm(jnp.concatenate(eks, axis=1), fw)
    dkl[...] = r[:, :LANES] + 2.0 * ks[...].astype(F32) * r[:, LANES:]
    dvl[:half] = top
    dvl[half:] = low


def last_kernel(
    s, bits, x, dx1, gain, ks, vv, pk, mine, other, fx, dq, dkl, dvl, wq, wk, wv,
    *refs,
):
    grad, dk, dv, ng, dh1 = refs[-5:]
    p = pl.program_id(0)
    rows = pk.shape[0]
    col = lanes_of(512)
    slot = lanes_of(LANES) % 64
    ones = jnp.broadcast_to(jnp.where(slot < 2, 1.0, 0.0), (rows, LANES)).astype(BF)
    v1 = jnp.concatenate([vv[...], ones], axis=1)
    st, z = state_of(mine, other, bits[2] == p // 2, 0)
    zh = z.astype(BF).astype(F32)
    zl = z - zh
    zero = jnp.zeros_like(st)
    row = lax.broadcasted_iota(jnp.int32, (64, 512), 0)
    zr = jnp.where(row == 0, zh, jnp.where(row == 1, zl, 0.0))
    rhs = jnp.concatenate(
        [
            jnp.where(col < 256, st, zero),
            jnp.where(col >= 256, st, zero),
            jnp.where(col < 256, zr, zero),
            jnp.where(col >= 256, zr, zero),
        ],
        axis=0,
    ).astype(BF)
    dpk = mm(v1, rhs)
    ek = (dpk * pk[...].astype(F32)).astype(BF)
    r = mm(ek, blocks_of(fx[0]))
    k = SHRINK * (dkl[...] + r[:, :LANES] + 2.0 * ks[...].astype(F32) * r[:, LANES:])
    k = k.astype(BF)
    v = (dvl[...] + mm_t(pk[...], rhs[:LANES])).astype(BF)
    dk[...], dv[...] = k, v
    w = jnp.concatenate([wq[...], wk[...], wv[...]], axis=1)
    part = mm_t(jnp.concatenate([dq[...], k, v], axis=1), w)

    @pl.when(p == 0)
    def _():
        dh1[...] = part

    @pl.when(p > 0)
    def _():
        dh1[...] += part

    @pl.when(p == pl.num_programs(0) - 1)
    def _():
        _, xh, inv = norm(x[0].astype(F32), gain[...], gain[...])
        e = dh1[...]
        ng[...] = two_rows(
            jnp.sum(e * xh, axis=0, keepdims=True), jnp.sum(e, axis=0, keepdims=True)
        )
        grad[0] = dx1[...] + norm_grad(e, xh, inv, gain[...])


def block_kernel(g0, g1, f0, f1, h0, h1, u0, u1, down, up, turned):
    p = pl.program_id(0)
    rows = h0.shape[0]

    @pl.when(p < 4)
    def _():
        down[...] = mm(g0[...].T, f0[...]) + mm(g1[...].T, f1[...])

    @pl.when(p == 4)
    def _():
        turned[:, :rows], turned[:, rows:] = h0[...].T, h1[...].T

    @pl.when(p >= 4)
    def _():
        up[...] = mm(turned[:, :rows], u0[...]) + mm(turned[:, rows:], u1[...])


def early_kernel(c, a0, a1, b0, b1, a2, a3, b2, b3, out):
    out[:, :512] = mm(a0[...].T, b0[...]) + mm(a1[...].T, b1[...])
    out[:, 512:] = mm(a2[...].T, b2[...]) + mm(a3[...].T, b3[...])


def late_kernel(c, a0, a1, b0, b1, b2, b3, b4, b5, n0, n1, n2, n3, out):
    a = jnp.concatenate([a0[...].T, a1[...].T], axis=1)
    for n, (first, second) in enumerate(((b0, b1), (b2, b3), (b4, b5))):
        both = jnp.concatenate([first[...], second[...]], axis=0)
        out[:, 512 * n : 512 * n + 512] = mm(a, both)
    sums = [n0[...] + n1[...], n2[...] + n3[...]]
    out[:, 1536:] = jnp.concatenate(sums + [jnp.zeros((112, out.shape[0]), F32)], axis=0).T


def params(limit):
    return pltpu.CompilerParams(vmem_limit_bytes=limit * 2**20)


def full(shape):
    return pl.BlockSpec(shape, lambda p, n=len(shape): (0,) * n)


def of_seq(s, shape):
    return pl.BlockSpec((1,) + shape, lambda p: (s, 0, 0))


def cols(rows, width, first=0):
    return pl.BlockSpec((rows, width), lambda p: (0, first + p))


SMEM = pl.BlockSpec(memory_space=pltpu.SMEM)
HEADS = pl.BlockSpec((2, 72, 256), lambda p: (p % 2, 0, 0))
PAIR = pl.BlockSpec((1, 512, 64), lambda p: (p, 0, 0))


def arr(shape, dtype):
    return jax.ShapeDtypeStruct(shape, dtype)


ANY = pl.BlockSpec(memory_space=pl.ANY)


def call(
    kernel, grid, ins, outs, scratch=(), flops=0, nbytes=0, scalars=0, aliases={},
    grant=16,
):
    def run(*args, after=()):
        count, waits = len(ins) + scalars, len(after)

        def waiting(*refs):
            kernel(*refs[:count], *refs[count + waits :])

        return pl.pallas_call(
            waiting,
            grid_spec=pltpu.PrefetchScalarGridSpec(
                num_scalar_prefetch=scalars,
                grid=(grid,),
                in_specs=list(ins) + [ANY] * waits,
                out_specs=[o[0] for o in outs],
                scratch_shapes=list(scratch),
            ),
            out_shape=[arr(*o[1:]) for o in outs],
            compiler_params=params(grant),
            input_output_aliases=aliases,
            cost_estimate=pl.CostEstimate(flops=flops, bytes_accessed=nbytes, transcendentals=0),
        )(*args, *after)

    return run


def simple(kernel, after, *parts):
    spec = full(parts[0].shape)
    return call(
        kernel, 1, [spec] * len(parts), [(spec, parts[0].shape, F32)],
        flops=parts[0].size, nbytes=12 * parts[0].size,
    )(*parts, after=after)[0]


def half_of(give):
    return (lambda c: 1 - c[0]) if give else (lambda c: c[0])


def whole(shape):
    return pl.BlockSpec(shape, lambda p, c: (0,) * len(shape))


def block_weights(gl, df, h2, du, after=()):
    rows, width = df[0].shape
    wide = gl[0].shape[1]
    n = wide // 512
    one = full((rows, width))
    first = lambda p: jnp.minimum(p, n - 1)
    second = lambda p: jnp.maximum(p - n, 0)
    sg = pl.BlockSpec((rows, 512), lambda p: (0, first(p)))
    su = pl.BlockSpec((rows, 512), lambda p: (0, second(p)))
    return call(
        block_kernel, 2 * n - 1, [sg, sg, one, one, one, one, su, su],
        [(pl.BlockSpec((512, width), lambda p: (first(p), 0)), (wide, width), F32),
         (pl.BlockSpec((width, 512), lambda p: (0, second(p))), (width, wide - 512), F32)],
        scratch=[pltpu.VMEM((width, 2 * rows), BF)],
        flops=8 * rows * width * wide, nbytes=8 * width * wide + 8 * rows * wide,
    )(*gl, *df, *h2, *du, after=after)


def early_weights(give, bits, h2, du, a, db, after=()):
    rows, n = db[0].shape
    m = n // 2
    at, end = half_of(give), du[0].shape[1] // 512 - 1
    sa, sb = pl.BlockSpec((rows, m), lambda p, c: (0, at(c))), whole((rows, n))
    sd = pl.BlockSpec((rows, 512), lambda p, c: (0, end))
    return call(
        early_kernel, 1, [sa, sa, sd, sd, sa, sa, sb, sb],
        [(whole((m, 2 * n)), (m, 2 * n), F32)],
        flops=8 * rows * m * n, nbytes=8 * m * n + 8 * rows * n, scalars=1,
    )(bits, *h2, *du, *a, *db, after=after)[0]


def late_weights(give, bits, h1, dq, dk, dv, ng1, ng2, after=()):
    rows, n = dk[0].shape
    m = n // 2
    at = half_of(give)
    sa, sb = pl.BlockSpec((rows, m), lambda p, c: (0, at(c))), whole((rows, n))
    sn = pl.BlockSpec((8, m), lambda p, c: (0, at(c)))
    wide = 3 * n + LANES
    return call(
        late_kernel, 1, [sa] * 2 + [sb] * 6 + [sn] * 4, [(whole((m, wide)), (m, wide), F32)],
        flops=12 * rows * m * n, nbytes=12 * m * n + 12 * rows * n, scalars=1,
    )(bits, *h1, *dq, *dk, *dv, *ng1, *ng2, after=after)[0]


FRONT = (
    "M0", "f", "M1", "f", "g", "Q0", "f", "g", "Q1", "f", "g", "A0", "f", "g", "A1", "g", "N0",
    "p", "N1", "q", "p",
)
BACK = (
    "p", "q", "Ge", "e", "I0a", "Ke", "p", "q", "e", "I0b", "I1a", "p", "q", "e", "I1b", "e",
    "L0", "q", "e", "L1", "Gk", "k", "Kk", "e", "k", "e", "k", "e", "k", "e", "k", "k", "Fe", "k",
    "k", "k", "Fk",
)


def body(
    comm,
    inputs,
    lengths,
    norm1_gain,
    norm1_bias,
    qkv_weight,
    features,
    out_weight,
    norm2_gain,
    norm2_bias,
    up_weight,
    down_weight,
    cotangent,
):
    seqs, rows, width = inputs.shape
    wide = up_weight.shape[1]
    first_row = (comm.position() * rows).astype(jnp.int32)
    meta = jnp.concatenate([first_row[None], lengths])
    fx = features.reshape(4, 512, 64)
    bits = comm.bits()
    g1, n1, g2, n2 = (v[None] for v in (norm1_gain, norm1_bias, norm2_gain, norm2_bias))
    vec = full((1, width))
    act = cols(rows, LANES)
    big = cols(rows, 512)
    heads = (4, 72, 256)
    states = [(full(heads), heads, F32)] * 2

    def maps_of(s, after):
        return call(
            functools.partial(map_kernel, s), 4,
            [SMEM, SMEM, of_seq(s, (rows, width)), vec, vec]
            + [cols(width, LANES, 4 * n) for n in (1, 2)] + [PAIR],
            [(full((rows, width)), (rows, width), BF)]
            + [(act, (rows, width), BF)] * 2
            + [(big, (rows, 2048), BF)] + states,
            flops=rows * 3_000_000, nbytes=8 * 2**20,
        )(meta, bits, inputs, g1, n1, qkv_weight, qkv_weight, fx, after=after)

    def queries_of(h1, after):
        return call(
            query_kernel, 4, [full((rows, width)), cols(width, LANES), PAIR],
            [(act, (rows, width), BF), (big, (rows, 2048), BF)],
            flops=rows * 1_800_000, nbytes=4 * 2**20,
        )(h1, qkv_weight, fx, after=after)

    def locals_of(s, after):
        _, _, _, vv, pq, pk = maps[s]
        return call(
            local_kernel, 4, [big, big, act],
            [(cols(rows, 256), (rows, 1024), F32)],
            flops=rows * 6_000_000, nbytes=7 * 2**20,
        )(pq, pk, vv, after=after)[0]

    def middle_of(s, prefix, after):
        pq = maps[s][4]
        return call(
                functools.partial(middle_kernel, s), wide // 1024,
                [SMEM, SMEM, of_seq(s, (rows, width)), of_seq(s, (rows, width)), full((rows, 2048)),
                 full((rows, 1024)), full(heads), full(heads), vec, vec, full((width, width)),
                 cols(width, 1024), pl.BlockSpec((1024, width), lambda p: (p, 0))] + [ANY] * s,
                [(of_seq(s, (rows, width)), inputs.shape, BF),
                 (full((rows, width)), (rows, width), F32),
                 (full((rows, 1024)), (rows, 1024), BF),
                 (full((rows, width)), (rows, width), BF),
                 (full((rows, width)), (rows, width), BF),
                 (full((rows, width)), (rows, width), BF),
                 (full((rows, width)), (rows, width), BF),
                 (cols(rows, 1024), (rows, wide), BF),
                 (cols(rows, 1024), (rows, wide), BF),
                 *states,
                 (full((8, width)), (8, width), F32)],
                scratch=[pltpu.VMEM((rows, width), F32), pltpu.VMEM((rows, width), F32),
                         pltpu.VMEM((rows, LANES), F32)]
                + [pltpu.VMEM((rows, width), F32)] * 3,
                flops=rows * 11_000_000, nbytes=24 * 2**20, grant=30, aliases={13: 0} if s else {},
            )(meta, bits, inputs, cotangent, pq, locals_[s], *prefix, g2, n2, out_weight,
              up_weight, down_weight, *([mids[0][0]] if s else []), after=after)

    def inner(s, part, after):
        _, qs, ks, vv, pq, pk = maps[s]
        here = lambda wide: pl.BlockSpec((rows, wide), lambda p: (0, p + 2 * part))
        side = pl.BlockSpec((2, 72, 256), lambda p: (p % 2, 0, 0))
        fxs = pl.BlockSpec((1, 512, 64), lambda p: (p + 2 * part, 0, 0))
        act, big = here(LANES), here(512)
        earlier = tuple(inners[s]) if part else ()
        return call(
            functools.partial(inner_kernel, part), 2,
            [SMEM, act, act, act, big, big, here(256), side, side, fxs] + [ANY] * len(earlier),
            [(act, (rows, width), BF), (act, (rows, width), F32), (act, (rows, width), F32)],
            flops=rows * 10_000_000, nbytes=6 * 2**20,
            aliases={10 + n: n for n in range(len(earlier))},
        )(bits, qs, ks, vv, pq, pk, mids[s][2], *state[s], fx, *earlier, after=after)

    def last(s, later, after):
        _, qs, ks, vv, pq, pk = maps[s]
        return call(
            functools.partial(last_kernel, s), 4,
            [SMEM, of_seq(s, (rows, width)), full((rows, width)), vec, act, act, big, HEADS, HEADS,
             PAIR,
             act, act, act] + [cols(width, LANES, 4 * n) for n in range(3)] + [ANY] * s,
            [(of_seq(s, (rows, width)), inputs.shape, F32), (act, (rows, width), BF),
             (act, (rows, width), BF), (full((8, width)), (8, width), F32)],
            scratch=[pltpu.VMEM((rows, width), F32)],
            flops=rows * 6_000_000, nbytes=11 * 2**20, aliases={16: 0} if s else {},
        )(bits, inputs, mids[s][1], g1, ks, vv, pk, *later, fx, *inners[s],
          qkv_weight, qkv_weight, qkv_weight, *([lasts[0][0]] if s else []), after=after)

    maps, locals_, mids, state, inners, lasts, kept, flows = {}, {}, {}, {}, {}, {}, {}, {}
    ends = {}

    def of_mids(*index):
        return [[mids[s][n] for s in range(seqs)] for n in index]

    def weights(name, give, after):
        if name == "e":
            return early_weights(give, bits, *of_mids(5, 8, 3, 4), after=after)
        h1 = [maps[s][0] for s in range(seqs)]
        dq = [inners[s][0] for s in range(seqs)]
        dk, dv, ng1 = ([lasts[s][n] for s in range(seqs)] for n in (1, 2, 3))
        return late_weights(give, bits, h1, dq, dk, dv, ng1, *of_mids(11), after=after)

    shapes = {
        "e": ((width, 512), (width, width)),
        "k": ((width, 3 * width), (width, LANES)),
    }

    def play(items, token):
        for item in items:
            after = () if token is None else (token,)
            kind, name = item[0], item[-1]
            s = int(item[1]) if item[1:2] in ("0", "1") else None
            if kind == "M":
                h1, ks, vv, pk, keep, token = maps_of(s, after)
                maps[s] = [h1, None, ks, vv, None, pk]
                flows["fg"[s]] = comm.carry(keep, token, bits, False)
                next(flows["fg"[s]])
            elif kind == "Q":
                maps[s][1], maps[s][4] = queries_of(maps[s][0], after)
                token = maps[s][1]
            elif kind == "A":
                token = locals_[s] = locals_of(s, after)
            elif kind == "N":
                state[s] = next(flows["fg"[s]])
                mids[s] = middle_of(s, state[s], after)
                token = mids[s][10]
                flows["pq"[s]] = comm.carry(mids[s][9], token, bits, True)
                next(flows["pq"[s]])
            elif kind == "I":
                inners[s] = inner(s, int(name == "b"), after)
                token = inners[s][1]
            elif kind == "L":
                lasts[s] = last(s, next(flows["pq"[s]]), after)
                token = lasts[s][0]
            elif kind == "G":
                token = weights(name, True, after)
                flows[name] = comm.sums(
                    token, functools.partial(kept.get, name), bits, shapes[name]
                )
                next(flows[name])
            elif kind == "K":
                token = kept[name] = weights(name, False, after)
            elif kind == "F":
                token = ends[name] = flows[name].send(after)
            else:
                token = flows[name].send(after)
        return token

    token = play(FRONT, None)
    parts = block_weights(*of_mids(7, 6, 5, 8), after=(token,))
    down_grad, up_grad = comm.whole_sum(tuple(parts))

    def rest():
        play(BACK, parts[1])
        up_end, outw_grad = comm.close(ends["e"], bits, shapes["e"])
        return up_end, outw_grad, ends["k"], lasts[seqs - 1][0]

    def nothing():
        shaped = [(width, 512), (width, width), (comm.late_rows(width), 3 * width + LANES)]
        return *(jnp.zeros(s, F32) for s in shaped), cotangent.astype(F32)

    up_end, outw_grad, late, grad = lax.cond(jnp.max(lengths) > 0, rest, nothing)
    up_grad = jnp.concatenate([up_grad, up_end], axis=1)
    qkv_grad, small = comm.close(late, bits, shapes["k"], after=(up_grad,))
    small = small[:, :16].T
    out = mids[seqs - 1][0]
    return (
        out,
        grad,
        small[0],
        small[1],
        qkv_grad,
        outw_grad,
        small[8],
        small[9],
        up_grad,
        down_grad,
    )


def solution(mesh):
    comm = AnySlice()
    if dict(mesh.shape) == {"seq": 8, "batch": 4}:
        comm = Slice32()
        mesh = Mesh(mesh.devices.reshape(4, 2, 2, 2), comm.axes)
    return jax.shard_map(
        functools.partial(body, comm),
        mesh=mesh,
        in_specs=(comm.rows, comm.lens) + (P(),) * 9 + (comm.rows,),
        out_specs=(comm.rows, comm.rows) + (P(),) * 8,
        check_vma=False,
    )
```
